32 devices in a mesh: wide: 8 (over y, x, core), narrow: 4 (over z).
Axes of the slice: x: 2, y: 2, z: 4, core: 2. Of those that a mesh axis runs over, the one named last changes fastest.
Arguments:
- enc_in: bfloat16 [8192, 768], P('wide'), may hold values from -6 to 6
- dec_in: bfloat16 [8192, 768], P('wide'), may hold values from -6 to 6
- dec_cot: bfloat16 [8192, 768], P('wide'), may hold values from -6 to 6
- segments: int32 [16, 512], P('wide'), may hold values from 0 to 3, never falling along the last dimension, each value on 1 to 256 neighbouring positions
- enc_attn_gain: bfloat16 [768], replicated, may hold values from 0.5 to 1.5
- enc_query: bfloat16 [768, 768], P('wide'), may hold values from -0.02734375 to 0.02734375
- enc_key: bfloat16 [768, 768], P('wide'), may hold values from -0.21875 to 0.21875
- enc_value: bfloat16 [768, 768], P('wide'), may hold values from -0.21875 to 0.21875
- enc_output: bfloat16 [768, 768], P('wide'), may hold values from -1.25 to 1.25
- enc_table: bfloat16 [32, 12], replicated, may hold values from -4 to 4
- enc_ffn_gain: bfloat16 [768], replicated, may hold values from 0.5 to 1.5
- enc_ffn_in: bfloat16 [768, 3072], P('wide'), may hold values from -0.21875 to 0.21875
- enc_ffn_out: bfloat16 [3072, 768], P('wide'), may hold values from -0.109375 to 0.109375
- dec_self_gain: bfloat16 [768], replicated, may hold values from 0.5 to 1.5
- dec_query: bfloat16 [768, 768], P('wide'), may hold values from -0.02734375 to 0.02734375
- dec_key: bfloat16 [768, 768], P('wide'), may hold values from -0.21875 to 0.21875
- dec_value: bfloat16 [768, 768], P('wide'), may hold values from -0.21875 to 0.21875
- dec_output: bfloat16 [768, 768], P('wide'), may hold values from -1.25 to 1.25
- dec_table: bfloat16 [32, 12], replicated, may hold values from -4 to 4
- dec_cross_gain: bfloat16 [768], replicated, may hold values from 0.5 to 1.5
- cross_query: bfloat16 [768, 768], P('wide'), may hold values from -0.02734375 to 0.02734375
- cross_key: bfloat16 [768, 768], P('wide'), may hold values from -0.21875 to 0.21875
- cross_value: bfloat16 [768, 768], P('wide'), may hold values from -0.21875 to 0.21875
- cross_output: bfloat16 [768, 768], P('wide'), may hold values from -1.25 to 1.25
- dec_ffn_gain: bfloat16 [768], replicated, may hold values from 0.5 to 1.5
- dec_ffn_in: bfloat16 [768, 3072], P('wide'), may hold values from -0.21875 to 0.21875
- dec_ffn_out: bfloat16 [3072, 768], P('wide'), may hold values from -0.109375 to 0.109375
Outputs:
- enc_out: bfloat16 [8192, 768], P('wide', 'narrow')
- dec_out: bfloat16 [8192, 768], P('wide', 'narrow')
- enc_in_grad: bfloat16 [8192, 768], P('wide', 'narrow')
- dec_in_grad: bfloat16 [8192, 768], P('wide', 'narrow')
- enc_attn_gain_grad: float32 [768], replicated
- enc_query_grad: float32 [768, 768], P('wide')
- enc_key_grad: float32 [768, 768], P('wide')
- enc_value_grad: float32 [768, 768], P('wide')
- enc_output_grad: float32 [768, 768], P('wide')
- enc_table_grad: float32 [32, 12], replicated
- enc_ffn_gain_grad: float32 [768], replicated
- enc_ffn_in_grad: float32 [768, 3072], P('wide')
- enc_ffn_out_grad: float32 [3072, 768], P('wide')
- dec_self_gain_grad: float32 [768], replicated
- dec_query_grad: float32 [768, 768], P('wide')
- dec_key_grad: float32 [768, 768], P('wide')
- dec_value_grad: float32 [768, 768], P('wide')
- dec_output_grad: float32 [768, 768], P('wide')
- dec_table_grad: float32 [32, 12], replicated
- dec_cross_gain_grad: float32 [768], replicated
- cross_query_grad: float32 [768, 768], P('wide')
- cross_key_grad: float32 [768, 768], P('wide')
- cross_value_grad: float32 [768, 768], P('wide')
- cross_output_grad: float32 [768, 768], P('wide')
- dec_ffn_gain_grad: float32 [768], replicated
- dec_ffn_in_grad: float32 [768, 3072], P('wide')
- dec_ffn_out_grad: float32 [3072, 768], P('wide')
The draws below stay inside these ranges and needn't reach their ends.
Inputs may be any that keep to these rules, and one draw needn't show every extreme that they name: `segments`: within each row of 512 positions the numbers never fall, each of the 4 documents has 1 to 256 positions, and one has exactly 256.
All inputs are finite; a program needn't handle non-finite values.
Results may differ from the reference program's by a relative error of at most 0.034.
Values may be sent and summed in bfloat16 or wider, within the bound.
No kernel may reach another device: no remote copies, remote signals or barrier semaphores. Data moves between devices by JAX's collectives and lax.ppermute only.
A program may use at most 384 MiB of HBM per device.

```python
import math
import jax
import jax.numpy as jnp
import numpy as np
from jax import lax

D = 768
HEADS = 12
HEAD = 64
FF = 3072
BUCKETS = 32
MAXDIST = 128
LEN = 512
DOCS = 4
ROWS = 16
TOKENS = 8192


def level_of(rng, dims, shards, low, largest):
    level, own = 1.0, jax.random.fold_in(rng, 6)
    for dim, parts in shards:
        steps = jnp.exp(jax.random.uniform(jax.random.fold_in(own, dim), (parts,), jnp.float32, low / len(shards), largest / len(shards)))
        level = level * jnp.repeat(steps, dims[dim] // parts).reshape([-1 if axis == dim else 1 for axis in range(len(dims))])
    return level


def length_profile(amount, total, most, skew):
    weights = [(1 << 20) // math.isqrt(grade ** skew) + 1 for grade in range(2, amount + 1)]
    spare, counts = total - most - (amount - 1), [1] * (amount - 1)
    while spare > 0:
        free = [i for i in range(amount - 1) if counts[i] < most]
        pool, remaining = sum([weights[i] for i in free]), spare
        for i in free:
            addition = min(most - counts[i], max(1, remaining * weights[i] // pool), spare)
            counts[i] = counts[i] + addition
            spare = spare - addition
    return np.array([most] + counts)


def ragged(key, amount, total, bound, lean):
    if amount == 2:
        one = jax.random.randint(key, (), max(1, total - bound), min(bound, total - 1) + 1)
        return jnp.stack([one, total - one])
    tallies = jnp.asarray(length_profile(amount, total, bound, lean), jnp.int32)
    twos = (amount - 1) // 2
    giver, taker = tallies[1:1 + 2 * twos:2], tallies[2:2 + 2 * twos:2]
    room = jnp.minimum(giver - 1, bound - taker)
    passed = jax.random.randint(jax.random.fold_in(key, 1), (twos,), 0, 1 << 20) % (room + 1)
    tallies = tallies.at[1:1 + 2 * twos:2].set(giver - passed).at[2:2 + 2 * twos:2].set(taker + passed)
    return tallies[jax.random.permutation(jax.random.fold_in(key, 2), amount)]


def gaussian(rng, extent, spread, limit, split=(), kind=jnp.bfloat16):
    level = level_of(rng, extent, split, -0.22, 0.18) if split else 1.0
    values = jax.random.normal(rng, extent, jnp.float32) * spread * level
    return jnp.minimum(jnp.maximum(values, -limit), limit).astype(kind)


def setup_inputs(seed: int = 0) -> dict:
    keys = jax.random.split(jax.random.key(seed), 28)
    return {
        "enc_in": gaussian(keys[0], (TOKENS, D), 1.0, 6.0, ((0, 8),)),
        "dec_in": gaussian(keys[1], (TOKENS, D), 1.0, 6.0, ((0, 8),)),
        "dec_cot": gaussian(keys[2], (TOKENS, D), 1.0, 6.0, ((0, 8),)),
        "segments": jax.vmap(lambda own: jnp.searchsorted(jnp.cumsum(ragged(own, DOCS, LEN, LEN // 2, 1)), jnp.arange(LEN), side="right"))(jax.random.split(keys[3], ROWS)).reshape((ROWS, LEN)).astype(jnp.int32),
        "enc_attn_gain": jnp.clip(1.0 + 0.1 * jax.random.normal(keys[4], (D,), jnp.float32), 0.5, 1.5).astype(jnp.bfloat16),
        "enc_query": gaussian(keys[5], (D, D), (D * HEAD) ** -0.5, 0.02734375, ((0, 8),)),
        "enc_key": gaussian(keys[6], (D, D), D ** -0.5, 0.21875, ((0, 8),)),
        "enc_value": gaussian(keys[7], (D, D), D ** -0.5, 0.21875, ((0, 8),)),
        "enc_output": gaussian(keys[8], (D, D), (D // 32) ** -0.5, 1.25, ((0, 8),)),
        "enc_table": gaussian(keys[9], (BUCKETS, HEADS), 1.0, 4.0),
        "enc_ffn_gain": jnp.clip(1.0 + 0.1 * jax.random.normal(keys[10], (D,), jnp.float32), 0.5, 1.5).astype(jnp.bfloat16),
        "enc_ffn_in": gaussian(keys[11], (D, FF), D ** -0.5, 0.21875, ((0, 8),)),
        "enc_ffn_out": gaussian(keys[12], (FF, D), FF ** -0.5, 0.109375, ((0, 8),)),
        "dec_self_gain": jnp.clip(1.0 + 0.1 * jax.random.normal(keys[13], (D,), jnp.float32), 0.5, 1.5).astype(jnp.bfloat16),
        "dec_query": gaussian(keys[14], (D, D), (D * HEAD) ** -0.5, 0.02734375, ((0, 8),)),
        "dec_key": gaussian(keys[15], (D, D), D ** -0.5, 0.21875, ((0, 8),)),
        "dec_value": gaussian(keys[16], (D, D), D ** -0.5, 0.21875, ((0, 8),)),
        "dec_output": gaussian(keys[17], (D, D), (D // 32) ** -0.5, 1.25, ((0, 8),)),
        "dec_table": gaussian(keys[18], (BUCKETS, HEADS), 1.0, 4.0),
        "dec_cross_gain": jnp.clip(1.0 + 0.1 * jax.random.normal(keys[19], (D,), jnp.float32), 0.5, 1.5).astype(jnp.bfloat16),
        "cross_query": gaussian(keys[20], (D, D), (D * HEAD) ** -0.5, 0.02734375, ((0, 8),)),
        "cross_key": gaussian(keys[21], (D, D), D ** -0.5, 0.21875, ((0, 8),)),
        "cross_value": gaussian(keys[22], (D, D), D ** -0.5, 0.21875, ((0, 8),)),
        "cross_output": gaussian(keys[23], (D, D), (D // 32) ** -0.5, 1.25, ((0, 8),)),
        "dec_ffn_gain": jnp.clip(1.0 + 0.1 * jax.random.normal(keys[24], (D,), jnp.float32), 0.5, 1.5).astype(jnp.bfloat16),
        "dec_ffn_in": gaussian(keys[25], (D, FF), D ** -0.5, 0.21875, ((0, 8),)),
        "dec_ffn_out": gaussian(keys[26], (FF, D), FF ** -0.5, 0.109375, ((0, 8),)),
    }


EPSILON = 1e-06
MASKED = -1000000000.0
HIGHEST = lax.Precision.HIGHEST

@jax.custom_vjp
def low(v):
    return lax.optimization_barrier(v.astype(jnp.bfloat16)).astype(jnp.float32)

@jax.custom_vjp
def low_back(v):
    return v

def low_keep(v):
    return (low(v), None)

def low_pass(kept, grad):
    return (grad,)

def back_keep(v):
    return (v, None)

def back_low(kept, grad):
    return (low(grad),)
low.defvjp(low_keep, low_pass)
low_back.defvjp(back_keep, back_low)

def bucket_table(length, both_ways, buckets, distance):
    offsets = np.arange(-(length - 1), length)
    reverse = -offsets
    result = np.zeros(offsets.shape, np.int64)
    if both_ways:
        half_count = buckets // 2
        result = result + (reverse < 0) * half_count
        reverse = np.abs(reverse)
    else:
        half_count = buckets
        reverse = np.maximum(reverse, 0)
    exact_count = half_count // 2
    scaled = np.log(np.maximum(reverse, 1) / exact_count) / np.log(distance / exact_count) * (half_count - exact_count)
    far_bucket = np.minimum(exact_count + np.floor(np.maximum(scaled, 0.0)).astype(np.int64), half_count - 1)
    return result + np.where(reverse < exact_count, reverse, far_bucket)

def position_bias(table, both_ways):
    flat_ids = bucket_table(LEN, both_ways, BUCKETS, MAXDIST)
    bucket_ids = flat_ids[np.arange(LEN)[None, :] - np.arange(LEN)[:, None] + LEN - 1]
    gathered = jnp.take(table, jnp.asarray(bucket_ids.astype(np.int32)), axis=0)
    return jnp.transpose(gathered, (2, 0, 1))

def matmul(values, matrix):
    return jnp.matmul(values, matrix, precision=HIGHEST)

def rms_norm(values, gain):
    return values * lax.rsqrt(lax.optimization_barrier(jnp.mean(values * values, axis=-1, keepdims=True)) + EPSILON) * gain

def segment_masks(seg_rows):
    same_doc = seg_rows[:, :, None] == seg_rows[:, None, :]
    query_pos = lax.broadcasted_iota(jnp.int32, (LEN, LEN), 0)
    key_pos = lax.broadcasted_iota(jnp.int32, (LEN, LEN), 1)
    return (same_doc, same_doc & (key_pos <= query_pos)[None])

def attend_rows(queries, key_rows, value_rows, pos_bias, allowed):

    def one_row(pieces):
        q_row, k_row, v_row, mask_row = pieces
        scores = jnp.einsum('qhd,khd->hqk', q_row.reshape(LEN, HEADS, HEAD), k_row.reshape(LEN, HEADS, HEAD), precision=HIGHEST)
        if pos_bias is not None:
            scores = scores + pos_bias
        scores = low_back(scores)
        scores = jnp.where(mask_row[None], scores, MASKED)
        weights_low = low(jax.nn.softmax(scores, axis=-1))
        mixed = jnp.einsum('hqk,khd->qhd', weights_low, v_row.reshape(LEN, HEADS, HEAD), precision=HIGHEST)
        return mixed.reshape(LEN, D)
    return lax.map(jax.checkpoint(one_row), (queries, key_rows, value_rows, allowed))

def attention_block(query_src, key_src, weights, pos_bias, allowed):
    w_query, w_key, w_value, w_out = weights
    queries = low(low_back(matmul(query_src, w_query)))
    key_rows = low(low_back(matmul(key_src, w_key)))
    value_rows = low(low_back(matmul(key_src, w_value)))
    mixed = low(low_back(attend_rows(queries, key_rows, value_rows, pos_bias, allowed)))
    return low_back(matmul(mixed, w_out))

def feed_forward(normed, w_in, w_out):
    pre_act = low_back(matmul(normed, w_in))
    hidden = low(jax.nn.gelu(pre_act))
    return low_back(matmul(hidden, w_out))

def forward(params, enc_rows, dec_rows, same_doc, causal):
    attn_gain, enc_query, enc_key, enc_value, enc_output, enc_table, ffn_gain, enc_ffn_in, enc_ffn_out, self_gain, dec_query, dec_key, dec_value, dec_output, dec_table, cross_gain, cross_query, cross_key, cross_value, cross_output, last_gain, dec_ffn_in, dec_ffn_out = params
    enc_bias = position_bias(enc_table, True)
    dec_bias = position_bias(dec_table, False)
    normed = low(rms_norm(enc_rows, attn_gain))
    middle = low_back(low(enc_rows + attention_block(normed, normed, (enc_query, enc_key, enc_value, enc_output), enc_bias, same_doc)))
    normed = low(rms_norm(middle, ffn_gain))
    enc_out = low_back(low(middle + feed_forward(normed, enc_ffn_in, enc_ffn_out)))
    normed = low(rms_norm(dec_rows, self_gain))
    first = dec_rows + attention_block(normed, normed, (dec_query, dec_key, dec_value, dec_output), dec_bias, causal)
    normed = low(rms_norm(first, cross_gain))
    second = low_back(low(first + attention_block(normed, enc_out, (cross_query, cross_key, cross_value, cross_output), None, same_doc)))
    normed = low(rms_norm(second, last_gain))
    dec_out = second + feed_forward(normed, dec_ffn_in, dec_ffn_out)
    return (enc_out, dec_out)

def reference(enc_in, dec_in, dec_cot, segments, enc_attn_gain, enc_query, enc_key, enc_value, enc_output, enc_table, enc_ffn_gain, enc_ffn_in, enc_ffn_out, dec_self_gain, dec_query, dec_key, dec_value, dec_output, dec_table, dec_cross_gain, cross_query, cross_key, cross_value, cross_output, dec_ffn_gain, dec_ffn_in, dec_ffn_out):
    params = tuple((weight.astype(jnp.float32) for weight in (enc_attn_gain, enc_query, enc_key, enc_value, enc_output, enc_table, enc_ffn_gain, enc_ffn_in, enc_ffn_out, dec_self_gain, dec_query, dec_key, dec_value, dec_output, dec_table, dec_cross_gain, cross_query, cross_key, cross_value, cross_output, dec_ffn_gain, dec_ffn_in, dec_ffn_out)))
    group_rows = 8 if ROWS % 8 == 0 else 1
    groups = ROWS // group_rows

    def grouped(values):
        return values.astype(jnp.float32).reshape(groups, group_rows, LEN, D)

    def step(totals, pieces):
        enc_rows, dec_rows, cot_rows, seg_rows = pieces
        same_doc, causal = segment_masks(seg_rows)

        def run(param_set, enc_values, dec_values):
            return forward(param_set, enc_values, dec_values, same_doc, causal)
        (enc_out, dec_out), pull = jax.vjp(run, params, enc_rows, dec_rows)
        param_grads, enc_grad, dec_grad = pull((jnp.zeros_like(enc_out), cot_rows))
        totals = tuple((total + grad_part for total, grad_part in zip(totals, param_grads)))
        return (totals, (enc_out.astype(jnp.bfloat16), dec_out.astype(jnp.bfloat16), enc_grad.astype(jnp.bfloat16), dec_grad.astype(jnp.bfloat16)))
    start = tuple((jnp.zeros(param.shape, jnp.float32) for param in params))
    totals, (enc_out, dec_out, enc_grad, dec_grad) = lax.scan(step, start, (grouped(enc_in), grouped(dec_in), grouped(dec_cot), segments.reshape(groups, group_rows, LEN)))
    return (enc_out.reshape(TOKENS, D), dec_out.reshape(TOKENS, D), enc_grad.reshape(TOKENS, D), dec_grad.reshape(TOKENS, D), totals[0], totals[1], totals[2], totals[3], totals[4], totals[5], totals[6], totals[7], totals[8], totals[9], totals[10], totals[11], totals[12], totals[13], totals[14], totals[15], totals[16], totals[17], totals[18], totals[19], totals[20], totals[21], totals[22])
```

```python
import functools

import jax
import jax.numpy as jnp
import numpy as np
from jax import lax
from jax.experimental import pallas as pl
from jax.experimental.pallas import tpu as pltpu
from jax.sharding import PartitionSpec as P

D = 768
HEADS = 12
HEAD = 64
PAIRS = HEADS // 2
FF = 3072
BUCKETS = 32
MAXDIST = 128
LEN = 512
TILE = 128
BLOCKS = LEN // TILE
CHUNK = 512

EPSILON = 1e-06
MASKED = -1000000000.0
VMEM_LIMIT = 60 * 1024 * 1024
f32 = jnp.float32
bf16 = jnp.bfloat16


def bucket_of(reverse, both_ways):
    result = np.zeros(reverse.shape, np.int64)
    if both_ways:
        half_count = BUCKETS // 2
        result = result + (reverse < 0) * half_count
        reverse = np.abs(reverse)
    else:
        half_count = BUCKETS
        reverse = np.maximum(reverse, 0)
    exact_count = half_count // 2
    scaled = (
        np.log(np.maximum(reverse, 1) / exact_count)
        / np.log(MAXDIST / exact_count)
        * (half_count - exact_count)
    )
    far_bucket = np.minimum(
        exact_count + np.floor(np.maximum(scaled, 0.0)).astype(np.int64), half_count - 1
    )
    return result + np.where(reverse < exact_count, reverse, far_bucket)


def tile_ids(both_ways):
    i = np.arange(TILE)[:, None]
    j = np.arange(TILE)[None, :]
    tiles = []
    for step in (0, 1, -1):
        n = i - j + step * TILE
        ids = bucket_of(n, both_ways)
        tiles.append(ids if both_ways else np.where(n < 0, BUCKETS, ids))
    far = bucket_of(np.array([2 * TILE - TILE + 1, -(2 * TILE - TILE + 1)]), both_ways)
    if not both_ways:
        far[1] = BUCKETS
    return np.stack(tiles).astype(np.int32), far.astype(np.int32)


def dot(a, b):
    return jnp.dot(a, b, preferred_element_type=f32)


def dot_nt(a, b):
    return lax.dot_general(a, b, (((1,), (1,)), ((), ())), preferred_element_type=f32)


def rms(v, gain):
    return v * lax.rsqrt(jnp.mean(v * v, axis=-1, keepdims=True) + EPSILON) * gain


def rms_back(v, gain, dy):
    r = lax.rsqrt(jnp.mean(v * v, axis=-1, keepdims=True) + EPSILON)
    dgain = jnp.sum(dy * v * r, axis=0, keepdims=True)
    gdy = dy * gain
    dv = r * gdy - v * (r * r * r * jnp.mean(gdy * v, axis=-1, keepdims=True))
    return dv, dgain


def half_lanes(value, which):
    lane = lax.broadcasted_iota(jnp.int32, value.shape, 1)
    return jnp.where((lane // HEAD) == which, value, jnp.zeros_like(value))


def tile_of(step):
    return {0: 0, 1: 1, -1: 2}.get(step)


def attn_fwd_kernel(has_bias, *refs):
    refs = list(refs)
    src, gain = refs[:2]
    refs = refs[2:]
    ksrc = None
    if not has_bias:
        ksrc = refs.pop(0)
    w, segr, segc = refs[:3]
    refs = refs[3:]
    if has_bias:
        bias, far = refs[:2]
        refs = refs[2:]
    z, q_o, k_o, v_o, o_o, p_o, q_s, k_s, v_s, o_s = refs

    a = rms(src[...].astype(f32), gain[...]).astype(bf16)
    b = a if ksrc is None else ksrc[...]
    for value, weight, out, scr in ((a, 0, q_o, q_s), (b, 1, k_o, k_s), (b, 2, v_o, v_s)):
        full = dot(value, w[weight]).astype(bf16)
        out[...] = full
        for p in range(PAIRS):
            scr[p] = full[:, p * TILE : (p + 1) * TILE]

    def pair(p, carry):
        qp, kp, vp = q_s[p], k_s[p], v_s[p]
        total = [None] * BLOCKS
        for which in range(2):
            h = 2 * p + which
            kz, vz = half_lanes(kp, which), half_lanes(vp, which)
            for bi in range(BLOCKS):
                rows = slice(bi * TILE, (bi + 1) * TILE)
                s = dot_nt(qp[rows], kz)
                if has_bias:
                    parts = []
                    for bj in range(BLOCKS):
                        step = bi - bj
                        part = s[:, bj * TILE : (bj + 1) * TILE]
                        if abs(step) < 2:
                            part = part + bias[h, tile_of(step)]
                        else:
                            part = part + far[h, 0 if step > 0 else 1]
                        parts.append(part)
                    s = jnp.concatenate(parts, axis=1)
                s = jnp.where(segc[rows] == segr[...], s, MASKED)
                e = jnp.exp(s - jnp.max(s, axis=-1, keepdims=True))
                prob = (e * (1.0 / jnp.sum(e, axis=-1, keepdims=True))).astype(bf16)
                p_o[h, rows, :] = prob
                o = dot(prob, vz)
                total[bi] = o if total[bi] is None else total[bi] + o
        o_s[p] = jnp.concatenate(total, axis=0).astype(bf16)
        return carry

    lax.fori_loop(0, PAIRS, pair, 0)
    mixed = jnp.concatenate([o_s[p] for p in range(PAIRS)], axis=1)
    o_o[...] = mixed
    z[...] = src[...].astype(f32) + dot(mixed, w[3])


def attn_fwd(src, gain, w, segr, segc, ksrc=None, bias=None, far=None):
    has_bias = bias is not None
    args = [src, gain] + ([] if has_bias else [ksrc]) + [w, segr, segc]
    vm = pl.BlockSpec(memory_space=pltpu.VMEM)
    specs = [vm] * len(args)
    if has_bias:
        args += [bias, far]
        specs += [vm, pl.BlockSpec(memory_space=pltpu.SMEM)]
    rows = jax.ShapeDtypeStruct((LEN, D), bf16)
    return pl.pallas_call(
        functools.partial(attn_fwd_kernel, has_bias),
        out_shape=(
            jax.ShapeDtypeStruct((LEN, D), f32),
            rows,
            rows,
            rows,
            rows,
            jax.ShapeDtypeStruct((HEADS, LEN, LEN), bf16),
        ),
        in_specs=specs,
        out_specs=(vm,) * 6,
        scratch_shapes=[pltpu.VMEM((PAIRS, LEN, TILE), bf16)] * 4,
        compiler_params=pltpu.CompilerParams(vmem_limit_bytes=VMEM_LIMIT),
        name="self_fwd" if has_bias else "cross_fwd",
    )(*args)


def attn_bwd_kernel(has_bias, *refs):
    refs = list(refs)
    gres, src, gain = refs[:3]
    refs = refs[3:]
    ksrc = None
    if not has_bias:
        ksrc = refs.pop(0)
    w, q_i, k_i, v_i, o_i, p_i = refs[:6]
    refs = refs[6:]
    din, dw, dgain = refs[:3]
    refs = refs[3:]
    if has_bias:
        dtile, dfar = refs[:2]
        refs = refs[2:]
    else:
        dkey = refs.pop(0)
    q_s, k_s, v_s, do_s, dq_s, dk_s, dv_s, ds_s = refs

    g = gres[...].astype(bf16)
    do = dot_nt(g, w[3]).astype(bf16)
    for value, scr in ((q_i[...], q_s), (k_i[...], k_s), (v_i[...], v_s), (do, do_s)):
        for p in range(PAIRS):
            scr[p] = value[:, p * TILE : (p + 1) * TILE]

    def pair(p, carry):
        qp, kp, vp, dop = q_s[p], k_s[p], v_s[p], do_s[p]
        q_t, do_t = qp.T, dop.T
        total = [None] * BLOCKS
        for which in range(2):
            h = 2 * p + which
            kz, vz = half_lanes(kp, which), half_lanes(vp, which)
            diag = {0: None, 1: None, -1: None, 2: None, -2: None}
            for bi in range(BLOCKS):
                rows = slice(bi * TILE, (bi + 1) * TILE)
                dp = dot_nt(dop[rows], vz)
                prob = p_i[h, rows, :].astype(f32)
                t = prob * dp
                ds = t - prob * jnp.sum(t, axis=-1, keepdims=True)
                if has_bias:
                    for bj in range(BLOCKS):
                        step = max(-2, min(2, bi - bj))
                        part = ds[:, bj * TILE : (bj + 1) * TILE]
                        diag[step] = part if diag[step] is None else diag[step] + part
                low = ds.astype(bf16)
                ds_s[which, rows, :] = low
                dq = dot(low, kz)
                total[bi] = dq if total[bi] is None else total[bi] + dq
            if has_bias:
                for step in (0, 1, -1):
                    dtile[h, tile_of(step)] = diag[step]
                for n, step in ((0, 2), (1, -2)):
                    dfar[h, n : n + 1, :] = jnp.sum(diag[step], axis=0, keepdims=True)
            half = slice(which * HEAD, (which + 1) * HEAD)
            dk_s[p, half, :] = dot(q_t[half], ds_s[which]).astype(bf16)
            dv_s[p, half, :] = dot(do_t[half], p_i[h]).astype(bf16)
        dq_s[p] = jnp.concatenate(total, axis=0).astype(bf16)
        return carry

    lax.fori_loop(0, PAIRS, pair, 0)
    v = src[...].astype(f32)
    a = rms(v, gain[...]).astype(bf16)
    a_t = a.T
    b_t = a_t if ksrc is None else ksrc[...].T
    dq = jnp.concatenate([dq_s[p] for p in range(PAIRS)], axis=1)
    dk_t = dk_s[...].reshape(D, LEN)
    dv_t = dv_s[...].reshape(D, LEN)
    query_side = dot_nt(dq, w[0])
    key_side = dot_nt(dk_t.T, w[1]) + dot_nt(dv_t.T, w[2])
    if has_bias:
        query_side = query_side + key_side
    else:
        dkey[...] = key_side.astype(bf16)
    dv, dg = rms_back(v, gain[...], query_side)
    dgain[...] = dg
    din[...] = gres[...].astype(f32) + dv
    dw[0] = dot(a_t, dq).astype(bf16)
    dw[1] = dot_nt(b_t, dk_t).astype(bf16)
    dw[2] = dot_nt(b_t, dv_t).astype(bf16)
    dw[3] = dot(o_i[...].T, g).astype(bf16)


def attn_bwd(gres, src, gain, w, saved, ksrc=None):
    has_bias = ksrc is None
    args = [gres, src, gain] + ([] if has_bias else [ksrc]) + [w, *saved]
    vm = pl.BlockSpec(memory_space=pltpu.VMEM)
    outs = [
        jax.ShapeDtypeStruct((LEN, D), f32),
        jax.ShapeDtypeStruct((4, D, D), bf16),
        jax.ShapeDtypeStruct((1, D), f32),
    ]
    if has_bias:
        outs += [
            jax.ShapeDtypeStruct((HEADS, 3, TILE, TILE), f32),
            jax.ShapeDtypeStruct((HEADS, 2, TILE), f32),
        ]
    else:
        outs += [jax.ShapeDtypeStruct((LEN, D), bf16)]
    return pl.pallas_call(
        functools.partial(attn_bwd_kernel, has_bias),
        out_shape=tuple(outs),
        in_specs=[vm] * len(args),
        out_specs=(vm,) * len(outs),
        scratch_shapes=[pltpu.VMEM((PAIRS, LEN, TILE), bf16)] * 5
        + [pltpu.VMEM((PAIRS, TILE, LEN), bf16)] * 2
        + [pltpu.VMEM((2, LEN, LEN), bf16)],
        compiler_params=pltpu.CompilerParams(vmem_limit_bytes=VMEM_LIMIT),
        name="self_bwd" if has_bias else "cross_bwd",
    )(*args)


GELU_C = float(np.sqrt(2.0 / np.pi))


def gelu_parts(u):
    inner = GELU_C * (u + 0.044715 * (u * u * u))
    t = jnp.tanh(inner)
    h = 0.5 * u * (1.0 + t)
    slope = 0.5 * (1.0 + t) + 0.5 * u * (1.0 - t * t) * GELU_C * (1.0 + 3 * 0.044715 * (u * u))
    return h, slope


def ffn_fwd_kernel(x, gain, wi, wo, out, n_s, acc):
    step = pl.program_id(0)

    @pl.when(step == 0)
    def _():
        v = x[...].astype(f32)
        n_s[...] = rms(v, gain[...]).astype(bf16)
        acc[...] = v

    h, _ = gelu_parts(dot(n_s[...], wi[...]))
    acc[...] += dot(h.astype(bf16), wo[...])

    @pl.when(step == pl.num_programs(0) - 1)
    def _():
        out[...] = acc[...].astype(bf16)


def ffn_fwd(x, gain, wi, wo):
    whole = pl.BlockSpec((LEN, D), lambda c: (0, 0))
    return pl.pallas_call(
        ffn_fwd_kernel,
        grid=(FF // CHUNK,),
        out_shape=jax.ShapeDtypeStruct((LEN, D), bf16),
        in_specs=[
            whole,
            pl.BlockSpec((1, D), lambda c: (0, 0)),
            pl.BlockSpec((D, CHUNK), lambda c: (0, c)),
            pl.BlockSpec((CHUNK, D), lambda c: (c, 0)),
        ],
        out_specs=whole,
        scratch_shapes=[pltpu.VMEM((LEN, D), bf16), pltpu.VMEM((LEN, D), f32)],
        compiler_params=pltpu.CompilerParams(vmem_limit_bytes=VMEM_LIMIT),
        name="ffn_fwd",
    )(x, gain, wi, wo)


def ffn_both_kernel(x, gain, g, wi, wo, out, dx, dgain, dwi, dwo, n_s, nt_s, acc, dn):
    step = pl.program_id(0)

    @pl.when(step == 0)
    def _():
        v = x[...].astype(f32)
        n = rms(v, gain[...]).astype(bf16)
        n_s[...] = n
        nt_s[...] = n.T
        acc[...] = v
        dn[...] = jnp.zeros_like(dn)

    h, slope = gelu_parts(dot(n_s[...], wi[...]))
    h = h.astype(bf16)
    acc[...] += dot(h, wo[...])
    dh = dot_nt(g[...], wo[...])
    du = (slope * dh).astype(bf16)
    dn[...] += dot_nt(du, wi[...])
    dwo[...] = dot(h.T, g[...]).astype(bf16)
    dwi[...] = dot(nt_s[...], du).astype(bf16)

    @pl.when(step == pl.num_programs(0) - 1)
    def _():
        out[...] = acc[...].astype(bf16)
        dv, dg = rms_back(x[...].astype(f32), gain[...], dn[...])
        dgain[...] = dg
        dx[...] = (g[...].astype(f32) + dv).astype(bf16)


def ffn_both(x, gain, g, wi, wo):
    whole = pl.BlockSpec((LEN, D), lambda c: (0, 0))
    one = pl.BlockSpec((1, D), lambda c: (0, 0))
    in_part = pl.BlockSpec((D, CHUNK), lambda c: (0, c))
    out_part = pl.BlockSpec((CHUNK, D), lambda c: (c, 0))
    rows = jax.ShapeDtypeStruct((LEN, D), bf16)
    return pl.pallas_call(
        ffn_both_kernel,
        grid=(FF // CHUNK,),
        out_shape=(
            rows,
            rows,
            jax.ShapeDtypeStruct((1, D), f32),
            jax.ShapeDtypeStruct((D, FF), bf16),
            jax.ShapeDtypeStruct((FF, D), bf16),
        ),
        in_specs=[whole, one, whole, in_part, out_part],
        out_specs=(whole, whole, one, in_part, out_part),
        scratch_shapes=[
            pltpu.VMEM((LEN, D), bf16),
            pltpu.VMEM((D, LEN), bf16),
            pltpu.VMEM((LEN, D), f32),
            pltpu.VMEM((LEN, D), f32),
        ],
        compiler_params=pltpu.CompilerParams(vmem_limit_bytes=VMEM_LIMIT),
        name="ffn_both",
    )(x, gain, g, wi, wo)


ALL = (0, 1, 2, 3)
ENC = (1, 2)
DEC = (0, 3)


def across(x, flip, planes):
    wide, narrow = lax.axis_size("wide"), lax.axis_size("narrow")
    pairs = [(i * narrow + n, (i ^ flip) * narrow + n) for i in range(wide) for n in planes]
    return lax.ppermute(x, ("wide", "narrow"), pairs)


def between(x, pairs):
    return lax.ppermute(x, "narrow", pairs)


def add(a, *others):
    total = a.astype(f32)
    for other in others:
        total = total + other.astype(f32)
    return total.astype(bf16)


def gathered(shard, planes=ALL):
    wide = lax.axis_size("wide")
    if wide != 8:
        return lax.all_gather(shard, "wide", axis=1, tiled=True)
    k, r, c = shard.shape
    h = r // 2
    me = lax.axis_index("wide")
    px = across(shard, 2, planes)
    py = across(shard, 4, planes)
    pc = across(shard, 1, planes)
    pd = jnp.concatenate([across(px[:, :h], 4, planes), across(py[:, h:], 2, planes)], axis=1)
    pieces = {0: shard, 2: px, 4: py, 6: pd, 1: pc}
    for flip in (2, 4, 6):
        pieces[flip ^ 1] = across(pieces[flip], 1, planes)
    full = jnp.zeros((k, 8, r, c), shard.dtype)
    for flip, piece in pieces.items():
        full = lax.dynamic_update_slice(full, piece[:, None], (0, me ^ flip, 0, 0))
    return full.reshape(k, 8 * r, c)


def scattered(full, planes=ALL):
    wide = lax.axis_size("wide")
    k, rows, c = full.shape
    r = rows // wide
    if wide != 8:
        return lax.psum_scatter(full, "wide", scatter_dimension=1, tiled=True)
    h = r // 2
    me = lax.axis_index("wide")
    blocks = full.reshape(k, 8, r, c)

    def block(flip):
        return lax.dynamic_slice(blocks, (0, me ^ flip, 0, 0), (k, 1, r, c))[:, 0]

    part = {f: add(block(f), across(block(f ^ 1), 1, planes)) for f in (6, 2, 4, 0)}
    to_y = across(part[6][:, :h], 2, planes)
    to_x = across(part[6][:, h:], 4, planes)
    for_x = jnp.concatenate([part[2][:, :h], add(part[2][:, h:], to_x)], axis=1)
    for_y = jnp.concatenate([add(part[4][:, :h], to_y), part[4][:, h:]], axis=1)
    return add(part[0], across(for_x, 2, planes), across(for_y, 4, planes))


def from_encoder(share, middle):
    total = add(share, between(share, [(1, 2), (2, 1)]))
    return jnp.where(middle, total, between(total, [(1, 0), (2, 3)]))


def from_decoder(share, middle):
    return from_encoder(between(share, [(0, 1), (3, 2)]), middle)


def summed(x):
    if lax.axis_size("wide") != 8:
        return lax.psum(x, ("wide", "narrow"))
    for flip in (1, 2, 4):
        x = x + across(x, flip, ALL)
    for flip in (1, 2):
        x = x + between(x, [(n, n ^ flip) for n in range(4)])
    return x


def on_device(
    enc_in,
    dec_in,
    dec_cot,
    segments,
    enc_attn_gain,
    enc_query,
    enc_key,
    enc_value,
    enc_output,
    enc_table,
    enc_ffn_gain,
    enc_ffn_in,
    enc_ffn_out,
    dec_self_gain,
    dec_query,
    dec_key,
    dec_value,
    dec_output,
    dec_table,
    dec_cross_gain,
    cross_query,
    cross_key,
    cross_value,
    cross_output,
    dec_ffn_gain,
    dec_ffn_in,
    dec_ffn_out,
):
    plane = lax.axis_index("narrow")
    is_enc = (plane == 1) | (plane == 2)
    row = plane // 2

    def own(x):
        return lax.dynamic_slice_in_dim(x, row * LEN, LEN, 0)

    def pick(enc, dec):
        return jnp.where(is_enc, enc, dec)

    def gain_of(g):
        return g.astype(f32).reshape(1, D)

    seg = lax.dynamic_slice_in_dim(segments, row, 1, 0)
    segr, segc = seg, seg.reshape(LEN, 1)
    src = pick(own(enc_in), own(dec_in))
    cot = own(dec_cot)

    w_attn = gathered(
        jnp.stack(
            [
                pick(enc_query, dec_query),
                pick(enc_key, dec_key),
                pick(enc_value, dec_value),
                pick(enc_output, dec_output),
            ]
        )
    )
    w_in = gathered(pick(enc_ffn_in, dec_ffn_in)[None])[0]
    w_out = gathered(pick(enc_ffn_out, dec_ffn_out)[None])[0]
    w_cross = gathered(jnp.stack([cross_query, cross_key, cross_value, cross_output]), DEC)

    enc_ids, enc_far = tile_ids(True)
    dec_ids, dec_far = tile_ids(False)
    ids = pick(jnp.asarray(enc_ids), jnp.asarray(dec_ids))
    far_ids = pick(jnp.asarray(enc_far), jnp.asarray(dec_far))
    buckets = jnp.arange(BUCKETS + 1, dtype=jnp.int32)
    hot = (ids[None] == buckets[:, None, None, None]).astype(bf16)
    far_hot = (far_ids[None] == buckets[:, None]).astype(bf16)
    table = jnp.concatenate([pick(enc_table, dec_table), jnp.full((1, HEADS), MASKED, bf16)])
    bias = jnp.einsum("bh,bsij->hsij", table, hot, preferred_element_type=f32)
    far = jnp.einsum("bh,bs->hs", table, far_hot, preferred_element_type=f32)

    gain_a = pick(gain_of(enc_attn_gain), gain_of(dec_self_gain))
    z1, *saved = attn_fwd(src, gain_a, w_attn, segr, segc, bias=bias, far=far)
    x1 = z1.astype(bf16)
    enc_gain = gain_of(enc_ffn_gain)
    enc_out = ffn_fwd(x1, enc_gain, w_in, w_out)
    memory = between(enc_out, [(1, 0), (2, 3)])
    gain_c = gain_of(dec_cross_gain)
    z2, *saved_c = attn_fwd(z1, gain_c, w_cross, segr, segc, ksrc=memory)
    z2 = z2.astype(bf16)

    dec_out, gz2, dgain_df, dwi_d, dwo_d = ffn_both(z2, gain_of(dec_ffn_gain), cot, w_in, w_out)
    gz1, dw_c, dgain_c, genc_out = attn_bwd(gz2, z1, gain_c, w_cross, saved_c, ksrc=memory)
    genc = between(genc_out, [(0, 1), (3, 2)])
    _, gx1, dgain_ef, dwi_e, dwo_e = ffn_both(x1, enc_gain, genc, w_in, w_out)
    gres = pick(gx1.astype(f32), gz1)
    din, dw_a, dgain_a, dtile, dfar = attn_bwd(gres, src, gain_a, w_attn, saved)

    def ffn_shares(dwi, dwo, planes):
        return scattered(dwi[None], planes)[0], scattered(dwo[None], planes)[0]

    si_d, so_d = ffn_shares(dwi_d, dwo_d, DEC)
    s_c = scattered(dw_c, DEC)
    si_e, so_e = ffn_shares(dwi_e, dwo_e, ENC)
    s_a = scattered(dw_a)
    gi_d, go_d, g_c, g_s = (from_decoder(s, is_enc).astype(f32) for s in (si_d, so_d, s_c, s_a))
    gi_e, go_e, g_e = (from_encoder(s, is_enc).astype(f32) for s in (si_e, so_e, s_a))

    dtable = jnp.einsum("hsij,bsij->bh", dtile.astype(bf16), hot, preferred_element_type=f32)
    dtable = dtable + jnp.einsum("hsj,bs->bh", dfar, far_hot.astype(f32))
    dtable = jnp.pad(dtable[:BUCKETS].reshape(1, BUCKETS * HEADS), ((0, 0), (0, D - BUCKETS * HEADS)))
    none = jnp.zeros((1, D), f32)

    def when_enc(x):
        return jnp.where(is_enc, x, 0.0)

    def when_dec(x):
        return jnp.where(is_enc, 0.0, x)

    small = jnp.concatenate(
        [
            when_enc(dgain_a),
            when_enc(dgain_ef),
            when_dec(dgain_a),
            when_dec(dgain_c),
            when_dec(dgain_df),
            when_enc(dtable),
            when_dec(dtable),
            none,
        ]
    )
    small = summed(small)
    tables = small[5:7, : BUCKETS * HEADS].reshape(2, BUCKETS, HEADS)

    def by_columns(x):
        parts = lax.all_to_all(x, "narrow", split_axis=1, concat_axis=0, tiled=True)
        rows = [parts[n * LEN : (n + 1) * LEN] for n in range(4)]
        return jnp.concatenate([rows[1], rows[2]]), jnp.concatenate([rows[0], rows[3]])

    enc_cols, dec_cols = by_columns(pick(enc_out, dec_out))
    enc_grad_cols, dec_grad_cols = by_columns(din.astype(bf16))
    return (
        enc_cols,
        dec_cols,
        enc_grad_cols,
        dec_grad_cols,
        small[0],
        g_e[0],
        g_e[1],
        g_e[2],
        g_e[3],
        tables[0],
        small[1],
        gi_e,
        go_e,
        small[2],
        g_s[0],
        g_s[1],
        g_s[2],
        g_s[3],
        tables[1],
        small[3],
        g_c[0],
        g_c[1],
        g_c[2],
        g_c[3],
        small[4],
        gi_d,
        go_d,
    )


def solution(mesh):
    rows, copied = P("wide", None), P()
    block = P("wide", "narrow")
    gains = (copied,)
    attention = (rows,) * 4
    placed = (
        (rows,) * 4
        + gains
        + attention
        + (copied,)
        + gains
        + (rows,) * 2
        + gains
        + attention
        + (copied,)
        + gains
        + attention
        + gains
        + (rows,) * 2
    )
    return jax.shard_map(
        on_device,
        mesh=mesh,
        in_specs=placed,
        out_specs=(block,) * 4 + placed[4:],
        check_vma=False,
    )
```

```python
import functools

import jax
import jax.numpy as jnp
import numpy as np
from jax import lax
from jax.experimental import pallas as pl
from jax.experimental.pallas import tpu as pltpu
from jax.sharding import PartitionSpec as P

D = 768
HEADS = 12
HEAD = 64
PAIRS = HEADS // 2
FF = 3072
BUCKETS = 32
MAXDIST = 128
LEN = 512
TILE = 128
BLOCKS = LEN // TILE
ROWS8 = D // 8

EPSILON = 1e-06
MASKED = -1000000000.0
VMEM_LIMIT = 60 * 1024 * 1024
f32 = jnp.float32
bf16 = jnp.bfloat16


def bucket_of(reverse, both_ways):
    result = np.zeros(reverse.shape, np.int64)
    if both_ways:
        half_count = BUCKETS // 2
        result = result + (reverse < 0) * half_count
        reverse = np.abs(reverse)
    else:
        half_count = BUCKETS
        reverse = np.maximum(reverse, 0)
    exact_count = half_count // 2
    scaled = (
        np.log(np.maximum(reverse, 1) / exact_count)
        / np.log(MAXDIST / exact_count)
        * (half_count - exact_count)
    )
    far_bucket = np.minimum(
        exact_count + np.floor(np.maximum(scaled, 0.0)).astype(np.int64), half_count - 1
    )
    return result + np.where(reverse < exact_count, reverse, far_bucket)


def tile_ids(both_ways):
    i = np.arange(TILE)[:, None]
    j = np.arange(TILE)[None, :]
    tiles = []
    for step in (0, 1, -1):
        n = i - j + step * TILE
        ids = bucket_of(n, both_ways)
        tiles.append(ids if both_ways else np.where(n < 0, BUCKETS, ids))
    far = bucket_of(np.array([2 * TILE - TILE + 1, -(2 * TILE - TILE + 1)]), both_ways)
    if not both_ways:
        far[1] = BUCKETS
    return np.stack(tiles).astype(np.int32), far.astype(np.int32)


def dot(a, b):
    return jnp.dot(a, b, preferred_element_type=f32)


def dot_nt(a, b):
    return lax.dot_general(a, b, (((1,), (1,)), ((), ())), preferred_element_type=f32)


def rms(v, gain):
    return v * lax.rsqrt(jnp.mean(v * v, axis=-1, keepdims=True) + EPSILON) * gain


def rms_back(v, gain, dy):
    r = lax.rsqrt(jnp.mean(v * v, axis=-1, keepdims=True) + EPSILON)
    dgain = jnp.sum(dy * v * r, axis=0, keepdims=True)
    gdy = dy * gain
    dv = r * gdy - v * (r * r * r * jnp.mean(gdy * v, axis=-1, keepdims=True))
    return dv, dgain


def half_lanes(value, which):
    lane = lax.broadcasted_iota(jnp.int32, value.shape, 1)
    return jnp.where((lane // HEAD) == which, value, jnp.zeros_like(value))


def tile_of(step):
    return {0: 0, 1: 1, -1: 2}.get(step)


def part_plan(count, k):
    if count == 1:
        return [(None, 0, k)]
    half = k // 2
    plan = [(0, 0, k), (2, 0, k), (4, 0, k), (6, 0, half), (6, half, half)]
    return plan + [(flip ^ 1, first, units) for flip, first, units in plan]


def attn_loads(me, parts, w_s, units, sem):
    copies = []
    for part, (flip, first, count) in zip(parts, part_plan(len(parts), 4)):
        for u in units:
            if first <= u < first + count:
                to = w_s.at[u] if flip is None else w_s.at[u, me ^ flip]
                copies.append(pltpu.make_async_copy(part.at[u - first], to, sem))
    return copies


def start_all(copies):
    for copy in copies:
        copy.start()


def wait_all(copies):
    for copy in copies:
        copy.wait()


def matrix(w_s, unit):
    return w_s[unit].reshape(D, D)


def put_blocks(me, value, unit, keep, send):
    value = value.astype(bf16)
    odd = (me % 2) == 1
    for i in range(4):
        even_rows = value[2 * i * ROWS8 : (2 * i + 1) * ROWS8]
        odd_rows = value[(2 * i + 1) * ROWS8 : (2 * i + 2) * ROWS8]
        slot = i ^ (me // 2)
        keep[slot, unit] = jnp.where(odd, odd_rows, even_rows)
        send[slot, unit] = jnp.where(odd, even_rows, odd_rows)


def attn_fwd_kernel(has_bias, nparts, *refs):
    refs = list(refs)
    me_ref, src, gain = refs[:3]
    refs = refs[3:]
    ksrc = None
    if not has_bias:
        ksrc = refs.pop(0)
    segr, segc = refs[:2]
    refs = refs[2:]
    if has_bias:
        bias, far = refs[:2]
        refs = refs[2:]
    parts = refs[:nparts]
    refs = refs[nparts:]
    z, zlow, q_o, k_o, v_o, o_o, p_o, w_s, q_s, k_s, v_s, o_s, p_s, w_sem, out_sem = refs
    me = me_ref[0]

    loads = [attn_loads(me, parts, w_s, (u,), w_sem.at[u]) for u in range(4)]
    for load in loads:
        start_all(load)
    a = rms(src[...].astype(f32), gain[...]).astype(bf16)
    b = a if ksrc is None else ksrc[...]
    outs = []
    for value, weight, out, scr in ((a, 0, q_o, q_s), (b, 1, k_o, k_s), (b, 2, v_o, v_s)):
        wait_all(loads[weight])
        full = dot(value, matrix(w_s, weight)).astype(bf16)
        for p in range(PAIRS):
            scr[p] = full[:, p * TILE : (p + 1) * TILE]
        outs.append(pltpu.make_async_copy(scr, out, out_sem.at[weight]))
        outs[-1].start()

    def prob_copy(p):
        return pltpu.make_async_copy(p_s.at[pl.ds(2 * p, 2)], p_o.at[pl.ds(2 * p, 2)], out_sem.at[4])

    def pair(p, carry):
        qp, kp, vp = q_s[p], k_s[p], v_s[p]
        total = [None] * BLOCKS
        for which in range(2):
            h = 2 * p + which
            kz, vz = half_lanes(kp, which), half_lanes(vp, which)
            for bi in range(BLOCKS):
                rows = slice(bi * TILE, (bi + 1) * TILE)
                s = dot_nt(qp[rows], kz)
                if has_bias:
                    tiles = []
                    for bj in range(BLOCKS):
                        step = bi - bj
                        part = s[:, bj * TILE : (bj + 1) * TILE]
                        if abs(step) < 2:
                            part = part + bias[h, tile_of(step)]
                        else:
                            part = part + far[h, 0 if step > 0 else 1]
                        tiles.append(part)
                    s = jnp.concatenate(tiles, axis=1)
                s = jnp.where(segc[rows] == segr[...], s, MASKED)
                e = jnp.exp(s - jnp.max(s, axis=-1, keepdims=True))
                prob = (e * (1.0 / jnp.sum(e, axis=-1, keepdims=True))).astype(bf16)
                p_s[h, rows, :] = prob
                o = dot(prob, vz)
                total[bi] = o if total[bi] is None else total[bi] + o
        o_s[p] = jnp.concatenate(total, axis=0).astype(bf16)
        prob_copy(p).start()
        return carry

    lax.fori_loop(0, PAIRS, pair, 0)
    outs.append(pltpu.make_async_copy(o_s, o_o, out_sem.at[3]))
    outs[-1].start()
    mixed = jnp.concatenate([o_s[p] for p in range(PAIRS)], axis=1)
    wait_all(loads[3])
    result = src[...].astype(f32) + dot(mixed, matrix(w_s, 3))
    z[...] = result
    zlow[...] = result.astype(bf16)
    wait_all(outs)
    for p in range(PAIRS):
        prob_copy(p).wait()


VM = pl.BlockSpec(memory_space=pltpu.VMEM)
SM = pl.BlockSpec(memory_space=pltpu.SMEM)
HBM = pl.BlockSpec(memory_space=pl.ANY)
HEAD_ROWS = jax.ShapeDtypeStruct((PAIRS, LEN, TILE), bf16)
LOW_ROWS = jax.ShapeDtypeStruct((LEN, D), bf16)
FULL_ROWS = jax.ShapeDtypeStruct((LEN, D), f32)
ONE_ROW = jax.ShapeDtypeStruct((1, D), f32)
PARAMS = pltpu.CompilerParams(vmem_limit_bytes=VMEM_LIMIT)


def attn_fwd(me, src, gain, parts, segr, segc, ksrc=None, bias=None, far=None):
    has_bias = bias is not None
    args = [me, src, gain] + ([] if has_bias else [ksrc]) + [segr, segc]
    specs = [SM] + [VM] * (len(args) - 1)
    if has_bias:
        args += [bias, far]
        specs += [VM, SM]
    args += parts
    specs += [HBM] * len(parts)
    return pl.pallas_call(
        functools.partial(attn_fwd_kernel, has_bias, len(parts)),
        out_shape=(FULL_ROWS, LOW_ROWS)
        + (HEAD_ROWS,) * 4
        + (jax.ShapeDtypeStruct((HEADS, LEN, LEN), bf16),),
        in_specs=specs,
        out_specs=(VM,) * 2 + (HBM,) * 5,
        scratch_shapes=[pltpu.VMEM((4, 8, ROWS8, D), bf16)]
        + [pltpu.VMEM((PAIRS, LEN, TILE), bf16)] * 4
        + [pltpu.VMEM((HEADS, LEN, LEN), bf16)]
        + [pltpu.SemaphoreType.DMA((4,)), pltpu.SemaphoreType.DMA((5,))],
        compiler_params=PARAMS,
        name="self_fwd" if has_bias else "cross_fwd",
    )(*args)


def attn_bwd_kernel(has_bias, nparts, *refs):
    refs = list(refs)
    me_ref, gres, src, gain = refs[:4]
    refs = refs[4:]
    gother = ksrc = None
    if has_bias:
        gother = refs.pop(0)
    else:
        ksrc = refs.pop(0)
    q_i, k_i, v_i, o_i, p_i = refs[:5]
    refs = refs[5:]
    parts = refs[:nparts]
    refs = refs[nparts:]
    din, keep, send, dgain = refs[:4]
    refs = refs[4:]
    if has_bias:
        dtile, dfar = refs[:2]
        refs = refs[2:]
    else:
        dkey = refs.pop(0)
    w_s, p_s, do_s, dq_s, dk_s, dv_s, ds_s, keep_s, send_s, w_sem, p_sem, out_sem = refs
    me = me_ref[0]

    out_load = attn_loads(me, parts, w_s, (3,), w_sem.at[0])
    rest_load = attn_loads(me, parts, w_s, (0, 1, 2), w_sem.at[1])

    def prob_copy(p):
        return pltpu.make_async_copy(p_i.at[pl.ds(2 * p, 2)], p_s.at[pl.ds(2 * p, 2)], p_sem.at[p])

    start_all(out_load)
    for p in range(PAIRS):
        prob_copy(p).start()
    start_all(rest_load)
    base = gres[...].astype(f32)
    if has_bias:
        base = jnp.where(me_ref[1] == 1, gother[...].astype(f32), base)
    g = base.astype(bf16)
    wait_all(out_load)
    do = dot_nt(g, matrix(w_s, 3)).astype(bf16)
    for p in range(PAIRS):
        do_s[p] = do[:, p * TILE : (p + 1) * TILE]

    def pair(p, carry):
        qp, kp, vp, dop = q_i[p], k_i[p], v_i[p], do_s[p]
        q_t, do_t = qp.T, dop.T
        total = [None] * BLOCKS
        prob_copy(p).wait()
        for which in range(2):
            h = 2 * p + which
            kz, vz = half_lanes(kp, which), half_lanes(vp, which)
            diag = {0: None, 1: None, -1: None, 2: None, -2: None}
            for bi in range(BLOCKS):
                rows = slice(bi * TILE, (bi + 1) * TILE)
                dp = dot_nt(dop[rows], vz)
                prob = p_s[h, rows, :].astype(f32)
                t = prob * dp
                ds = t - prob * jnp.sum(t, axis=-1, keepdims=True)
                if has_bias:
                    for bj in range(BLOCKS):
                        step = max(-2, min(2, bi - bj))
                        part = ds[:, bj * TILE : (bj + 1) * TILE]
                        diag[step] = part if diag[step] is None else diag[step] + part
                low = ds.astype(bf16)
                ds_s[which, rows, :] = low
                dq = dot(low, kz)
                total[bi] = dq if total[bi] is None else total[bi] + dq
            if has_bias:
                for step in (0, 1, -1):
                    dtile[h, tile_of(step)] = diag[step].astype(bf16)
                for n, step in ((0, 2), (1, -2)):
                    dfar[h, n : n + 1, :] = jnp.sum(diag[step], axis=0, keepdims=True)
            half = slice(which * HEAD, (which + 1) * HEAD)
            dk_s[p, half, :] = dot(q_t[half], ds_s[which]).astype(bf16)
            dv_s[p, half, :] = dot(do_t[half], p_s[h]).astype(bf16)
        dq_s[p] = jnp.concatenate(total, axis=0).astype(bf16)
        return carry

    lax.fori_loop(0, PAIRS, pair, 0)
    v = src[...].astype(f32)
    a = rms(v, gain[...]).astype(bf16)
    a_t = a.T
    b_t = a_t if ksrc is None else ksrc[...].T
    dq = jnp.concatenate([dq_s[p] for p in range(PAIRS)], axis=1)
    dk_t = dk_s[...].reshape(D, LEN)
    dv_t = dv_s[...].reshape(D, LEN)
    put_blocks(me, dot(a_t, dq), 0, keep_s, send_s)
    put_blocks(me, dot_nt(b_t, dk_t), 1, keep_s, send_s)
    put_blocks(me, dot_nt(b_t, dv_t), 2, keep_s, send_s)
    mixed = jnp.concatenate([o_i[p] for p in range(PAIRS)], axis=1)
    put_blocks(me, dot(mixed.T, g), 3, keep_s, send_s)
    outs = [
        pltpu.make_async_copy(send_s, send, out_sem.at[0]),
        pltpu.make_async_copy(keep_s, keep, out_sem.at[1]),
    ]
    start_all(outs)
    wait_all(rest_load)
    query_side = dot_nt(dq, matrix(w_s, 0))
    key_side = dot_nt(dk_t.T, matrix(w_s, 1)) + dot_nt(dv_t.T, matrix(w_s, 2))
    if has_bias:
        query_side = query_side + key_side
    else:
        dkey[...] = key_side.astype(bf16)
    dv, dg = rms_back(v, gain[...], query_side)
    dgain[...] = dg
    din[...] = (base + dv).astype(din.dtype)
    wait_all(outs)


BLOCKS4 = jax.ShapeDtypeStruct((4, 4, ROWS8, D), bf16)
BLOCKS8 = jax.ShapeDtypeStruct((4, 8, ROWS8, D), bf16)


def attn_bwd(me, gres, src, gain, parts, saved, ksrc=None, gother=None):
    has_bias = ksrc is None
    args = [me, gres, src, gain, gother if has_bias else ksrc, *saved, *parts]
    specs = [SM] + [VM] * 8 + [HBM] + [HBM] * len(parts)
    outs = [LOW_ROWS if has_bias else FULL_ROWS, BLOCKS4, BLOCKS4, ONE_ROW]
    if has_bias:
        outs += [
            jax.ShapeDtypeStruct((HEADS, 3, TILE, TILE), bf16),
            jax.ShapeDtypeStruct((HEADS, 2, TILE), f32),
        ]
    else:
        outs += [LOW_ROWS]
    return pl.pallas_call(
        functools.partial(attn_bwd_kernel, has_bias, len(parts)),
        out_shape=tuple(outs),
        in_specs=specs,
        out_specs=tuple([VM, HBM, HBM] + [VM] * (len(outs) - 3)),
        scratch_shapes=[
            pltpu.VMEM((4, 8, ROWS8, D), bf16),
            pltpu.VMEM((HEADS, LEN, LEN), bf16),
            pltpu.VMEM((PAIRS, LEN, TILE), bf16),
            pltpu.VMEM((PAIRS, LEN, TILE), bf16),
            pltpu.VMEM((PAIRS, TILE, LEN), bf16),
            pltpu.VMEM((PAIRS, TILE, LEN), bf16),
            pltpu.VMEM((2, LEN, LEN), bf16),
            pltpu.VMEM((4, 4, ROWS8, D), bf16),
            pltpu.VMEM((4, 4, ROWS8, D), bf16),
            pltpu.SemaphoreType.DMA((2,)),
            pltpu.SemaphoreType.DMA((PAIRS,)),
            pltpu.SemaphoreType.DMA((2,)),
        ],
        compiler_params=PARAMS,
        name="self_bwd" if has_bias else "cross_bwd",
    )(*args)


GELU_C = float(np.sqrt(2.0 / np.pi))


def gelu_parts(u):
    square = u * u
    t = jnp.tanh(GELU_C * (u + 0.044715 * (u * square)))
    half = 0.5 + 0.5 * t
    slope = half + (half * (1.0 - t)) * (u * (GELU_C + (3 * 0.044715 * GELU_C) * square))
    return u * half, slope


def ffn_kernel(mode, nparts, *refs):
    fwd, bwd = mode != "bwd", mode != "fwd"
    refs = list(refs)
    me_ref, x, gain = refs[:3]
    refs = refs[3:]
    g = refs.pop(0) if bwd else None
    if mode == "bwd":
        h_i, slope_i = refs[:2]
        refs = refs[2:]
    parts = refs[:nparts]
    refs = refs[nparts:]
    out = refs.pop(0) if fwd else None
    if mode == "fwd":
        h_o, slope_o = refs[:2]
        refs = refs[2:]
    if bwd:
        dx, dgain, keep, send = refs[:4]
        refs = refs[4:]
    wi_s, wo_s, w_sem = refs[:3]
    refs = refs[3:]
    if fwd:
        n_s, acc = refs[:2]
        refs = refs[2:]
    if bwd:
        nt_s, dn, keep_s, send_s, out_sem = refs
    me = me_ref[0]
    step = pl.program_id(0)
    plan = part_plan(nparts, 8)

    def in_loads(unit):
        copies = []
        for part, (flip, first, count) in zip(parts, plan):
            if first == 0:
                to = wi_s.at[unit] if flip is None else wi_s.at[unit, me ^ flip]
                copies.append(pltpu.make_async_copy(part.at[unit], to, w_sem.at[unit]))
        return copies

    def out_loads():
        copies = []
        for part, (flip, first, count) in zip(parts, plan):
            if first + count == 8:
                if flip is None:
                    for k in range(4):
                        copies.append(
                            pltpu.make_async_copy(part.at[4 + k], wo_s.at[:, k], w_sem.at[4])
                        )
                else:
                    copies.append(
                        pltpu.make_async_copy(
                            part.at[pl.ds(4 - first, 4)], wo_s.at[me ^ flip], w_sem.at[4]
                        )
                    )
        return copies

    @pl.when(step == 0)
    def _():
        start_all(in_loads(0))
        start_all(out_loads())
        for unit in range(1, 4):
            start_all(in_loads(unit))
        v = x[...].astype(f32)
        n = rms(v, gain[...]).astype(bf16)
        if fwd:
            n_s[...] = n
            acc[...] = v
        if bwd:
            nt_s[...] = n.T
            dn[...] = jnp.zeros_like(dn)

    for unit in range(4):

        @pl.when(step == unit)
        def _():
            wait_all(in_loads(unit))

    wi = wi_s[step].reshape(D, D)
    if fwd:
        h, slope = gelu_parts(dot(n_s[...], wi))
        h = h.astype(bf16)
        if mode == "fwd":
            h_o[0] = h
            slope_o[0] = slope.astype(bf16)
    else:
        h, slope = h_i[0], slope_i[0].astype(f32)

    @pl.when(step == 0)
    def _():
        wait_all(out_loads())

    wo = wo_s[pl.ds(2 * step, 2)].reshape(D, D)
    if fwd:
        acc[...] += dot(h, wo)
    if bwd:
        du = (slope * dot_nt(g[...], wo)).astype(bf16)
        dn[...] += dot_nt(du, wi)
        put_blocks(me, dot(nt_s[...], du), step, keep_s, send_s)
        dwo = dot(h.T, g[...]).astype(bf16)
        odd = (me % 2) == 1
        slot = step ^ (me // 2)
        for k in range(4):
            first, second = dwo[k * ROWS8 : (k + 1) * ROWS8], dwo[(4 + k) * ROWS8 : (5 + k) * ROWS8]
            keep_s[slot, 4 + k] = jnp.where(odd, second, first)
            send_s[slot, 4 + k] = jnp.where(odd, first, second)

        def outs(c):
            slot = c ^ (me // 2)
            copies = []
            for n, (here, there) in enumerate(((send_s, send), (keep_s, keep))):
                copies.append(
                    pltpu.make_async_copy(here.at[:, c], there.at[:, c], out_sem.at[2 * n])
                )
                last = pl.ds(4, 4)
                copies.append(
                    pltpu.make_async_copy(here.at[slot, last], there.at[slot, last], out_sem.at[2 * n + 1])
                )
            return copies

        start_all(outs(step))

    @pl.when(step == pl.num_programs(0) - 1)
    def _():
        if fwd:
            out[...] = acc[...].astype(bf16)
        if bwd:
            dv, dg = rms_back(x[...].astype(f32), gain[...], dn[...])
            dgain[...] = dg
            dx[...] = (g[...].astype(f32) + dv).astype(bf16)
            for c in range(4):
                wait_all(outs(c))


def ffn(mode, me, x, gain, parts, g=None, saved=()):
    fwd, bwd = mode != "bwd", mode != "fwd"
    whole = pl.BlockSpec((LEN, D), lambda c: (0, 0))
    one = pl.BlockSpec((1, D), lambda c: (0, 0))
    hidden = pl.BlockSpec((1, LEN, D), lambda c: (c, 0, 0))
    hidden_shape = jax.ShapeDtypeStruct((4, LEN, D), bf16)
    args, specs = [me, x, gain], [SM, whole, one]
    if bwd:
        args, specs = args + [g], specs + [whole]
    args += list(saved)
    specs += [hidden] * len(saved)
    args += parts
    specs += [HBM] * len(parts)
    shapes, out_specs = [], []
    scratch = [
        pltpu.VMEM((4, 8, ROWS8, D), bf16),
        pltpu.VMEM((8, 4, ROWS8, D), bf16),
        pltpu.SemaphoreType.DMA((5,)),
    ]
    if fwd:
        shapes, out_specs = [LOW_ROWS], [whole]
        scratch += [pltpu.VMEM((LEN, D), bf16), pltpu.VMEM((LEN, D), f32)]
    if mode == "fwd":
        shapes += [hidden_shape] * 2
        out_specs += [hidden] * 2
    if bwd:
        shapes += [LOW_ROWS, ONE_ROW, BLOCKS8, BLOCKS8]
        out_specs += [whole, one, HBM, HBM]
        scratch += [
            pltpu.VMEM((D, LEN), bf16),
            pltpu.VMEM((LEN, D), f32),
            pltpu.VMEM((4, 8, ROWS8, D), bf16),
            pltpu.VMEM((4, 8, ROWS8, D), bf16),
            pltpu.SemaphoreType.DMA((4,)),
        ]
    return pl.pallas_call(
        functools.partial(ffn_kernel, mode, len(parts)),
        grid=(4,),
        out_shape=tuple(shapes),
        in_specs=specs,
        out_specs=tuple(out_specs),
        scratch_shapes=scratch,
        compiler_params=PARAMS,
        name="ffn_" + mode,
    )(*args)


def wide_add(*values):
    total = values[0].astype(f32)
    for value in values[1:]:
        total = total + value.astype(f32)
    return total.astype(bf16)


def diag_kernel(keep, recv, by_x, by_y):
    half = by_x.shape[0]
    total = wide_add(keep[0], recv[0])
    by_x[...] = total[:half]
    by_y[...] = total[half:]


def diag_add(keep, recv):
    _, k, r, c = keep.shape
    last = pl.BlockSpec((1, k, r, c), lambda i: (3, 0, 0, 0))
    half = pl.BlockSpec((k // 2, r, c), lambda i: (0, 0, 0))
    shape = jax.ShapeDtypeStruct((k // 2, r, c), bf16)
    return pl.pallas_call(
        diag_kernel,
        grid=(1,),
        out_shape=(shape, shape),
        in_specs=[last, last],
        out_specs=(half, half),
        compiler_params=PARAMS,
        name="diag_add",
    )(keep, recv)


def rest_kernel(keep, recv, from_x, from_y, own, for_x, for_y):
    half = from_x.shape[0]
    own[...] = wide_add(keep[0], recv[0])
    for_x[:half] = wide_add(keep[1, :half], recv[1, :half])
    for_x[half:] = wide_add(keep[1, half:], recv[1, half:], from_y[...])
    for_y[:half] = wide_add(keep[2, :half], recv[2, :half], from_x[...])
    for_y[half:] = wide_add(keep[2, half:], recv[2, half:])


def rest_add(keep, recv, from_x, from_y):
    _, k, r, c = keep.shape
    first = pl.BlockSpec((3, k, r, c // 2), lambda i: (0, 0, 0, i))
    half = pl.BlockSpec((k // 2, r, c // 2), lambda i: (0, 0, i))
    full = pl.BlockSpec((k, r, c // 2), lambda i: (0, 0, i))
    shape = jax.ShapeDtypeStruct((k, r, c), bf16)
    return pl.pallas_call(
        rest_kernel,
        grid=(2,),
        out_shape=(shape,) * 3,
        in_specs=[first, first, half, half],
        out_specs=(full,) * 3,
        compiler_params=PARAMS,
        name="rest_add",
    )(keep, recv, from_x, from_y)


ALL = (0, 1, 2, 3)
ENC = (1, 2)
DEC = (0, 3)


def across(x, flip, planes):
    wide, narrow = lax.axis_size("wide"), lax.axis_size("narrow")
    pairs = [(i * narrow + n, (i ^ flip) * narrow + n) for i in range(wide) for n in planes]
    return lax.ppermute(x, ("wide", "narrow"), pairs)


def between(x, pairs):
    return lax.ppermute(x, "narrow", pairs)


def in_units(local):
    return jnp.transpose(local.reshape(local.shape[0], 4, D), (1, 0, 2))


def out_units(local):
    return local.reshape(4, local.shape[0] // 4, D)


def tie(*values):
    return lax.optimization_barrier(values)


def whole_pack(shard):
    k = shard.shape[0]
    full = lax.all_gather(shard, "wide", axis=1)
    if k == 8:
        inner = full[:4].reshape(4, 8, ROWS8, D)
        outer = jnp.transpose(full[4:], (1, 0, 2, 3)).reshape(8, 4, ROWS8, D)
        return [jnp.concatenate([inner, jnp.transpose(outer, (1, 0, 2, 3))])]
    return [full.reshape(k, 8, ROWS8, D)]


def gather_near(shard, planes=ALL):
    return across(shard, 2, planes), across(shard, 4, planes), across(shard, 1, planes)


def gather_far(shard, near, planes=ALL):
    px, py, pc = near
    k = shard.shape[0]
    first = across(px[: k // 2], 4, planes)
    second = across(py[k // 2 :], 2, planes)
    parts = [px, py, first, second]
    return [shard] + parts + [pc] + [across(part, 1, planes) for part in parts]


def whole_scatter(keep, send):
    k = keep.shape[1]
    blocks = jnp.stack([keep, send], axis=1).reshape(8, k, ROWS8, D)
    inner = jnp.transpose(blocks[:, :4], (1, 0, 2, 3)).reshape(4, D, D)
    inner = lax.psum_scatter(inner, "wide", scatter_dimension=1, tiled=True)
    if k == 4:
        return inner
    outer = lax.psum_scatter(blocks[:, 4:].reshape(FF, D), "wide", scatter_dimension=0, tiled=True)
    return jnp.concatenate([inner, outer.reshape(inner.shape)])


class Scatter:
    def __init__(self, keep, send, planes=ALL):
        self.keep, self.planes = keep, planes
        self.small = lax.axis_size("wide") == 8
        self.state = (send,)
        if self.small:
            self.state = (across(send, 1, planes),)
        self.phase = 0

    def go(self):
        if not self.small:
            return self
        if self.phase == 0:
            (self.recv,) = self.state
            by_x, by_y = diag_add(self.keep, self.recv)
            self.state = across(by_x, 2, self.planes), across(by_y, 4, self.planes)
        elif self.phase == 1:
            own, for_x, for_y = rest_add(self.keep, self.recv, *self.state)
            self.state = own, across(for_x, 2, self.planes), across(for_y, 4, self.planes)
        self.phase += 1
        return self

    def result(self):
        if not self.small:
            return whole_scatter(self.keep, self.state[0])
        return wide_add(*self.state)


def tie_all(scatters, *values):
    counts = [len(s.state) for s in scatters]
    flat = tie(*[v for s in scatters for v in s.state], *values)
    for s, count in zip(scatters, counts):
        s.state, flat = flat[:count], flat[count:]
    return flat


def over_planes(share, middle):
    total = wide_add(share, between(share, [(1, 2), (2, 1)]))
    return jnp.where(middle, total, between(total, [(1, 0), (2, 3)]))


def summed(x):
    if lax.axis_size("wide") != 8:
        return lax.psum(x, ("wide", "narrow"))
    for flip in (1, 2, 4):
        x = x + across(x, flip, ALL)
    for flip in (1, 2):
        x = x + between(x, [(n, n ^ flip) for n in range(4)])
    return x


def on_device(
    enc_in,
    dec_in,
    dec_cot,
    segments,
    enc_attn_gain,
    enc_query,
    enc_key,
    enc_value,
    enc_output,
    enc_table,
    enc_ffn_gain,
    enc_ffn_in,
    enc_ffn_out,
    dec_self_gain,
    dec_query,
    dec_key,
    dec_value,
    dec_output,
    dec_table,
    dec_cross_gain,
    cross_query,
    cross_key,
    cross_value,
    cross_output,
    dec_ffn_gain,
    dec_ffn_in,
    dec_ffn_out,
):
    plane = lax.axis_index("narrow")
    is_enc = (plane == 1) | (plane == 2)
    row = plane // 2

    def own(x):
        return lax.dynamic_slice_in_dim(x, row * LEN, LEN, 0)

    def pick(enc, dec):
        return jnp.where(is_enc, enc, dec)

    def gain_of(g):
        return g.astype(f32).reshape(1, D)

    seg = lax.dynamic_slice_in_dim(segments, row, 1, 0)
    segr, segc = seg, seg.reshape(LEN, 1)
    src = pick(own(enc_in), own(dec_in))
    cot = own(dec_cot)

    me = lax.axis_index("wide") if lax.axis_size("wide") == 8 else 0
    me = jnp.stack([jnp.asarray(me, jnp.int32), is_enc.astype(jnp.int32)])

    pack_a = jnp.stack(
        [
            pick(enc_query, dec_query),
            pick(enc_key, dec_key),
            pick(enc_value, dec_value),
            pick(enc_output, dec_output),
        ]
    )
    pack_f = jnp.concatenate(
        [in_units(pick(enc_ffn_in, dec_ffn_in)), out_units(pick(enc_ffn_out, dec_ffn_out))]
    )
    pack_c = jnp.stack([cross_query, cross_key, cross_value, cross_output])
    small = lax.axis_size("wide") == 8
    if small:
        near_a = gather_near(pack_a)

    enc_ids, enc_far = tile_ids(True)
    dec_ids, dec_far = tile_ids(False)
    ids = pick(jnp.asarray(enc_ids), jnp.asarray(dec_ids))
    far_ids = pick(jnp.asarray(enc_far), jnp.asarray(dec_far))
    buckets = jnp.arange(BUCKETS + 1, dtype=jnp.int32)
    hot = (ids[None] == buckets[:, None, None, None]).astype(bf16)
    far_hot = (far_ids[None] == buckets[:, None]).astype(bf16)
    table = jnp.concatenate([pick(enc_table, dec_table), jnp.full((1, HEADS), MASKED, bf16)])
    bias = jnp.einsum("bh,bsij->hsij", table, hot, preferred_element_type=f32)
    far = jnp.einsum("bh,bs->hs", table, far_hot, preferred_element_type=f32)

    gain_a = pick(gain_of(enc_attn_gain), gain_of(dec_self_gain))
    enc_gain = gain_of(enc_ffn_gain)
    gain_c = gain_of(dec_cross_gain)
    if small:
        *near_a, pack_f, bias, far, src, cot, segc, me = tie(
            *near_a, pack_f, bias, far, src, cot, segc, me
        )
        w_attn = gather_far(pack_a, near_a)
        near_f = gather_near(pack_f)
    else:
        w_attn, w_ffn, w_cross = whole_pack(pack_a), whole_pack(pack_f), whole_pack(pack_c)
    z1, x1, *saved = attn_fwd(me, src, gain_a, w_attn, segr, segc, bias=bias, far=far)
    if small:
        z1, x1, *near_f, pack_c = tie(z1, x1, *near_f, pack_c)
        w_ffn = gather_far(pack_f, near_f)
        near_c = gather_near(pack_c, DEC)
    enc_out, *saved_f = ffn("fwd", me, x1, enc_gain, w_ffn)
    if small:
        enc_out, *near_c = tie(enc_out, *near_c)
    memory = between(enc_out, [(1, 0), (2, 3)])
    if small:
        w_cross = gather_far(pack_c, near_c, DEC)
    _, z2, *saved_c = attn_fwd(me, z1, gain_c, w_cross, segr, segc, ksrc=memory)

    def by_columns(x):
        return lax.all_to_all(x, "narrow", split_axis=1, concat_axis=0, tiled=True)

    def rows_by_block(parts):
        rows = [parts[n * LEN : (n + 1) * LEN] for n in range(4)]
        return jnp.concatenate([rows[1], rows[2]]), jnp.concatenate([rows[0], rows[3]])

    dec_out, gz2, dgain_df, *blocks = ffn("both", me, z2, gain_of(dec_ffn_gain), w_ffn, cot)
    sum_df = Scatter(*blocks, DEC)
    out_cols = by_columns(pick(enc_out, dec_out))
    gz1, *blocks, dgain_c, genc_out = attn_bwd(me, gz2, z1, gain_c, w_cross, saved_c, ksrc=memory)
    genc_out, gz1, out_cols, *blocks = tie_all([sum_df], genc_out, gz1, out_cols, *blocks)
    genc = between(genc_out, [(0, 1), (3, 2)])
    sum_c = Scatter(*blocks, DEC)
    sum_df.go()
    (genc,) = tie_all([sum_df, sum_c], genc)
    sum_df.go()
    sum_c.go()
    gx1, dgain_ef, *blocks = ffn("bwd", me, x1, enc_gain, w_ffn, genc, saved_f)
    gx1, *blocks = tie_all([sum_df, sum_c], gx1, *blocks)
    sum_ef = Scatter(*blocks, ENC)
    s_df = sum_df.result()
    part_df = between(s_df, [(0, 1), (3, 2)])
    sum_c.go()
    din, *blocks, dgain_a, dtile, dfar = attn_bwd(
        me, gz1, src, gain_a, w_attn, saved, gother=gx1
    )
    din, dgain_a, dtile, dfar, part_df, *blocks = tie_all(
        [sum_ef, sum_c], din, dgain_a, dtile, dfar, part_df, *blocks
    )
    sum_a = Scatter(*blocks)
    grad_cols = by_columns(din)
    sum_ef.go()
    s_c = sum_c.result()
    part_c = between(s_c, [(0, 1), (3, 2)])
    tie_all([sum_ef, sum_a])
    sum_ef.go()
    sum_a.go()
    s_ef = sum_ef.result()
    s_a = sum_a.go().result()
    part_s = between(s_a, [(0, 1), (3, 2)])

    def rows_of(f):
        return jnp.transpose(f[:4], (1, 0, 2)).reshape(-1, FF), f[4:].reshape(-1, D)

    g_df, g_c, g_s, g_ef, g_e = (
        over_planes(s, is_enc).astype(f32) for s in (part_df, part_c, part_s, s_ef, s_a)
    )
    gi_d, go_d = rows_of(g_df)
    gi_e, go_e = rows_of(g_ef)

    dtable = jnp.einsum("hsij,bsij->bh", dtile, hot, preferred_element_type=f32)
    dtable = dtable + jnp.einsum("hsj,bs->bh", dfar, far_hot.astype(f32))
    dtable = jnp.pad(dtable[:BUCKETS].reshape(1, BUCKETS * HEADS), ((0, 0), (0, D - BUCKETS * HEADS)))
    none = jnp.zeros((1, D), f32)

    def when_enc(x):
        return jnp.where(is_enc, x, 0.0)

    def when_dec(x):
        return jnp.where(is_enc, 0.0, x)

    sums = jnp.concatenate(
        [
            when_enc(dgain_a),
            when_enc(dgain_ef),
            when_dec(dgain_a),
            when_dec(dgain_c),
            when_dec(dgain_df),
            when_enc(dtable),
            when_dec(dtable),
            none,
        ]
    )
    sums = summed(sums)
    tables = sums[5:7, : BUCKETS * HEADS].reshape(2, BUCKETS, HEADS)

    enc_cols, dec_cols = rows_by_block(out_cols)
    enc_grad_cols, dec_grad_cols = rows_by_block(grad_cols)
    return (
        enc_cols,
        dec_cols,
        enc_grad_cols,
        dec_grad_cols,
        sums[0],
        g_e[0],
        g_e[1],
        g_e[2],
        g_e[3],
        tables[0],
        sums[1],
        gi_e,
        go_e,
        sums[2],
        g_s[0],
        g_s[1],
        g_s[2],
        g_s[3],
        tables[1],
        sums[3],
        g_c[0],
        g_c[1],
        g_c[2],
        g_c[3],
        sums[4],
        gi_d,
        go_d,
    )


def solution(mesh):
    rows, copied = P("wide", None), P()
    block = P("wide", "narrow")
    gains = (copied,)
    attention = (rows,) * 4
    placed = (
        (rows,) * 4
        + gains
        + attention
        + (copied,)
        + gains
        + (rows,) * 2
        + gains
        + attention
        + (copied,)
        + gains
        + attention
        + gains
        + (rows,) * 2
    )
    return jax.shard_map(
        on_device,
        mesh=mesh,
        in_specs=placed,
        out_specs=(block,) * 4 + placed[4:],
        check_vma=False,
    )
```

```python
import functools

import jax
import jax.numpy as jnp
import numpy as np
from jax import lax
from jax.experimental import pallas as pl
from jax.experimental.pallas import tpu as pltpu
from jax.sharding import PartitionSpec as P

D = 768
HEADS = 12
HEAD = 64
PAIRS = HEADS // 2
FF = 3072
BUCKETS = 32
MAXDIST = 128
LEN = 512
TILE = 128
BLOCKS = LEN // TILE
ROWS8 = D // 8
EXTRA = 16

EPSILON = 1e-06
MASKED = -1000000000.0
VMEM_LIMIT = 60 * 1024 * 1024
f32 = jnp.float32
bf16 = jnp.bfloat16


def bucket_of(reverse, both_ways):
    result = np.zeros(reverse.shape, np.int64)
    if both_ways:
        half_count = BUCKETS // 2
        result = result + (reverse < 0) * half_count
        reverse = np.abs(reverse)
    else:
        half_count = BUCKETS
        reverse = np.maximum(reverse, 0)
    exact_count = half_count // 2
    scaled = (
        np.log(np.maximum(reverse, 1) / exact_count)
        / np.log(MAXDIST / exact_count)
        * (half_count - exact_count)
    )
    far_bucket = np.minimum(
        exact_count + np.floor(np.maximum(scaled, 0.0)).astype(np.int64), half_count - 1
    )
    return result + np.where(reverse < exact_count, reverse, far_bucket)


def tile_ids(both_ways):
    i = np.arange(TILE)[:, None]
    j = np.arange(TILE)[None, :]
    tiles = []
    for step in (0, 1, -1):
        n = i - j + step * TILE
        ids = bucket_of(n, both_ways)
        tiles.append(ids if both_ways else np.where(n < 0, BUCKETS, ids))
    far = bucket_of(np.array([2 * TILE - TILE + 1, -(2 * TILE - TILE + 1)]), both_ways)
    if not both_ways:
        far[1] = BUCKETS
    return np.stack(tiles).astype(np.int32), far.astype(np.int32)


def sum_ids(both_ways):
    p = np.arange(2 * TILE)
    parts = []
    for step in (0, 1, -1):
        n = TILE - 1 - p + step * TILE
        ids = bucket_of(n, both_ways)
        parts.append(np.where((p == 2 * TILE - 1) | ((n < 0) & (not both_ways)), TILE, ids))
    far = tile_ids(both_ways)[1]
    parts += [np.full(TILE, b if b < BUCKETS else TILE) for b in far]
    return np.concatenate(parts).astype(np.int32)


def dot(a, b):
    return jnp.dot(a, b, preferred_element_type=f32)


def dot_nt(a, b):
    return lax.dot_general(a, b, (((1,), (1,)), ((), ())), preferred_element_type=f32)


def rms(v, gain):
    return v * lax.rsqrt(jnp.mean(v * v, axis=-1, keepdims=True) + EPSILON) * gain


def rms_back(v, gain, dy):
    r = lax.rsqrt(jnp.mean(v * v, axis=-1, keepdims=True) + EPSILON)
    dgain = jnp.sum(dy * v * r, axis=0, keepdims=True)
    gdy = dy * gain
    dv = r * gdy - v * (r * r * r * jnp.mean(gdy * v, axis=-1, keepdims=True))
    return dv, dgain


def half_lanes(value, which):
    lane = lax.broadcasted_iota(jnp.int32, value.shape, 1)
    return jnp.where((lane // HEAD) == which, value, jnp.zeros_like(value))


def tile_of(step):
    return {0: 0, 1: 1, -1: 2}.get(step)


def part_plan(count, k):
    if count == 1:
        return [(None, 0, k)]
    half = k // 2
    plan = [(0, 0, k), (2, 0, k), (4, 0, k), (6, 0, half), (6, half, half)]
    return plan + [(flip ^ 1, first, units) for flip, first, units in plan]


def attn_loads(me, parts, w_s, units, sem):
    copies = []
    for part, (flip, first, count) in zip(parts, part_plan(len(parts), 4)):
        for u in units:
            if first <= u < first + count:
                to = w_s.at[u] if flip is None else w_s.at[u, me ^ flip]
                copies.append(pltpu.make_async_copy(part.at[u - first], to, sem))
    return copies


def only(role, kernel):
    if role is None:
        return kernel

    def guarded(me_ref, *refs):
        @pl.when(me_ref[1] == role)
        def _():
            kernel(me_ref, *refs)

    return guarded


def start_all(copies):
    for copy in copies:
        copy.start()


def wait_all(copies):
    for copy in copies:
        copy.wait()


def matrix(w_s, unit):
    return w_s[unit].reshape(D, D)


def put_blocks(me, value, unit, keep, send):
    value = value.astype(bf16)
    odd = (me % 2) == 1
    for i in range(4):
        even_rows = value[2 * i * ROWS8 : (2 * i + 1) * ROWS8]
        odd_rows = value[(2 * i + 1) * ROWS8 : (2 * i + 2) * ROWS8]
        slot = i ^ (me // 2)
        rows = slice(unit * ROWS8, (unit + 1) * ROWS8) if isinstance(unit, int) else unit
        keep[slot, rows, :] = jnp.where(odd, odd_rows, even_rows)
        send[slot, rows, :] = jnp.where(odd, even_rows, odd_rows)


def attn_fwd_kernel(has_bias, nparts, *refs):
    refs = list(refs)
    me_ref, src, gain = refs[:3]
    refs = refs[3:]
    ksrc = None
    if not has_bias:
        ksrc = refs.pop(0)
    segr, segc = refs[:2]
    refs = refs[2:]
    if has_bias:
        bias, far = refs[:2]
        refs = refs[2:]
    parts = refs[:nparts]
    refs = refs[nparts:]
    z, zlow, q_o, k_o, v_o, o_o, p_o, w_s, q_s, k_s, v_s, o_s, p_s, w_sem, out_sem = refs
    me = me_ref[0]

    loads = [attn_loads(me, parts, w_s, (u,), w_sem.at[u]) for u in range(4)]
    for load in loads:
        start_all(load)
    a = rms(src[...].astype(f32), gain[...]).astype(bf16)
    b = a if ksrc is None else ksrc[...]
    outs = []
    for value, weight, out, scr in ((a, 0, q_o, q_s), (b, 1, k_o, k_s), (b, 2, v_o, v_s)):
        wait_all(loads[weight])
        full = dot(value, matrix(w_s, weight)).astype(bf16)
        for p in range(PAIRS):
            scr[p] = full[:, p * TILE : (p + 1) * TILE]
        outs.append(pltpu.make_async_copy(scr, out, out_sem.at[weight]))
        outs[-1].start()

    def prob_copy(p):
        return pltpu.make_async_copy(p_s.at[pl.ds(2 * p, 2)], p_o.at[pl.ds(2 * p, 2)], out_sem.at[4])

    def pair(p, carry):
        qp, kp, vp = q_s[p], k_s[p], v_s[p]
        total = [None] * BLOCKS
        for which in range(2):
            h = 2 * p + which
            kz, vz = half_lanes(kp, which), half_lanes(vp, which)
            for bi in range(BLOCKS):
                rows = slice(bi * TILE, (bi + 1) * TILE)
                s = dot_nt(qp[rows], kz)
                if has_bias:
                    tiles = []
                    for bj in range(BLOCKS):
                        step = bi - bj
                        part = s[:, bj * TILE : (bj + 1) * TILE]
                        if abs(step) < 2:
                            part = part + bias[h, tile_of(step)]
                        else:
                            part = part + far[h, 0 if step > 0 else 1]
                        tiles.append(part)
                    s = jnp.concatenate(tiles, axis=1)
                s = jnp.where(segc[rows] == segr[...], s, MASKED)
                e = jnp.exp(s - jnp.max(s, axis=-1, keepdims=True))
                prob = (e * (1.0 / jnp.sum(e, axis=-1, keepdims=True))).astype(bf16)
                p_s[h, rows, :] = prob
                o = dot(prob, vz)
                total[bi] = o if total[bi] is None else total[bi] + o
        o_s[p] = jnp.concatenate(total, axis=0).astype(bf16)
        prob_copy(p).start()
        return carry

    lax.fori_loop(0, PAIRS, pair, 0)
    outs.append(pltpu.make_async_copy(o_s, o_o, out_sem.at[3]))
    outs[-1].start()
    mixed = jnp.concatenate([o_s[p] for p in range(PAIRS)], axis=1)
    wait_all(loads[3])
    result = src[...].astype(f32) + dot(mixed, matrix(w_s, 3))
    z[...] = result
    zlow[...] = result.astype(bf16)
    wait_all(outs)
    for p in range(PAIRS):
        prob_copy(p).wait()


VM = pl.BlockSpec(memory_space=pltpu.VMEM)
SM = pl.BlockSpec(memory_space=pltpu.SMEM)
HBM = pl.BlockSpec(memory_space=pl.ANY)
HEAD_ROWS = jax.ShapeDtypeStruct((PAIRS, LEN, TILE), bf16)
LOW_ROWS = jax.ShapeDtypeStruct((LEN, D), bf16)
FULL_ROWS = jax.ShapeDtypeStruct((LEN, D), f32)
ONE_ROW = jax.ShapeDtypeStruct((1, D), f32)
PARAMS = pltpu.CompilerParams(vmem_limit_bytes=VMEM_LIMIT)


def attn_fwd(me, src, gain, parts, segr, segc, ksrc=None, bias=None, far=None):
    has_bias = bias is not None
    args = [me, src, gain] + ([] if has_bias else [ksrc]) + [segr, segc]
    specs = [SM] + [VM] * (len(args) - 1)
    if has_bias:
        args += [bias, far]
        specs += [VM, SM]
    args += parts
    specs += [HBM] * len(parts)
    return pl.pallas_call(
        only(
            None if has_bias else 0,
            functools.partial(attn_fwd_kernel, has_bias, len(parts)),
        ),
        out_shape=(FULL_ROWS, LOW_ROWS)
        + (HEAD_ROWS,) * 4
        + (jax.ShapeDtypeStruct((HEADS, LEN, LEN), bf16),),
        in_specs=specs,
        out_specs=(VM,) * 2 + (HBM,) * 5,
        scratch_shapes=[pltpu.VMEM((4, 8, ROWS8, D), bf16)]
        + [pltpu.VMEM((PAIRS, LEN, TILE), bf16)] * 4
        + [pltpu.VMEM((HEADS, LEN, LEN), bf16)]
        + [pltpu.SemaphoreType.DMA((4,)), pltpu.SemaphoreType.DMA((5,))],
        compiler_params=PARAMS,
        name="self_fwd" if has_bias else "cross_fwd",
    )(*args)


def attn_bwd_kernel(has_bias, nparts, *refs):
    refs = list(refs)
    me_ref, gres, src, gain = refs[:4]
    refs = refs[4:]
    gother = ksrc = None
    if has_bias:
        gother, gains, hot = refs[:3]
        refs = refs[3:]
    else:
        ksrc = refs.pop(0)
    q_i, k_i, v_i, o_i, p_i = refs[:5]
    refs = refs[5:]
    parts = refs[:nparts]
    refs = refs[nparts:]
    din, keep, send = refs[:3]
    refs = refs[3:]
    if has_bias:
        vec_s = refs.pop()
    else:
        dgain, dkey = refs[:2]
        refs = refs[2:]
    w_s, p_s, do_s, dq_s, dk_s, dv_s, ds_s, keep_s, send_s, w_sem, p_sem, out_sem = refs
    me = me_ref[0]

    out_load = attn_loads(me, parts, w_s, (3,), w_sem.at[0])
    rest_load = attn_loads(me, parts, w_s, (0, 1, 2), w_sem.at[1])

    def prob_copy(p):
        return pltpu.make_async_copy(p_i.at[pl.ds(2 * p, 2)], p_s.at[pl.ds(2 * p, 2)], p_sem.at[p])

    start_all(out_load)
    for p in range(PAIRS):
        prob_copy(p).start()
    start_all(rest_load)
    base = gres[...].astype(f32)
    if has_bias:
        base = jnp.where(me_ref[1] == 1, gother[...].astype(f32), base)
    g = base.astype(bf16)
    wait_all(out_load)
    do = dot_nt(g, matrix(w_s, 3)).astype(bf16)
    for p in range(PAIRS):
        do_s[p] = do[:, p * TILE : (p + 1) * TILE]

    if has_bias:
        down = lax.broadcasted_iota(jnp.int32, (TILE, TILE), 0)
        along = lax.broadcasted_iota(jnp.int32, (TILE, TILE), 1)
        mirror = (down + along == TILE - 1).astype(bf16)

    def pair(p, carry):
        qp, kp, vp, dop = q_i[p], k_i[p], v_i[p], do_s[p]
        q_t, do_t = qp.T, dop.T
        total = [None] * BLOCKS
        prob_copy(p).wait()
        for which in range(2):
            h = 2 * p + which
            kz, vz = half_lanes(kp, which), half_lanes(vp, which)
            diag = {0: None, 1: None, -1: None, 2: None, -2: None}
            for bi in range(BLOCKS):
                rows = slice(bi * TILE, (bi + 1) * TILE)
                dp = dot_nt(dop[rows], vz)
                prob = p_s[h, rows, :].astype(f32)
                t = prob * dp
                ds = t - prob * jnp.sum(t, axis=-1, keepdims=True)
                if has_bias:
                    for bj in range(BLOCKS):
                        step = max(-2, min(2, bi - bj))
                        part = ds[:, bj * TILE : (bj + 1) * TILE]
                        diag[step] = part if diag[step] is None else diag[step] + part
                low = ds.astype(bf16)
                ds_s[which, rows, :] = low
                dq = dot(low, kz)
                total[bi] = dq if total[bi] is None else total[bi] + dq
            if has_bias:
                near = jnp.concatenate([diag[step] for step in (0, 1, -1)], axis=1)
                near = dot(mirror, near.astype(bf16))
                nothing = jnp.zeros((TILE, TILE), f32)
                for t in range(3):
                    part = near[:, t * TILE : (t + 1) * TILE]
                    part = pltpu.roll(
                        jnp.concatenate([part, nothing], axis=1), 0, 1, stride=1, stride_axis=0
                    )
                    vec_s[h, :, 2 * t * TILE : 2 * (t + 1) * TILE] = jnp.sum(
                        part, axis=0, keepdims=True
                    )
                for n, step in ((6, 2), (7, -2)):
                    vec_s[h, :, n * TILE : (n + 1) * TILE] = jnp.sum(
                        diag[step], axis=0, keepdims=True
                    )
            half = slice(which * HEAD, (which + 1) * HEAD)
            dk_s[p, half, :] = dot(q_t[half], ds_s[which]).astype(bf16)
            dv_s[p, half, :] = dot(do_t[half], p_s[h]).astype(bf16)
        dq_s[p] = jnp.concatenate(total, axis=0).astype(bf16)
        return carry

    lax.fori_loop(0, PAIRS, pair, 0)
    v = src[...].astype(f32)
    a = rms(v, gain[...]).astype(bf16)
    a_t = a.T
    b_t = a_t if ksrc is None else ksrc[...].T
    dq = jnp.concatenate([dq_s[p] for p in range(PAIRS)], axis=1)
    dk_t = dk_s[...].reshape(D, LEN)
    dv_t = dv_s[...].reshape(D, LEN)
    wait_all(rest_load)
    query_side = dot_nt(dq, matrix(w_s, 0))
    key_side = dot_nt(dk_t.T, matrix(w_s, 1)) + dot_nt(dv_t.T, matrix(w_s, 2))
    if has_bias:
        query_side = query_side + key_side
    else:
        dkey[...] = key_side.astype(bf16)
    dv, dg = rms_back(v, gain[...], query_side)
    din[...] = (base + dv).astype(din.dtype)
    if has_bias:
        table = dot(vec_s[...].reshape(HEADS, 8 * TILE).astype(bf16), hot[...])
        table = jnp.concatenate([table, jnp.zeros((HEADS, D - TILE), f32)], axis=1)
        rows = jnp.concatenate([table, dg, gains[...], jnp.zeros((1, D), f32)], axis=0)
        for slot in range(4):
            keep_s[slot, D // 2 :, :] = rows.astype(bf16)
            send_s[slot, D // 2 :, :] = rows.astype(bf16)
    else:
        dgain[...] = dg
    put_blocks(me, dot(a_t, dq), 0, keep_s, send_s)
    put_blocks(me, dot_nt(b_t, dk_t), 1, keep_s, send_s)
    put_blocks(me, dot_nt(b_t, dv_t), 2, keep_s, send_s)
    mixed = jnp.concatenate([o_i[p] for p in range(PAIRS)], axis=1)
    put_blocks(me, dot(mixed.T, g), 3, keep_s, send_s)
    outs = [
        pltpu.make_async_copy(send_s, send, out_sem.at[0]),
        pltpu.make_async_copy(keep_s, keep, out_sem.at[1]),
    ]
    start_all(outs)
    wait_all(outs)


BLOCKS8 = jax.ShapeDtypeStruct((4, D, D), bf16)


def attn_bwd(me, gres, src, gain, parts, saved, ksrc=None, others=()):
    has_bias = ksrc is None
    args = [me, gres, src, gain] + (list(others) if has_bias else [ksrc]) + [*saved, *parts]
    specs = [SM] + [VM] * (len(args) - 2 - len(parts)) + [HBM] * (1 + len(parts))
    rows = D // 2 + (EXTRA if has_bias else 0)
    pack = jax.ShapeDtypeStruct((4, rows, D), bf16)
    outs = [LOW_ROWS, pack, pack] if has_bias else [FULL_ROWS, pack, pack, ONE_ROW, LOW_ROWS]
    return pl.pallas_call(
        only(
            None if has_bias else 0,
            functools.partial(attn_bwd_kernel, has_bias, len(parts)),
        ),
        out_shape=tuple(outs),
        in_specs=specs,
        out_specs=tuple([VM, HBM, HBM] + [VM] * (len(outs) - 3)),
        scratch_shapes=[
            pltpu.VMEM((4, 8, ROWS8, D), bf16),
            pltpu.VMEM((HEADS, LEN, LEN), bf16),
            pltpu.VMEM((PAIRS, LEN, TILE), bf16),
            pltpu.VMEM((PAIRS, LEN, TILE), bf16),
            pltpu.VMEM((PAIRS, TILE, LEN), bf16),
            pltpu.VMEM((PAIRS, TILE, LEN), bf16),
            pltpu.VMEM((2, LEN, LEN), bf16),
            pltpu.VMEM((4, rows, D), bf16),
            pltpu.VMEM((4, rows, D), bf16),
            pltpu.SemaphoreType.DMA((2,)),
            pltpu.SemaphoreType.DMA((PAIRS,)),
            pltpu.SemaphoreType.DMA((2,)),
        ]
        + ([pltpu.VMEM((HEADS, 1, 8 * TILE), f32)] if has_bias else []),
        compiler_params=PARAMS,
        name="self_bwd" if has_bias else "cross_bwd",
    )(*args)


GELU_C = float(np.sqrt(2.0 / np.pi))


def gelu_parts(u):
    square = u * u
    t = jnp.tanh(GELU_C * (u + 0.044715 * (u * square)))
    half = 0.5 + 0.5 * t
    slope = half + (half * (1.0 - t)) * (u * (GELU_C + (3 * 0.044715 * GELU_C) * square))
    return u * half, slope


def ffn_kernel(mode, nparts, *refs):
    fwd, bwd = mode != "bwd", mode != "fwd"
    refs = list(refs)
    me_ref, x, gain = refs[:3]
    refs = refs[3:]
    g = refs.pop(0) if bwd else None
    if mode == "bwd":
        h_i, slope_i = refs[:2]
        refs = refs[2:]
    parts = refs[:nparts]
    refs = refs[nparts:]
    out = refs.pop(0) if fwd else None
    if mode == "fwd":
        h_o, slope_o = refs[:2]
        refs = refs[2:]
    if bwd:
        dx, dgain, keep, send = refs[:4]
        refs = refs[4:]
    wi_s, wo_s, w_sem = refs[:3]
    refs = refs[3:]
    if fwd:
        n_s, acc = refs[:2]
        refs = refs[2:]
    if bwd:
        nt_s, dn, keep_s, send_s, out_sem = refs
    me = me_ref[0]
    step = pl.program_id(0)
    plan = part_plan(nparts, 8)

    def in_loads(unit):
        copies = []
        for part, (flip, first, count) in zip(parts, plan):
            if first == 0:
                to = wi_s.at[unit] if flip is None else wi_s.at[unit, me ^ flip]
                copies.append(pltpu.make_async_copy(part.at[unit], to, w_sem.at[unit]))
        return copies

    def out_loads():
        copies = []
        for part, (flip, first, count) in zip(parts, plan):
            if first + count == 8:
                if flip is None:
                    for k in range(4):
                        copies.append(
                            pltpu.make_async_copy(part.at[4 + k], wo_s.at[:, k], w_sem.at[4])
                        )
                else:
                    copies.append(
                        pltpu.make_async_copy(
                            part.at[pl.ds(4 - first, 4)], wo_s.at[me ^ flip], w_sem.at[4]
                        )
                    )
        return copies

    @pl.when(step == 0)
    def _():
        start_all(in_loads(0))
        start_all(out_loads())
        for unit in range(1, 4):
            start_all(in_loads(unit))
        v = x[...].astype(f32)
        n = rms(v, gain[...]).astype(bf16)
        if fwd:
            n_s[...] = n
            acc[...] = v
        if bwd:
            nt_s[...] = n.T
            dn[...] = jnp.zeros_like(dn)

    for unit in range(4):

        @pl.when(step == unit)
        def _():
            wait_all(in_loads(unit))

    wi = wi_s[step].reshape(D, D)
    if fwd:
        h, slope = gelu_parts(dot(n_s[...], wi))
        h = h.astype(bf16)
        if mode == "fwd":
            h_o[0] = h
            slope_o[0] = slope.astype(bf16)
    else:
        h, slope = h_i[0], slope_i[0].astype(f32)

    @pl.when(step == 0)
    def _():
        wait_all(out_loads())

    wo = wo_s[pl.ds(2 * step, 2)].reshape(D, D)
    if fwd:
        acc[...] += dot(h, wo)
    if bwd:
        du = (slope * dot_nt(g[...], wo)).astype(bf16)
        dn[...] += dot_nt(du, wi)
        in_rows = pl.ds(pl.multiple_of(step * ROWS8, 32), ROWS8)
        put_blocks(me, dot(nt_s[...], du), in_rows, keep_s, send_s)
        dwo = dot(h.T, g[...]).astype(bf16)
        odd = (me % 2) == 1
        slot = step ^ (me // 2)
        for k in range(4):
            first, second = dwo[k * ROWS8 : (k + 1) * ROWS8], dwo[(4 + k) * ROWS8 : (5 + k) * ROWS8]
            rows = slice((4 + k) * ROWS8, (5 + k) * ROWS8)
            keep_s[slot, rows, :] = jnp.where(odd, second, first)
            send_s[slot, rows, :] = jnp.where(odd, first, second)

        def outs(c):
            slot = c ^ (me // 2)
            copies = []
            for n, (here, there) in enumerate(((send_s, send), (keep_s, keep))):
                part = pl.ds(pl.multiple_of(c * ROWS8, 32), ROWS8)
                copies.append(
                    pltpu.make_async_copy(here.at[:, part], there.at[:, part], out_sem.at[2 * n])
                )
                last = pl.ds(D // 2, D // 2)
                copies.append(
                    pltpu.make_async_copy(here.at[slot, last], there.at[slot, last], out_sem.at[2 * n + 1])
                )
            return copies

        start_all(outs(step))

    @pl.when(step == pl.num_programs(0) - 1)
    def _():
        if fwd:
            out[...] = acc[...].astype(bf16)
        if bwd:
            dv, dg = rms_back(x[...].astype(f32), gain[...], dn[...])
            dgain[...] = dg
            dx[...] = (g[...].astype(f32) + dv).astype(bf16)
            for c in range(4):
                wait_all(outs(c))


def ffn(mode, me, x, gain, parts, g=None, saved=()):
    fwd, bwd = mode != "bwd", mode != "fwd"
    whole = pl.BlockSpec((LEN, D), lambda c: (0, 0))
    one = pl.BlockSpec((1, D), lambda c: (0, 0))
    hidden = pl.BlockSpec((1, LEN, D), lambda c: (c, 0, 0))
    hidden_shape = jax.ShapeDtypeStruct((4, LEN, D), bf16)
    args, specs = [me, x, gain], [SM, whole, one]
    if bwd:
        args, specs = args + [g], specs + [whole]
    args += list(saved)
    specs += [hidden] * len(saved)
    args += parts
    specs += [HBM] * len(parts)
    shapes, out_specs = [], []
    scratch = [
        pltpu.VMEM((4, 8, ROWS8, D), bf16),
        pltpu.VMEM((8, 4, ROWS8, D), bf16),
        pltpu.SemaphoreType.DMA((5,)),
    ]
    if fwd:
        shapes, out_specs = [LOW_ROWS], [whole]
        scratch += [pltpu.VMEM((LEN, D), bf16), pltpu.VMEM((LEN, D), f32)]
    if mode == "fwd":
        shapes += [hidden_shape] * 2
        out_specs += [hidden] * 2
    if bwd:
        shapes += [LOW_ROWS, ONE_ROW, BLOCKS8, BLOCKS8]
        out_specs += [whole, one, HBM, HBM]
        scratch += [
            pltpu.VMEM((D, LEN), bf16),
            pltpu.VMEM((LEN, D), f32),
            pltpu.VMEM((4, D, D), bf16),
            pltpu.VMEM((4, D, D), bf16),
            pltpu.SemaphoreType.DMA((4,)),
        ]
    return pl.pallas_call(
        only(0 if mode == "both" else 1, functools.partial(ffn_kernel, mode, len(parts))),
        grid=(4,),
        out_shape=tuple(shapes),
        in_specs=specs,
        out_specs=tuple(out_specs),
        scratch_shapes=scratch,
        compiler_params=PARAMS,
        name="ffn_" + mode,
    )(*args)


def wide_add(*values):
    total = values[0].astype(f32)
    for value in values[1:]:
        total = total + value.astype(f32)
    return total.astype(bf16)


def diag_kernel(me_ref, keep, recv, by_x, by_y, keep_s, recv_s, sem):
    half = by_x.shape[0]
    loads = [
        pltpu.make_async_copy(keep.at[3], keep_s, sem.at[0]),
        pltpu.make_async_copy(recv.at[3], recv_s, sem.at[1]),
    ]
    start_all(loads)
    wait_all(loads)
    keep_s[...] = wide_add(keep_s[...], recv_s[...])
    stores = [
        pltpu.make_async_copy(keep_s.at[:half], by_x, sem.at[0]),
        pltpu.make_async_copy(keep_s.at[half:], by_y, sem.at[1]),
    ]
    start_all(stores)
    wait_all(stores)


def diag_add(role, me, keep, recv):
    _, r, c = keep.shape
    half = r // 32 * 16
    return pl.pallas_call(
        only(role, diag_kernel),
        out_shape=tuple(jax.ShapeDtypeStruct((n, c), bf16) for n in (half, r - half)),
        in_specs=[SM, HBM, HBM],
        out_specs=(HBM, HBM),
        scratch_shapes=[pltpu.VMEM((r, c), bf16)] * 2 + [pltpu.SemaphoreType.DMA((2,))],
        compiler_params=PARAMS,
        name="diag_add",
    )(me, keep, recv)


def rest_kernel(
    me_ref, keep, recv, from_x, from_y, own, for_x, for_y, keep_s, recv_s, x_s, y_s, sem
):
    half = from_x.shape[0]
    loads = []
    for slot in range(3):
        loads.append(pltpu.make_async_copy(keep.at[slot], keep_s.at[slot], sem.at[2 * slot]))
        loads.append(pltpu.make_async_copy(recv.at[slot], recv_s.at[slot], sem.at[2 * slot + 1]))
    loads.append(pltpu.make_async_copy(from_x, x_s, sem.at[6]))
    loads.append(pltpu.make_async_copy(from_y, y_s, sem.at[7]))
    start_all(loads[2:4] + loads[6:] + loads[4:6] + loads[:2])
    stores = []
    for slot, out in ((1, for_x), (2, for_y), (0, own)):
        wait_all(loads[2 * slot : 2 * slot + 2])
        if slot == 1:
            wait_all(loads[6:])
            top, low = (), (y_s[...],)
        else:
            top, low = ((x_s[...],), ()) if slot == 2 else ((), ())
        keep_s[slot, :half] = wide_add(keep_s[slot, :half], recv_s[slot, :half], *top)
        keep_s[slot, half:] = wide_add(keep_s[slot, half:], recv_s[slot, half:], *low)
        stores.append(pltpu.make_async_copy(keep_s.at[slot], out, sem.at[8 + slot]))
        stores[-1].start()
    wait_all(stores)


def rest_add(role, me, keep, recv, from_x, from_y):
    _, r, c = keep.shape
    half = r // 32 * 16
    shape = jax.ShapeDtypeStruct((r, c), bf16)
    return pl.pallas_call(
        only(role, rest_kernel),
        out_shape=(shape,) * 3,
        in_specs=[SM] + [HBM] * 4,
        out_specs=(HBM,) * 3,
        scratch_shapes=[pltpu.VMEM((3, r, c), bf16)] * 2
        + [pltpu.VMEM((half, c), bf16), pltpu.VMEM((r - half, c), bf16)]
        + [pltpu.SemaphoreType.DMA((11,))],
        compiler_params=PARAMS,
        name="rest_add",
    )(me, keep, recv, from_x, from_y)


ALL = (0, 1, 2, 3)
ENC = (1, 2)
DEC = (0, 3)


def across(x, flip, planes):
    wide, narrow = lax.axis_size("wide"), lax.axis_size("narrow")
    pairs = [(i * narrow + n, (i ^ flip) * narrow + n) for i in range(wide) for n in planes]
    return lax.ppermute(x, ("wide", "narrow"), pairs)


def between(x, pairs):
    return lax.ppermute(x, "narrow", pairs)


def in_units(local):
    return jnp.transpose(local.reshape(local.shape[0], 4, D), (1, 0, 2))


def out_units(local):
    return local.reshape(4, local.shape[0] // 4, D)


def tie(*values):
    return lax.optimization_barrier(values)


def whole_pack(shard):
    k = shard.shape[0]
    full = lax.all_gather(shard, "wide", axis=1)
    if k == 8:
        inner = full[:4].reshape(4, 8, ROWS8, D)
        outer = jnp.transpose(full[4:], (1, 0, 2, 3)).reshape(8, 4, ROWS8, D)
        return [jnp.concatenate([inner, jnp.transpose(outer, (1, 0, 2, 3))])]
    return [full.reshape(k, 8, ROWS8, D)]


def gather_near(shard, planes=ALL):
    return across(shard, 2, planes), across(shard, 4, planes), across(shard, 1, planes)


def gather_far(shard, near, planes=ALL):
    px, py, pc = near
    k = shard.shape[0]
    first = across(px[: k // 2], 4, planes)
    second = across(py[k // 2 :], 2, planes)
    parts = [px, py, first, second]
    return [shard] + parts + [pc] + [across(part, 1, planes) for part in parts]


def whole_scatter(keep, send):
    blocks = jnp.stack([keep, send], axis=1).reshape(8, -1, D)
    k = blocks.shape[1] // ROWS8
    weights = blocks[:, : k * ROWS8].reshape(8, k, ROWS8, D)
    inner = jnp.transpose(weights[:, :4], (1, 0, 2, 3)).reshape(4, D, D)
    inner = lax.psum_scatter(inner, "wide", scatter_dimension=1, tiled=True).reshape(-1, D)
    if k == 8:
        last = weights[:, 4:].reshape(FF, D)
        last = lax.psum_scatter(last, "wide", scatter_dimension=0, tiled=True)
    else:
        last = lax.psum(blocks[0, k * ROWS8 :], "wide")
    return jnp.concatenate([inner, last])


class Scatter:
    def __init__(self, me, keep, send, planes):
        self.me, self.keep, self.planes = me, keep, planes
        self.role = {ENC: 1, DEC: 0, ALL: None}[planes]
        self.small = lax.axis_size("wide") == 8
        self.state = (send,)
        if self.small:
            self.state = (across(send, 1, planes),)
        self.phase, self.token = 0, keep

    def go(self):
        if not self.small:
            return self
        if self.phase == 0:
            (self.recv,) = self.state
            by_x, by_y = diag_add(self.role, self.me, self.keep, self.recv)
            self.token = by_x
            self.state = across(by_x, 2, self.planes), across(by_y, 4, self.planes)
        elif self.phase == 1:
            own, for_x, for_y = rest_add(self.role, self.me, self.keep, self.recv, *self.state)
            self.token = own
            self.state = own, across(for_x, 2, self.planes), across(for_y, 4, self.planes)
        self.phase += 1
        return self

    def result(self):
        if not self.small:
            return whole_scatter(self.keep, self.state[0])
        return wide_add(*self.state)


def tie_all(scatters, *values):
    counts = [len(s.state) for s in scatters]
    flat = tie(*[v for s in scatters for v in s.state], *values)
    for s, count in zip(scatters, counts):
        s.state, flat = flat[:count], flat[count:]
    return flat


class FromMiddle:
    def __init__(self, share, middle):
        self.share, self.middle = share, middle
        self.state = (between(share, [(1, 2), (2, 1)]),)

    def go(self):
        self.total = wide_add(self.share, *self.state)
        self.state = (between(self.total, [(1, 0), (2, 3)]),)
        return self

    def result(self):
        return jnp.where(self.middle, self.total, *self.state).astype(f32)


class FromEnds:
    def __init__(self, share, middle):
        self.share, self.middle = share, middle
        self.got, self.state = [], (between(share, [(0, 1), (3, 2)]),)

    def go(self):
        self.got.append(self.state[0])
        pairs = [(1, 2), (2, 1)] if len(self.got) == 1 else [(1, 0), (2, 3)]
        self.state = (between(self.state[0], pairs),)
        return self

    def result(self):
        near, far = self.got
        first = jnp.where(self.middle, near, self.share).astype(f32)
        return first + jnp.where(self.middle, far, *self.state).astype(f32)


def on_device(
    enc_in,
    dec_in,
    dec_cot,
    segments,
    enc_attn_gain,
    enc_query,
    enc_key,
    enc_value,
    enc_output,
    enc_table,
    enc_ffn_gain,
    enc_ffn_in,
    enc_ffn_out,
    dec_self_gain,
    dec_query,
    dec_key,
    dec_value,
    dec_output,
    dec_table,
    dec_cross_gain,
    cross_query,
    cross_key,
    cross_value,
    cross_output,
    dec_ffn_gain,
    dec_ffn_in,
    dec_ffn_out,
):
    plane = lax.axis_index("narrow")
    is_enc = (plane == 1) | (plane == 2)
    row = plane // 2

    def own(x):
        return lax.dynamic_slice_in_dim(x, row * LEN, LEN, 0)

    def pick(enc, dec):
        return jnp.where(is_enc, enc, dec)

    def gain_of(g):
        return g.astype(f32).reshape(1, D)

    seg = lax.dynamic_slice_in_dim(segments, row, 1, 0)
    segr, segc = seg, seg.reshape(LEN, 1)
    src = pick(own(enc_in), own(dec_in))
    cot = own(dec_cot)

    me = lax.axis_index("wide") if lax.axis_size("wide") == 8 else 0
    me = jnp.stack([jnp.asarray(me, jnp.int32), is_enc.astype(jnp.int32)])

    pack_a = jnp.stack(
        [
            pick(enc_query, dec_query),
            pick(enc_key, dec_key),
            pick(enc_value, dec_value),
            pick(enc_output, dec_output),
        ]
    )
    pack_f = jnp.concatenate(
        [in_units(pick(enc_ffn_in, dec_ffn_in)), out_units(pick(enc_ffn_out, dec_ffn_out))]
    )
    pack_c = jnp.stack([cross_query, cross_key, cross_value, cross_output])
    shard_rows = enc_query.shape[0]
    small = lax.axis_size("wide") == 8
    if small:
        near_a = gather_near(pack_a)

    enc_ids, enc_far = tile_ids(True)
    dec_ids, dec_far = tile_ids(False)
    ids = pick(jnp.asarray(enc_ids), jnp.asarray(dec_ids))
    far_ids = pick(jnp.asarray(enc_far), jnp.asarray(dec_far))
    buckets = jnp.arange(BUCKETS + 1, dtype=jnp.int32)
    hot = (ids[None] == buckets[:, None, None, None]).astype(bf16)
    far_hot = (far_ids[None] == buckets[:, None]).astype(bf16)
    table = jnp.concatenate([pick(enc_table, dec_table), jnp.full((1, HEADS), MASKED, bf16)])
    bias = jnp.einsum("bh,bsij->hsij", table, hot, preferred_element_type=f32)
    far = jnp.einsum("bh,bs->hs", table, far_hot, preferred_element_type=f32)
    enc_sums, dec_sums = sum_ids(True), sum_ids(False)
    sums_of = pick(jnp.asarray(enc_sums), jnp.asarray(dec_sums))
    sum_hot = (sums_of[:, None] == jnp.arange(TILE, dtype=jnp.int32)).astype(bf16)

    gain_a = pick(gain_of(enc_attn_gain), gain_of(dec_self_gain))
    enc_gain = gain_of(enc_ffn_gain)
    gain_c = gain_of(dec_cross_gain)
    if small:
        *near_a, pack_f, bias, far, src, cot, segc, me = tie(
            *near_a, pack_f, bias, far, src, cot, segc, me
        )
        w_attn = gather_far(pack_a, near_a)
        near_f = gather_near(pack_f)
    else:
        w_attn, w_ffn, w_cross = whole_pack(pack_a), whole_pack(pack_f), whole_pack(pack_c)
    z1, x1, *saved = attn_fwd(me, src, gain_a, w_attn, segr, segc, bias=bias, far=far)
    if small:
        z1, x1, *near_f, pack_c = tie(z1, x1, *near_f, pack_c)
        w_ffn = gather_far(pack_f, near_f)
        near_c = gather_near(pack_c, DEC)
    enc_out, *saved_f = ffn("fwd", me, x1, enc_gain, w_ffn)
    if small:
        enc_out, *near_c = tie(enc_out, *near_c)
    memory = between(enc_out, [(1, 0), (2, 3)])
    if small:
        w_cross = gather_far(pack_c, near_c, DEC)
    _, z2, *saved_c = attn_fwd(me, z1, gain_c, w_cross, segr, segc, ksrc=memory)

    def by_columns(x):
        return lax.all_to_all(x, "narrow", split_axis=1, concat_axis=0, tiled=True)

    def rows_by_block(parts):
        rows = [parts[n * LEN : (n + 1) * LEN] for n in range(4)]
        return jnp.concatenate([rows[1], rows[2]]), jnp.concatenate([rows[0], rows[3]])

    dec_out, gz2, dgain_df, *blocks = ffn("both", me, z2, gain_of(dec_ffn_gain), w_ffn, cot)
    sum_df = Scatter(me, *blocks, DEC)
    out_cols = by_columns(pick(enc_out, dec_out))
    gz1, *blocks, dgain_c, genc_out = attn_bwd(
        me, gz2, z1, gain_c, w_cross, saved_c, ksrc=memory
    )
    genc_out, gz1, out_cols, *blocks = tie_all([sum_df], genc_out, gz1, out_cols, *blocks)
    genc = between(genc_out, [(0, 1), (3, 2)])
    sum_c = Scatter(me, *blocks, DEC)
    sum_df.go()
    (gz1,) = tie_all([sum_df, sum_c], gz1)
    sum_df.go()
    sum_c.go()
    gx1, dgain_ef, *blocks = ffn("bwd", me, x1, enc_gain, w_ffn, genc, saved_f)
    gx1, *blocks = tie_all([sum_c], gx1, *blocks)
    sum_ef = Scatter(me, *blocks, ENC)
    gains = jnp.concatenate([pick(dgain_ef, dgain_df), dgain_c])
    din, *blocks = attn_bwd(
        me, gz1, src, gain_a, w_attn, saved, others=(gx1, gains, sum_hot)
    )
    din, *blocks = tie_all([sum_ef, sum_c, sum_df], din, *blocks)
    sum_a = Scatter(me, *blocks, ALL)
    sum_ef.go()
    tie_all([sum_df, sum_c], sum_ef.token)
    all_df = FromEnds(sum_df.result(), is_enc)
    tie_all([sum_c], all_df.share)
    sum_c.go()
    tie_all([sum_ef, sum_a], all_df.share)
    sum_ef.go()
    tie_all([sum_a], sum_ef.token)
    sum_a.go()
    tie_all([sum_c], sum_a.token)
    all_c = FromEnds(sum_c.result(), is_enc)
    tie_all([all_df], all_c.share)
    all_df.go()
    din, _ = tie(din, sum_a.token)
    grad_cols = by_columns(din)
    tie_all([sum_a, all_c])
    sum_a.go()
    all_c.go()
    tie_all([sum_ef, all_df], sum_a.token)
    all_ef = FromMiddle(sum_ef.result(), is_enc)
    all_df.go()
    tie_all([sum_a, all_c], all_ef.share)
    s_a = sum_a.result()
    all_e = FromMiddle(s_a, is_enc)
    all_s = FromEnds(s_a, is_enc)
    all_c.go()
    tie_all([all_ef], s_a)
    all_ef.go()
    tie_all([all_e, all_s], all_ef.total)
    all_e.go()
    all_s.go()
    tie_all([all_s], all_e.total)
    all_s.go()

    def split(f):
        return f[: 4 * shard_rows].reshape(4, shard_rows, D), f[4 * shard_rows :]

    g_df, g_c, g_s, g_ef, g_e = (
        split(p.result()) for p in (all_df, all_c, all_s, all_ef, all_e)
    )
    gi_e, gi_d = (jnp.transpose(g[0], (1, 0, 2)).reshape(-1, FF) for g in (g_ef, g_df))
    go_e, go_d = g_ef[1], g_df[1]
    more_e, more_s = g_e[1], g_s[1]
    g_e, g_s, g_c = g_e[0], g_s[0], g_c[0]
    tables = [jnp.transpose(m[:HEADS, :BUCKETS]) for m in (more_e, more_s)]
    sums = [more_e[HEADS], more_e[HEADS + 1], more_s[HEADS], more_s[HEADS + 2], more_s[HEADS + 1]]
    enc_cols, dec_cols = rows_by_block(out_cols)
    enc_grad_cols, dec_grad_cols = rows_by_block(grad_cols)
    return (
        enc_cols,
        dec_cols,
        enc_grad_cols,
        dec_grad_cols,
        sums[0],
        g_e[0],
        g_e[1],
        g_e[2],
        g_e[3],
        tables[0],
        sums[1],
        gi_e,
        go_e,
        sums[2],
        g_s[0],
        g_s[1],
        g_s[2],
        g_s[3],
        tables[1],
        sums[3],
        g_c[0],
        g_c[1],
        g_c[2],
        g_c[3],
        sums[4],
        gi_d,
        go_d,
    )


def solution(mesh):
    rows, copied = P("wide", None), P()
    block = P("wide", "narrow")
    gains = (copied,)
    attention = (rows,) * 4
    placed = (
        (rows,) * 4
        + gains
        + attention
        + (copied,)
        + gains
        + (rows,) * 2
        + gains
        + attention
        + (copied,)
        + gains
        + attention
        + gains
        + (rows,) * 2
    )
    return jax.shard_map(
        on_device,
        mesh=mesh,
        in_specs=placed,
        out_specs=(block,) * 4 + placed[4:],
        check_vma=False,
    )
```

```python
import functools

import jax
import jax.numpy as jnp
import numpy as np
from jax import lax
from jax.experimental import pallas as pl
from jax.experimental.pallas import tpu as pltpu
from jax.sharding import PartitionSpec as P

D = 768
HEADS = 12
HEAD = 64
PAIRS = HEADS // 2
FF = 3072
BUCKETS = 32
MAXDIST = 128
LEN = 512
TILE = 128
BLOCKS = LEN // TILE
ROWS8 = D // 8
EXTRA = 16

EPSILON = 1e-06
MASKED = -1000000000.0
VMEM_LIMIT = 60 * 1024 * 1024
f32 = jnp.float32
bf16 = jnp.bfloat16


def bucket_of(reverse, both_ways):
    result = np.zeros(reverse.shape, np.int64)
    if both_ways:
        half_count = BUCKETS // 2
        result = result + (reverse < 0) * half_count
        reverse = np.abs(reverse)
    else:
        half_count = BUCKETS
        reverse = np.maximum(reverse, 0)
    exact_count = half_count // 2
    scaled = (
        np.log(np.maximum(reverse, 1) / exact_count)
        / np.log(MAXDIST / exact_count)
        * (half_count - exact_count)
    )
    far_bucket = np.minimum(
        exact_count + np.floor(np.maximum(scaled, 0.0)).astype(np.int64), half_count - 1
    )
    return result + np.where(reverse < exact_count, reverse, far_bucket)


def tile_ids(both_ways):
    i = np.arange(TILE)[:, None]
    j = np.arange(TILE)[None, :]
    tiles = []
    for step in (0, 1, -1):
        n = i - j + step * TILE
        ids = bucket_of(n, both_ways)
        tiles.append(ids if both_ways else np.where(n < 0, BUCKETS, ids))
    far = bucket_of(np.array([2 * TILE - TILE + 1, -(2 * TILE - TILE + 1)]), both_ways)
    if not both_ways:
        far[1] = BUCKETS
    return np.stack(tiles).astype(np.int32), far.astype(np.int32)


def sum_ids(both_ways):
    p = np.arange(2 * TILE)
    parts = []
    for step in (0, 1, -1):
        n = TILE - 1 - p + step * TILE
        ids = bucket_of(n, both_ways)
        parts.append(np.where((p == 2 * TILE - 1) | ((n < 0) & (not both_ways)), TILE, ids))
    far = tile_ids(both_ways)[1]
    parts += [np.full(TILE, b if b < BUCKETS else TILE) for b in far]
    return np.concatenate(parts).astype(np.int32)


def dot(a, b):
    return jnp.dot(a, b, preferred_element_type=f32)


def dot_nt(a, b):
    return lax.dot_general(a, b, (((1,), (1,)), ((), ())), preferred_element_type=f32)


def rms(v, gain):
    return v * lax.rsqrt(jnp.mean(v * v, axis=-1, keepdims=True) + EPSILON) * gain


def rms_back(v, gain, dy):
    r = lax.rsqrt(jnp.mean(v * v, axis=-1, keepdims=True) + EPSILON)
    dgain = jnp.sum(dy * v * r, axis=0, keepdims=True)
    gdy = dy * gain
    dv = r * gdy - v * (r * r * r * jnp.mean(gdy * v, axis=-1, keepdims=True))
    return dv, dgain


def half_lanes(value, which):
    lane = lax.broadcasted_iota(jnp.int32, value.shape, 1)
    return jnp.where((lane // HEAD) == which, value, jnp.zeros_like(value))


def tile_of(step):
    return {0: 0, 1: 1, -1: 2}.get(step)


def part_plan(count, k):
    if count == 1:
        return [(None, 0, k)]
    half = k // 2
    plan = [(0, 0, k), (2, 0, k), (4, 0, k), (6, 0, half), (6, half, half)]
    return plan + [(flip ^ 1, first, units) for flip, first, units in plan]


def attn_loads(me, parts, w_s, units, sem):
    copies = []
    for part, (flip, first, count) in zip(parts, part_plan(len(parts), 4)):
        for u in units:
            if first <= u < first + count:
                to = w_s.at[u] if flip is None else w_s.at[u, me ^ flip]
                copies.append(pltpu.make_async_copy(part.at[u - first], to, sem))
    return copies


def only(role, kernel):
    if role is None:
        return kernel

    def guarded(me_ref, *refs):
        @pl.when(me_ref[1] == role)
        def _():
            kernel(me_ref, *refs)

    return guarded


def start_all(copies):
    for copy in copies:
        copy.start()


def wait_all(copies):
    for copy in copies:
        copy.wait()


def matrix(w_s, unit):
    return w_s[unit].reshape(D, D)


def put_blocks(me, value, unit, keep, send):
    value = value.astype(bf16)
    odd = (me % 2) == 1
    for i in range(4):
        even_rows = value[2 * i * ROWS8 : (2 * i + 1) * ROWS8]
        odd_rows = value[(2 * i + 1) * ROWS8 : (2 * i + 2) * ROWS8]
        slot = i ^ (me // 2)
        rows = slice(unit * ROWS8, (unit + 1) * ROWS8) if isinstance(unit, int) else unit
        keep[slot, rows, :] = jnp.where(odd, odd_rows, even_rows)
        send[slot, rows, :] = jnp.where(odd, even_rows, odd_rows)


def attn_fwd_kernel(has_bias, nparts, *refs):
    refs = list(refs)
    me_ref, src, gain = refs[:3]
    refs = refs[3:]
    ksrc = None
    if not has_bias:
        ksrc = refs.pop(0)
    segr, segc = refs[:2]
    refs = refs[2:]
    if has_bias:
        bias, far = refs[:2]
        refs = refs[2:]
    parts = refs[:nparts]
    refs = refs[nparts:]
    z, zlow, q_o, k_o, v_o, o_o, p_o, w_s, q_s, k_s, v_s, o_s, p_s, w_sem, out_sem = refs
    me = me_ref[0]

    loads = [attn_loads(me, parts, w_s, (u,), w_sem.at[u]) for u in range(4)]
    for load in loads:
        start_all(load)
    a = rms(src[...].astype(f32), gain[...]).astype(bf16)
    b = a if ksrc is None else ksrc[...]
    outs = []
    for value, weight, out, scr in ((a, 0, q_o, q_s), (b, 1, k_o, k_s), (b, 2, v_o, v_s)):
        wait_all(loads[weight])
        full = dot(value, matrix(w_s, weight)).astype(bf16)
        for p in range(PAIRS):
            scr[p] = full[:, p * TILE : (p + 1) * TILE]
        outs.append(pltpu.make_async_copy(scr, out, out_sem.at[weight]))
        outs[-1].start()

    def prob_copy(p):
        return pltpu.make_async_copy(p_s.at[pl.ds(2 * p, 2)], p_o.at[pl.ds(2 * p, 2)], out_sem.at[4])

    def pair(p, carry):
        qp, kp, vp = q_s[p], k_s[p], v_s[p]
        total = [None] * BLOCKS
        for which in range(2):
            h = 2 * p + which
            kz, vz = half_lanes(kp, which), half_lanes(vp, which)
            for bi in range(BLOCKS):
                rows = slice(bi * TILE, (bi + 1) * TILE)
                s = dot_nt(qp[rows], kz)
                if has_bias:
                    tiles = []
                    for bj in range(BLOCKS):
                        step = bi - bj
                        part = s[:, bj * TILE : (bj + 1) * TILE]
                        if abs(step) < 2:
                            part = part + bias[h, tile_of(step)]
                        else:
                            part = part + far[h, 0 if step > 0 else 1]
                        tiles.append(part)
                    s = jnp.concatenate(tiles, axis=1)
                s = jnp.where(segc[rows] == segr[...], s, MASKED)
                e = jnp.exp(s - jnp.max(s, axis=-1, keepdims=True))
                prob = (e * (1.0 / jnp.sum(e, axis=-1, keepdims=True))).astype(bf16)
                p_s[h, rows, :] = prob
                o = dot(prob, vz)
                total[bi] = o if total[bi] is None else total[bi] + o
        o_s[p] = jnp.concatenate(total, axis=0).astype(bf16)
        prob_copy(p).start()
        return carry

    lax.fori_loop(0, PAIRS, pair, 0)
    outs.append(pltpu.make_async_copy(o_s, o_o, out_sem.at[3]))
    outs[-1].start()
    mixed = jnp.concatenate([o_s[p] for p in range(PAIRS)], axis=1)
    wait_all(loads[3])
    result = src[...].astype(f32) + dot(mixed, matrix(w_s, 3))
    z[...] = result
    zlow[...] = result.astype(bf16)
    wait_all(outs)
    for p in range(PAIRS):
        prob_copy(p).wait()


VM = pl.BlockSpec(memory_space=pltpu.VMEM)
SM = pl.BlockSpec(memory_space=pltpu.SMEM)
HBM = pl.BlockSpec(memory_space=pl.ANY)
HEAD_ROWS = jax.ShapeDtypeStruct((PAIRS, LEN, TILE), bf16)
LOW_ROWS = jax.ShapeDtypeStruct((LEN, D), bf16)
FULL_ROWS = jax.ShapeDtypeStruct((LEN, D), f32)
ONE_ROW = jax.ShapeDtypeStruct((1, D), f32)
PARAMS = pltpu.CompilerParams(vmem_limit_bytes=VMEM_LIMIT)


def attn_fwd(me, src, gain, parts, segr, segc, ksrc=None, bias=None, far=None):
    has_bias = bias is not None
    args = [me, src, gain] + ([] if has_bias else [ksrc]) + [segr, segc]
    specs = [SM] + [VM] * (len(args) - 1)
    if has_bias:
        args += [bias, far]
        specs += [VM, SM]
    args += parts
    specs += [HBM] * len(parts)
    return pl.pallas_call(
        only(
            None if has_bias else 0,
            functools.partial(attn_fwd_kernel, has_bias, len(parts)),
        ),
        out_shape=(FULL_ROWS, LOW_ROWS)
        + (HEAD_ROWS,) * 4
        + (jax.ShapeDtypeStruct((HEADS, LEN, LEN), bf16),),
        in_specs=specs,
        out_specs=(VM,) * 2 + (HBM,) * 5,
        scratch_shapes=[pltpu.VMEM((4, 8, ROWS8, D), bf16)]
        + [pltpu.VMEM((PAIRS, LEN, TILE), bf16)] * 4
        + [pltpu.VMEM((HEADS, LEN, LEN), bf16)]
        + [pltpu.SemaphoreType.DMA((4,)), pltpu.SemaphoreType.DMA((5,))],
        compiler_params=PARAMS,
        name="self_fwd" if has_bias else "cross_fwd",
    )(*args)


def attn_bwd_kernel(has_bias, nparts, *refs):
    refs = list(refs)
    me_ref, gres, src, gain = refs[:4]
    refs = refs[4:]
    gother = ksrc = None
    if has_bias:
        gother, gains, hot = refs[:3]
        refs = refs[3:]
    else:
        ksrc = refs.pop(0)
    q_i, k_i, v_i, o_i, p_i = refs[:5]
    refs = refs[5:]
    parts = refs[:nparts]
    refs = refs[nparts:]
    din, keep, send = refs[:3]
    refs = refs[3:]
    if has_bias:
        vec_s = refs.pop()
    else:
        dgain, dkey = refs[:2]
        refs = refs[2:]
    w_s, p_s, do_s, dq_s, dk_s, dv_s, ds_s, keep_s, send_s, w_sem, p_sem, out_sem = refs
    me = me_ref[0]

    out_load = attn_loads(me, parts, w_s, (3,), w_sem.at[0])
    rest_load = attn_loads(me, parts, w_s, (0, 1, 2), w_sem.at[1])

    def prob_copy(p):
        return pltpu.make_async_copy(p_i.at[pl.ds(2 * p, 2)], p_s.at[pl.ds(2 * p, 2)], p_sem.at[p])

    start_all(out_load)
    for p in range(PAIRS):
        prob_copy(p).start()
    start_all(rest_load)
    base = gres[...].astype(f32)
    if has_bias:
        base = jnp.where(me_ref[1] == 1, gother[...].astype(f32), base)
    g = base.astype(bf16)
    wait_all(out_load)
    do = dot_nt(g, matrix(w_s, 3)).astype(bf16)
    for p in range(PAIRS):
        do_s[p] = do[:, p * TILE : (p + 1) * TILE]

    if has_bias:
        down = lax.broadcasted_iota(jnp.int32, (TILE, TILE), 0)
        along = lax.broadcasted_iota(jnp.int32, (TILE, TILE), 1)
        mirror = (down + along == TILE - 1).astype(bf16)

    def pair(p, carry):
        qp, kp, vp, dop = q_i[p], k_i[p], v_i[p], do_s[p]
        q_t, do_t = qp.T, dop.T
        total = [None] * BLOCKS
        prob_copy(p).wait()
        for which in range(2):
            h = 2 * p + which
            kz, vz = half_lanes(kp, which), half_lanes(vp, which)
            diag = {0: None, 1: None, -1: None, 2: None, -2: None}
            for bi in range(BLOCKS):
                rows = slice(bi * TILE, (bi + 1) * TILE)
                dp = dot_nt(dop[rows], vz)
                prob = p_s[h, rows, :].astype(f32)
                t = prob * dp
                ds = t - prob * jnp.sum(t, axis=-1, keepdims=True)
                if has_bias:
                    for bj in range(BLOCKS):
                        step = max(-2, min(2, bi - bj))
                        part = ds[:, bj * TILE : (bj + 1) * TILE]
                        diag[step] = part if diag[step] is None else diag[step] + part
                low = ds.astype(bf16)
                ds_s[which, rows, :] = low
                dq = dot(low, kz)
                total[bi] = dq if total[bi] is None else total[bi] + dq
            if has_bias:
                near = jnp.concatenate([diag[step] for step in (0, 1, -1)], axis=1)
                near = dot(mirror, near.astype(bf16))
                nothing = jnp.zeros((TILE, TILE), f32)
                for t in range(3):
                    part = near[:, t * TILE : (t + 1) * TILE]
                    part = pltpu.roll(
                        jnp.concatenate([part, nothing], axis=1), 0, 1, stride=1, stride_axis=0
                    )
                    vec_s[h, :, 2 * t * TILE : 2 * (t + 1) * TILE] = jnp.sum(
                        part, axis=0, keepdims=True
                    )
                for n, step in ((6, 2), (7, -2)):
                    vec_s[h, :, n * TILE : (n + 1) * TILE] = jnp.sum(
                        diag[step], axis=0, keepdims=True
                    )
            half = slice(which * HEAD, (which + 1) * HEAD)
            dk_s[p, half, :] = dot(q_t[half], ds_s[which]).astype(bf16)
            dv_s[p, half, :] = dot(do_t[half], p_s[h]).astype(bf16)
        dq_s[p] = jnp.concatenate(total, axis=0).astype(bf16)
        return carry

    lax.fori_loop(0, PAIRS, pair, 0)
    v = src[...].astype(f32)
    a = rms(v, gain[...]).astype(bf16)
    a_t = a.T
    b_t = a_t if ksrc is None else ksrc[...].T
    dq = jnp.concatenate([dq_s[p] for p in range(PAIRS)], axis=1)
    dk_t = dk_s[...].reshape(D, LEN)
    dv_t = dv_s[...].reshape(D, LEN)
    wait_all(rest_load)
    query_side = dot_nt(dq, matrix(w_s, 0))
    key_side = dot_nt(dk_t.T, matrix(w_s, 1)) + dot_nt(dv_t.T, matrix(w_s, 2))
    if has_bias:
        query_side = query_side + key_side
    else:
        dkey[...] = key_side.astype(bf16)
    dv, dg = rms_back(v, gain[...], query_side)
    din[...] = (base + dv).astype(din.dtype)
    if has_bias:
        table = dot(vec_s[...].reshape(HEADS, 8 * TILE).astype(bf16), hot[...])
        table = jnp.concatenate([table, jnp.zeros((HEADS, D - TILE), f32)], axis=1)
        rows = jnp.concatenate([table, dg, gains[...], jnp.zeros((1, D), f32)], axis=0)
        for slot in range(4):
            keep_s[slot, D // 2 :, :] = rows.astype(bf16)
            send_s[slot, D // 2 :, :] = rows.astype(bf16)
    else:
        dgain[...] = dg
    put_blocks(me, dot(a_t, dq), 0, keep_s, send_s)
    put_blocks(me, dot_nt(b_t, dk_t), 1, keep_s, send_s)
    put_blocks(me, dot_nt(b_t, dv_t), 2, keep_s, send_s)
    mixed = jnp.concatenate([o_i[p] for p in range(PAIRS)], axis=1)
    put_blocks(me, dot(mixed.T, g), 3, keep_s, send_s)
    outs = [
        pltpu.make_async_copy(send_s, send, out_sem.at[0]),
        pltpu.make_async_copy(keep_s, keep, out_sem.at[1]),
    ]
    start_all(outs)
    wait_all(outs)


BLOCKS8 = jax.ShapeDtypeStruct((4, D, D), bf16)


def attn_bwd(me, gres, src, gain, parts, saved, ksrc=None, others=()):
    has_bias = ksrc is None
    args = [me, gres, src, gain] + (list(others) if has_bias else [ksrc]) + [*saved, *parts]
    specs = [SM] + [VM] * (len(args) - 2 - len(parts)) + [HBM] * (1 + len(parts))
    rows = D // 2 + (EXTRA if has_bias else 0)
    pack = jax.ShapeDtypeStruct((4, rows, D), bf16)
    outs = [LOW_ROWS, pack, pack] if has_bias else [FULL_ROWS, pack, pack, ONE_ROW, LOW_ROWS]
    return pl.pallas_call(
        only(
            None if has_bias else 0,
            functools.partial(attn_bwd_kernel, has_bias, len(parts)),
        ),
        out_shape=tuple(outs),
        in_specs=specs,
        out_specs=tuple([VM, HBM, HBM] + [VM] * (len(outs) - 3)),
        scratch_shapes=[
            pltpu.VMEM((4, 8, ROWS8, D), bf16),
            pltpu.VMEM((HEADS, LEN, LEN), bf16),
            pltpu.VMEM((PAIRS, LEN, TILE), bf16),
            pltpu.VMEM((PAIRS, LEN, TILE), bf16),
            pltpu.VMEM((PAIRS, TILE, LEN), bf16),
            pltpu.VMEM((PAIRS, TILE, LEN), bf16),
            pltpu.VMEM((2, LEN, LEN), bf16),
            pltpu.VMEM((4, rows, D), bf16),
            pltpu.VMEM((4, rows, D), bf16),
            pltpu.SemaphoreType.DMA((2,)),
            pltpu.SemaphoreType.DMA((PAIRS,)),
            pltpu.SemaphoreType.DMA((2,)),
        ]
        + ([pltpu.VMEM((HEADS, 1, 8 * TILE), f32)] if has_bias else []),
        compiler_params=PARAMS,
        name="self_bwd" if has_bias else "cross_bwd",
    )(*args)


GELU_C = float(np.sqrt(2.0 / np.pi))


def gelu_parts(u):
    square = u * u
    t = jnp.tanh(GELU_C * (u + 0.044715 * (u * square)))
    half = 0.5 + 0.5 * t
    slope = half + (half * (1.0 - t)) * (u * (GELU_C + (3 * 0.044715 * GELU_C) * square))
    return u * half, slope


def ffn_kernel(mode, nparts, *refs):
    fwd, bwd = mode != "bwd", mode != "fwd"
    refs = list(refs)
    me_ref, x, gain = refs[:3]
    refs = refs[3:]
    g = refs.pop(0) if bwd else None
    if mode == "bwd":
        h_i, slope_i = refs[:2]
        refs = refs[2:]
    parts = refs[:nparts]
    refs = refs[nparts:]
    out = refs.pop(0) if fwd else None
    if mode == "fwd":
        h_o, slope_o = refs[:2]
        refs = refs[2:]
    if bwd:
        dx, dgain, keep, send = refs[:4]
        refs = refs[4:]
    wi_s, wo_s, w_sem = refs[:3]
    refs = refs[3:]
    if fwd:
        n_s, acc = refs[:2]
        refs = refs[2:]
    if bwd:
        nt_s, dn, keep_s, send_s, out_sem = refs
    me = me_ref[0]
    step = pl.program_id(0)
    plan = part_plan(nparts, 8)

    def in_loads(unit):
        copies = []
        for part, (flip, first, count) in zip(parts, plan):
            if first == 0:
                to = wi_s.at[unit] if flip is None else wi_s.at[unit, me ^ flip]
                copies.append(pltpu.make_async_copy(part.at[unit], to, w_sem.at[unit]))
        return copies

    def out_loads():
        copies = []
        for part, (flip, first, count) in zip(parts, plan):
            if first + count == 8:
                if flip is None:
                    for k in range(4):
                        copies.append(
                            pltpu.make_async_copy(part.at[4 + k], wo_s.at[:, k], w_sem.at[4])
                        )
                else:
                    copies.append(
                        pltpu.make_async_copy(
                            part.at[pl.ds(4 - first, 4)], wo_s.at[me ^ flip], w_sem.at[4]
                        )
                    )
        return copies

    @pl.when(step == 0)
    def _():
        start_all(in_loads(0))
        start_all(out_loads())
        for unit in range(1, 4):
            start_all(in_loads(unit))
        v = x[...].astype(f32)
        n = rms(v, gain[...]).astype(bf16)
        if fwd:
            n_s[...] = n
            acc[...] = v
        if bwd:
            nt_s[...] = n.T
            dn[...] = jnp.zeros_like(dn)

    for unit in range(4):

        @pl.when(step == unit)
        def _():
            wait_all(in_loads(unit))

    wi = wi_s[step].reshape(D, D)
    if fwd:
        h, slope = gelu_parts(dot(n_s[...], wi))
        h = h.astype(bf16)
        if mode == "fwd":
            h_o[0] = h
            slope_o[0] = slope.astype(bf16)
    else:
        h, slope = h_i[0], slope_i[0].astype(f32)

    @pl.when(step == 0)
    def _():
        wait_all(out_loads())

    wo = wo_s[pl.ds(2 * step, 2)].reshape(D, D)
    if fwd:
        acc[...] += dot(h, wo)
    if bwd:
        du = (slope * dot_nt(g[...], wo)).astype(bf16)
        dn[...] += dot_nt(du, wi)
        in_rows = pl.ds(pl.multiple_of(step * ROWS8, 32), ROWS8)
        put_blocks(me, dot(nt_s[...], du), in_rows, keep_s, send_s)
        dwo = dot(h.T, g[...]).astype(bf16)
        odd = (me % 2) == 1
        slot = step ^ (me // 2)
        for k in range(4):
            first, second = dwo[k * ROWS8 : (k + 1) * ROWS8], dwo[(4 + k) * ROWS8 : (5 + k) * ROWS8]
            rows = slice((4 + k) * ROWS8, (5 + k) * ROWS8)
            keep_s[slot, rows, :] = jnp.where(odd, second, first)
            send_s[slot, rows, :] = jnp.where(odd, first, second)

        def outs(c):
            slot = c ^ (me // 2)
            copies = []
            for n, (here, there) in enumerate(((send_s, send), (keep_s, keep))):
                part = pl.ds(pl.multiple_of(c * ROWS8, 32), ROWS8)
                copies.append(
                    pltpu.make_async_copy(here.at[:, part], there.at[:, part], out_sem.at[2 * n])
                )
                last = pl.ds(D // 2, D // 2)
                copies.append(
                    pltpu.make_async_copy(here.at[slot, last], there.at[slot, last], out_sem.at[2 * n + 1])
                )
            return copies

        start_all(outs(step))

    @pl.when(step == pl.num_programs(0) - 1)
    def _():
        if fwd:
            out[...] = acc[...].astype(bf16)
        if bwd:
            dv, dg = rms_back(x[...].astype(f32), gain[...], dn[...])
            dgain[...] = dg
            dx[...] = (g[...].astype(f32) + dv).astype(bf16)
            for c in range(4):
                wait_all(outs(c))


def ffn(mode, me, x, gain, parts, g=None, saved=()):
    fwd, bwd = mode != "bwd", mode != "fwd"
    whole = pl.BlockSpec((LEN, D), lambda c: (0, 0))
    one = pl.BlockSpec((1, D), lambda c: (0, 0))
    hidden = pl.BlockSpec((1, LEN, D), lambda c: (c, 0, 0))
    hidden_shape = jax.ShapeDtypeStruct((4, LEN, D), bf16)
    args, specs = [me, x, gain], [SM, whole, one]
    if bwd:
        args, specs = args + [g], specs + [whole]
    args += list(saved)
    specs += [hidden] * len(saved)
    args += parts
    specs += [HBM] * len(parts)
    shapes, out_specs = [], []
    scratch = [
        pltpu.VMEM((4, 8, ROWS8, D), bf16),
        pltpu.VMEM((8, 4, ROWS8, D), bf16),
        pltpu.SemaphoreType.DMA((5,)),
    ]
    if fwd:
        shapes, out_specs = [LOW_ROWS], [whole]
        scratch += [pltpu.VMEM((LEN, D), bf16), pltpu.VMEM((LEN, D), f32)]
    if mode == "fwd":
        shapes += [hidden_shape] * 2
        out_specs += [hidden] * 2
    if bwd:
        shapes += [LOW_ROWS, ONE_ROW, BLOCKS8, BLOCKS8]
        out_specs += [whole, one, HBM, HBM]
        scratch += [
            pltpu.VMEM((D, LEN), bf16),
            pltpu.VMEM((LEN, D), f32),
            pltpu.VMEM((4, D, D), bf16),
            pltpu.VMEM((4, D, D), bf16),
            pltpu.SemaphoreType.DMA((4,)),
        ]
    return pl.pallas_call(
        only(0 if mode == "both" else 1, functools.partial(ffn_kernel, mode, len(parts))),
        grid=(4,),
        out_shape=tuple(shapes),
        in_specs=specs,
        out_specs=tuple(out_specs),
        scratch_shapes=scratch,
        compiler_params=PARAMS,
        name="ffn_" + mode,
    )(*args)


def wide_add(*values):
    total = values[0].astype(f32)
    for value in values[1:]:
        total = total + value.astype(f32)
    return total.astype(bf16)


def diag_kernel(me_ref, keep, recv, by_x, by_y, keep_s, recv_s, sem):
    half = by_x.shape[0]
    loads = [
        pltpu.make_async_copy(keep.at[3], keep_s, sem.at[0]),
        pltpu.make_async_copy(recv.at[3], recv_s, sem.at[1]),
    ]
    start_all(loads)
    wait_all(loads)
    keep_s[...] = wide_add(keep_s[...], recv_s[...])
    stores = [
        pltpu.make_async_copy(keep_s.at[:half], by_x, sem.at[0]),
        pltpu.make_async_copy(keep_s.at[half:], by_y, sem.at[1]),
    ]
    start_all(stores)
    wait_all(stores)


def diag_add(role, me, keep, recv):
    _, r, c = keep.shape
    half = r // 32 * 16
    return pl.pallas_call(
        only(role, diag_kernel),
        out_shape=tuple(jax.ShapeDtypeStruct((n, c), bf16) for n in (half, r - half)),
        in_specs=[SM, HBM, HBM],
        out_specs=(HBM, HBM),
        scratch_shapes=[pltpu.VMEM((r, c), bf16)] * 2 + [pltpu.SemaphoreType.DMA((2,))],
        compiler_params=PARAMS,
        name="diag_add",
    )(me, keep, recv)


def rest_kernel(
    me_ref, keep, recv, from_x, from_y, own, for_x, for_y, keep_s, recv_s, x_s, y_s, sem
):
    half = from_x.shape[0]
    loads = []
    for slot in range(3):
        loads.append(pltpu.make_async_copy(keep.at[slot], keep_s.at[slot], sem.at[2 * slot]))
        loads.append(pltpu.make_async_copy(recv.at[slot], recv_s.at[slot], sem.at[2 * slot + 1]))
    loads.append(pltpu.make_async_copy(from_x, x_s, sem.at[6]))
    loads.append(pltpu.make_async_copy(from_y, y_s, sem.at[7]))
    start_all(loads[2:4] + loads[6:] + loads[4:6] + loads[:2])
    stores = []
    for slot, out in ((1, for_x), (2, for_y), (0, own)):
        wait_all(loads[2 * slot : 2 * slot + 2])
        if slot == 1:
            wait_all(loads[6:])
            top, low = (), (y_s[...],)
        else:
            top, low = ((x_s[...],), ()) if slot == 2 else ((), ())
        keep_s[slot, :half] = wide_add(keep_s[slot, :half], recv_s[slot, :half], *top)
        keep_s[slot, half:] = wide_add(keep_s[slot, half:], recv_s[slot, half:], *low)
        stores.append(pltpu.make_async_copy(keep_s.at[slot], out, sem.at[8 + slot]))
        stores[-1].start()
    wait_all(stores)


def rest_add(role, me, keep, recv, from_x, from_y):
    _, r, c = keep.shape
    half = r // 32 * 16
    shape = jax.ShapeDtypeStruct((r, c), bf16)
    return pl.pallas_call(
        only(role, rest_kernel),
        out_shape=(shape,) * 3,
        in_specs=[SM] + [HBM] * 4,
        out_specs=(HBM,) * 3,
        scratch_shapes=[pltpu.VMEM((3, r, c), bf16)] * 2
        + [pltpu.VMEM((half, c), bf16), pltpu.VMEM((r - half, c), bf16)]
        + [pltpu.SemaphoreType.DMA((11,))],
        compiler_params=PARAMS,
        name="rest_add",
    )(me, keep, recv, from_x, from_y)


ALL = (0, 1, 2, 3)
ENC = (1, 2)
DEC = (0, 3)


def across(x, flip, planes):
    wide, narrow = lax.axis_size("wide"), lax.axis_size("narrow")
    pairs = [(i * narrow + n, (i ^ flip) * narrow + n) for i in range(wide) for n in planes]
    return lax.ppermute(x, ("wide", "narrow"), pairs)


def between(x, pairs):
    return lax.ppermute(x, "narrow", pairs)


def in_units(local):
    return jnp.transpose(local.reshape(local.shape[0], 4, D), (1, 0, 2))


def out_units(local):
    return local.reshape(4, local.shape[0] // 4, D)


def tie(*values):
    return lax.optimization_barrier(values)


def whole_pack(shard):
    k = shard.shape[0]
    full = lax.all_gather(shard, "wide", axis=1)
    if k == 8:
        inner = full[:4].reshape(4, 8, ROWS8, D)
        outer = jnp.transpose(full[4:], (1, 0, 2, 3)).reshape(8, 4, ROWS8, D)
        return [jnp.concatenate([inner, jnp.transpose(outer, (1, 0, 2, 3))])]
    return [full.reshape(k, 8, ROWS8, D)]


def gather_near(shard, planes=ALL):
    return across(shard, 2, planes), across(shard, 4, planes), across(shard, 1, planes)


def gather_far(shard, near, planes=ALL):
    px, py, pc = near
    k = shard.shape[0]
    first = across(px[: k // 2], 4, planes)
    second = across(py[k // 2 :], 2, planes)
    parts = [px, py, first, second]
    return [shard] + parts + [pc] + [across(part, 1, planes) for part in parts]


def whole_scatter(keep, send):
    blocks = jnp.stack([keep, send], axis=1).reshape(8, -1, D)
    k = blocks.shape[1] // ROWS8
    weights = blocks[:, : k * ROWS8].reshape(8, k, ROWS8, D)
    inner = jnp.transpose(weights[:, :4], (1, 0, 2, 3)).reshape(4, D, D)
    inner = lax.psum_scatter(inner, "wide", scatter_dimension=1, tiled=True).reshape(-1, D)
    if k == 8:
        last = weights[:, 4:].reshape(FF, D)
        last = lax.psum_scatter(last, "wide", scatter_dimension=0, tiled=True)
    else:
        last = lax.psum(blocks[0, k * ROWS8 :], "wide")
    return jnp.concatenate([inner, last])


class Scatter:
    def __init__(self, me, keep, send, planes):
        self.me, self.keep, self.planes = me, keep, planes
        self.role = {ENC: 1, DEC: 0, ALL: None}[planes]
        self.small = lax.axis_size("wide") == 8
        self.state = (send,)
        if self.small:
            self.state = (across(send, 1, planes),)
        self.phase, self.token = 0, keep

    def go(self):
        if not self.small:
            return self
        if self.phase == 0:
            (self.recv,) = self.state
            by_x, by_y = diag_add(self.role, self.me, self.keep, self.recv)
            self.token = by_x
            self.state = across(by_x, 2, self.planes), across(by_y, 4, self.planes)
        elif self.phase == 1:
            own, for_x, for_y = rest_add(self.role, self.me, self.keep, self.recv, *self.state)
            self.token = own
            self.state = own, across(for_x, 2, self.planes), across(for_y, 4, self.planes)
        self.phase += 1
        return self

    def result(self):
        if not self.small:
            return whole_scatter(self.keep, self.state[0])
        return wide_add(*self.state)

    def halves(self):
        if not self.small:
            return jnp.split(self.result(), 2)
        half = self.state[0].shape[0] // 2
        return wide_add(*[v[:half] for v in self.state]), wide_add(*[v[half:] for v in self.state])


def tie_all(scatters, *values):
    counts = [len(s.state) for s in scatters]
    flat = tie(*[v for s in scatters for v in s.state], *values)
    for s, count in zip(scatters, counts):
        s.state, flat = flat[:count], flat[count:]
    return flat


class FromMiddle:
    def __init__(self, share, middle):
        self.share, self.middle = share, middle
        self.state = (between(share, [(1, 2), (2, 1)]),)

    def go(self):
        self.total = wide_add(self.share, *self.state)
        self.state = (between(self.total, [(1, 0), (2, 3)]),)
        return self

    def result(self):
        return jnp.where(self.middle, self.total, *self.state).astype(f32)


class FromEnds:
    def __init__(self, share, middle):
        self.share, self.middle = share, middle
        self.got, self.state = [], (between(share, [(0, 1), (3, 2)]),)

    def go(self):
        self.got.append(self.state[0])
        pairs = [(1, 2), (2, 1)] if len(self.got) == 1 else [(1, 0), (2, 3)]
        self.state = (between(self.state[0], pairs),)
        return self

    def result(self):
        near, far = self.got
        first = jnp.where(self.middle, near, self.share).astype(f32)
        return first + jnp.where(self.middle, far, *self.state).astype(f32)


def on_device(
    enc_in,
    dec_in,
    dec_cot,
    segments,
    enc_attn_gain,
    enc_query,
    enc_key,
    enc_value,
    enc_output,
    enc_table,
    enc_ffn_gain,
    enc_ffn_in,
    enc_ffn_out,
    dec_self_gain,
    dec_query,
    dec_key,
    dec_value,
    dec_output,
    dec_table,
    dec_cross_gain,
    cross_query,
    cross_key,
    cross_value,
    cross_output,
    dec_ffn_gain,
    dec_ffn_in,
    dec_ffn_out,
):
    plane = lax.axis_index("narrow")
    is_enc = (plane == 1) | (plane == 2)
    row = plane // 2

    def own(x):
        return lax.dynamic_slice_in_dim(x, row * LEN, LEN, 0)

    def pick(enc, dec):
        return jnp.where(is_enc, enc, dec)

    def gain_of(g):
        return g.astype(f32).reshape(1, D)

    seg = lax.dynamic_slice_in_dim(segments, row, 1, 0)
    segr, segc = seg, seg.reshape(LEN, 1)
    src = pick(own(enc_in), own(dec_in))
    cot = own(dec_cot)

    me = lax.axis_index("wide") if lax.axis_size("wide") == 8 else 0
    me = jnp.stack([jnp.asarray(me, jnp.int32), is_enc.astype(jnp.int32)])

    pack_a = jnp.stack(
        [
            pick(enc_query, dec_query),
            pick(enc_key, dec_key),
            pick(enc_value, dec_value),
            pick(enc_output, dec_output),
        ]
    )
    pack_f = jnp.concatenate(
        [in_units(pick(enc_ffn_in, dec_ffn_in)), out_units(pick(enc_ffn_out, dec_ffn_out))]
    )
    pack_c = jnp.stack([cross_query, cross_key, cross_value, cross_output])
    shard_rows = enc_query.shape[0]
    small = lax.axis_size("wide") == 8
    if small:
        near_a = gather_near(pack_a)

    enc_ids, enc_far = tile_ids(True)
    dec_ids, dec_far = tile_ids(False)
    ids = pick(jnp.asarray(enc_ids), jnp.asarray(dec_ids))
    far_ids = pick(jnp.asarray(enc_far), jnp.asarray(dec_far))
    buckets = jnp.arange(BUCKETS + 1, dtype=jnp.int32)
    hot = (ids[None] == buckets[:, None, None, None]).astype(bf16)
    far_hot = (far_ids[None] == buckets[:, None]).astype(bf16)
    table = jnp.concatenate([pick(enc_table, dec_table), jnp.full((1, HEADS), MASKED, bf16)])
    bias = jnp.einsum("bh,bsij->hsij", table, hot, preferred_element_type=f32)
    far = jnp.einsum("bh,bs->hs", table, far_hot, preferred_element_type=f32)
    enc_sums, dec_sums = sum_ids(True), sum_ids(False)
    sums_of = pick(jnp.asarray(enc_sums), jnp.asarray(dec_sums))
    sum_hot = (sums_of[:, None] == jnp.arange(TILE, dtype=jnp.int32)).astype(bf16)

    gain_a = pick(gain_of(enc_attn_gain), gain_of(dec_self_gain))
    enc_gain = gain_of(enc_ffn_gain)
    gain_c = gain_of(dec_cross_gain)
    if small:
        *near_a, pack_f, bias, far, src, cot, segc, me = tie(
            *near_a, pack_f, bias, far, src, cot, segc, me
        )
        w_attn = gather_far(pack_a, near_a)
        near_f = gather_near(pack_f)
    else:
        w_attn, w_ffn, w_cross = whole_pack(pack_a), whole_pack(pack_f), whole_pack(pack_c)
    z1, x1, *saved = attn_fwd(me, src, gain_a, w_attn, segr, segc, bias=bias, far=far)
    if small:
        z1, x1, *near_f, pack_c = tie(z1, x1, *near_f, pack_c)
        w_ffn = gather_far(pack_f, near_f)
        near_c = gather_near(pack_c, DEC)
    enc_out, *saved_f = ffn("fwd", me, x1, enc_gain, w_ffn)
    if small:
        enc_out, *near_c = tie(enc_out, *near_c)
    memory = between(enc_out, [(1, 0), (2, 3)])
    if small:
        w_cross = gather_far(pack_c, near_c, DEC)
    _, z2, *saved_c = attn_fwd(me, z1, gain_c, w_cross, segr, segc, ksrc=memory)

    def by_columns(x):
        return lax.all_to_all(x, "narrow", split_axis=1, concat_axis=0, tiled=True)

    def rows_by_block(parts):
        rows = [parts[n * LEN : (n + 1) * LEN] for n in range(4)]
        return jnp.concatenate([rows[1], rows[2]]), jnp.concatenate([rows[0], rows[3]])

    dec_out, gz2, dgain_df, *blocks = ffn("both", me, z2, gain_of(dec_ffn_gain), w_ffn, cot)
    sum_df = Scatter(me, *blocks, DEC)
    gz1, *blocks_c, dgain_c, genc_out = attn_bwd(
        me, gz2, z1, gain_c, w_cross, saved_c, ksrc=memory
    )
    genc = between(genc_out, [(0, 1), (3, 2)])
    sum_c = Scatter(me, *blocks_c, DEC)
    out_rows = pick(enc_out, dec_out)
    (out_rows,) = tie_all([sum_df, sum_c], out_rows)
    sum_df.go()
    genc, out_rows, _ = tie(genc, out_rows, sum_df.token)
    gx1, dgain_ef, *blocks = ffn("bwd", me, x1, enc_gain, w_ffn, genc, saved_f)
    gx1, out_rows, *blocks = tie_all([sum_df], gx1, out_rows, *blocks)
    sum_ef = Scatter(me, *blocks, ENC)
    sum_df.go()
    out_rows, _ = tie_all([sum_c], out_rows, sum_df.token)
    out_cols = by_columns(out_rows)
    sum_c.go()
    gains = jnp.concatenate([pick(dgain_ef, dgain_df), dgain_c])
    din, *blocks = attn_bwd(
        me, gz1, src, gain_a, w_attn, saved, others=(gx1, gains, sum_hot)
    )
    din, out_cols, *blocks = tie_all([sum_ef, sum_c, sum_df], din, out_cols, *blocks)
    sum_a = Scatter(me, *blocks, ALL)
    sum_ef.go()
    tie_all([sum_df, sum_c], sum_ef.token)
    first, last = sum_df.halves()
    all_d1 = FromEnds(first, is_enc)
    last = tie(last, first)[0]
    all_d2 = FromEnds(last, is_enc)
    tie_all([sum_c], last)
    sum_c.go()
    tie_all([sum_ef, sum_a], last)
    sum_ef.go()
    tie_all([all_d1], sum_ef.token)
    all_d1.go()
    tie_all([sum_a], sum_ef.token)
    sum_a.go()
    tie_all([all_d2, sum_c], sum_a.token)
    all_d2.go()
    all_c = FromEnds(sum_c.result(), is_enc)
    din, _ = tie(din, sum_a.token)
    grad_cols = by_columns(din)
    tie_all([sum_a, all_d1])
    sum_a.go()
    all_d1.go()
    tie_all([sum_ef, all_c, all_d2], sum_a.token)
    first, last = sum_ef.halves()
    all_f1 = FromMiddle(first, is_enc)
    last = tie(last, first)[0]
    all_f2 = FromMiddle(last, is_enc)
    all_d2.go()
    all_c.go()
    tie_all([sum_a], last)
    s_a = sum_a.result()
    all_e = FromMiddle(s_a, is_enc)
    all_s = FromEnds(s_a, is_enc)
    tie_all([all_f1], s_a)
    all_f1.go()
    tie_all([all_f2], all_f1.total)
    all_f2.go()
    tie_all([all_e, all_s, all_c], all_f2.total)
    all_e.go()
    all_s.go()
    all_c.go()
    tie_all([all_s], all_e.total)
    all_s.go()

    def split(f):
        return f[: 4 * shard_rows].reshape(4, shard_rows, D), f[4 * shard_rows :]

    g_c, g_s, g_e = (split(p.result()) for p in (all_c, all_s, all_e))

    def in_rows(f):
        return jnp.transpose(f.result().reshape(4, shard_rows, D), (1, 0, 2)).reshape(-1, FF)

    gi_e, gi_d = in_rows(all_f1), in_rows(all_d1)
    go_e, go_d = all_f2.result(), all_d2.result()
    more_e, more_s = g_e[1], g_s[1]
    g_e, g_s, g_c = g_e[0], g_s[0], g_c[0]
    tables = [jnp.transpose(m[:HEADS, :BUCKETS]) for m in (more_e, more_s)]
    sums = [more_e[HEADS], more_e[HEADS + 1], more_s[HEADS], more_s[HEADS + 2], more_s[HEADS + 1]]
    enc_cols, dec_cols = rows_by_block(out_cols)
    enc_grad_cols, dec_grad_cols = rows_by_block(grad_cols)
    return (
        enc_cols,
        dec_cols,
        enc_grad_cols,
        dec_grad_cols,
        sums[0],
        g_e[0],
        g_e[1],
        g_e[2],
        g_e[3],
        tables[0],
        sums[1],
        gi_e,
        go_e,
        sums[2],
        g_s[0],
        g_s[1],
        g_s[2],
        g_s[3],
        tables[1],
        sums[3],
        g_c[0],
        g_c[1],
        g_c[2],
        g_c[3],
        sums[4],
        gi_d,
        go_d,
    )


def solution(mesh):
    rows, copied = P("wide", None), P()
    block = P("wide", "narrow")
    gains = (copied,)
    attention = (rows,) * 4
    placed = (
        (rows,) * 4
        + gains
        + attention
        + (copied,)
        + gains
        + (rows,) * 2
        + gains
        + attention
        + (copied,)
        + gains
        + attention
        + gains
        + (rows,) * 2
    )
    return jax.shard_map(
        on_device,
        mesh=mesh,
        in_specs=placed,
        out_specs=(block,) * 4 + placed[4:],
        check_vma=False,
    )
```

```python
import functools

import jax
import jax.numpy as jnp
import numpy as np
from jax import lax
from jax.experimental import pallas as pl
from jax.experimental.pallas import tpu as pltpu
from jax.sharding import PartitionSpec as P

D = 768
HEADS = 12
HEAD = 64
PAIRS = HEADS // 2
FF = 3072
BUCKETS = 32
MAXDIST = 128
LEN = 512
TILE = 128
BLOCKS = LEN // TILE
ROWS8 = D // 8
EXTRA = 16
PIECES = 2

EPSILON = 1e-06
MASKED = -1000000000.0
VMEM_LIMIT = 60 * 1024 * 1024
f32 = jnp.float32
bf16 = jnp.bfloat16


def bucket_of(reverse, both_ways):
    result = np.zeros(reverse.shape, np.int64)
    if both_ways:
        half_count = BUCKETS // 2
        result = result + (reverse < 0) * half_count
        reverse = np.abs(reverse)
    else:
        half_count = BUCKETS
        reverse = np.maximum(reverse, 0)
    exact_count = half_count // 2
    scaled = (
        np.log(np.maximum(reverse, 1) / exact_count)
        / np.log(MAXDIST / exact_count)
        * (half_count - exact_count)
    )
    far_bucket = np.minimum(
        exact_count + np.floor(np.maximum(scaled, 0.0)).astype(np.int64), half_count - 1
    )
    return result + np.where(reverse < exact_count, reverse, far_bucket)


def tile_ids(both_ways):
    i = np.arange(TILE)[:, None]
    j = np.arange(TILE)[None, :]
    tiles = []
    for step in (0, 1, -1):
        n = i - j + step * TILE
        ids = bucket_of(n, both_ways)
        tiles.append(ids if both_ways else np.where(n < 0, BUCKETS, ids))
    far = bucket_of(np.array([2 * TILE - TILE + 1, -(2 * TILE - TILE + 1)]), both_ways)
    if not both_ways:
        far[1] = BUCKETS
    return np.stack(tiles).astype(np.int32), far.astype(np.int32)


def sum_ids(both_ways):
    p = np.arange(2 * TILE)
    parts = []
    for step in (0, 1, -1):
        n = TILE - 1 - p + step * TILE
        ids = bucket_of(n, both_ways)
        parts.append(np.where((p == 2 * TILE - 1) | ((n < 0) & (not both_ways)), TILE, ids))
    far = tile_ids(both_ways)[1]
    parts += [np.full(TILE, b if b < BUCKETS else TILE) for b in far]
    return np.concatenate(parts).astype(np.int32)


def dot(a, b):
    return jnp.dot(a, b, preferred_element_type=f32)


def dot_nt(a, b):
    return lax.dot_general(a, b, (((1,), (1,)), ((), ())), preferred_element_type=f32)


def rms(v, gain):
    return v * lax.rsqrt(jnp.mean(v * v, axis=-1, keepdims=True) + EPSILON) * gain


def rms_back(v, gain, dy):
    r = lax.rsqrt(jnp.mean(v * v, axis=-1, keepdims=True) + EPSILON)
    dgain = jnp.sum(dy * v * r, axis=0, keepdims=True)
    gdy = dy * gain
    dv = r * gdy - v * (r * r * r * jnp.mean(gdy * v, axis=-1, keepdims=True))
    return dv, dgain


def half_lanes(value, which):
    lane = lax.broadcasted_iota(jnp.int32, value.shape, 1)
    return jnp.where((lane // HEAD) == which, value, jnp.zeros_like(value))


def tile_of(step):
    return {0: 0, 1: 1, -1: 2}.get(step)


def part_plan(count, k):
    if count == 1:
        return [(None, 0, k)]
    half = k // 2
    plan = [(0, 0, k), (2, 0, k), (4, 0, k), (6, 0, half), (6, half, half)]
    return plan + [(flip ^ 1, first, units) for flip, first, units in plan]


def attn_loads(me, parts, w_s, units, sem):
    copies = []
    for part, (flip, first, count) in zip(parts, part_plan(len(parts), 4)):
        for u in units:
            if first <= u < first + count:
                to = w_s.at[u] if flip is None else w_s.at[u, me ^ flip]
                copies.append(pltpu.make_async_copy(part.at[u - first], to, sem))
    return copies


def only(role, kernel):
    if role is None:
        return kernel

    def guarded(me_ref, *refs):
        @pl.when(me_ref[1] == role)
        def _():
            kernel(me_ref, *refs)

    return guarded


def start_all(copies):
    for copy in copies:
        copy.start()


def wait_all(copies):
    for copy in copies:
        copy.wait()


def matrix(w_s, unit):
    return w_s[unit].reshape(D, D)


def put_blocks(me, value, unit, keep, send):
    value = value.astype(bf16)
    odd = (me % 2) == 1
    for i in range(4):
        even_rows = value[2 * i * ROWS8 : (2 * i + 1) * ROWS8]
        odd_rows = value[(2 * i + 1) * ROWS8 : (2 * i + 2) * ROWS8]
        slot = i ^ (me // 2)
        rows = slice(unit * ROWS8, (unit + 1) * ROWS8) if isinstance(unit, int) else unit
        keep[slot, rows, :] = jnp.where(odd, odd_rows, even_rows)
        send[slot, rows, :] = jnp.where(odd, even_rows, odd_rows)


def attn_fwd_kernel(has_bias, nparts, *refs):
    refs = list(refs)
    me_ref, src, gain = refs[:3]
    refs = refs[3:]
    ksrc = None
    if not has_bias:
        ksrc = refs.pop(0)
    segr, segc = refs[:2]
    refs = refs[2:]
    if has_bias:
        bias, far = refs[:2]
        refs = refs[2:]
    parts = refs[:nparts]
    refs = refs[nparts:]
    z, zlow, q_o, k_o, v_o, o_o, p_o, w_s, q_s, k_s, v_s, o_s, p_s, w_sem, out_sem = refs
    me = me_ref[0]

    loads = [attn_loads(me, parts, w_s, (u,), w_sem.at[u]) for u in range(4)]
    for load in loads:
        start_all(load)
    a = rms(src[...].astype(f32), gain[...]).astype(bf16)
    b = a if ksrc is None else ksrc[...]
    outs = []
    for value, weight, out, scr in ((a, 0, q_o, q_s), (b, 1, k_o, k_s), (b, 2, v_o, v_s)):
        wait_all(loads[weight])
        full = dot(value, matrix(w_s, weight)).astype(bf16)
        for p in range(PAIRS):
            scr[p] = full[:, p * TILE : (p + 1) * TILE]
        outs.append(pltpu.make_async_copy(scr, out, out_sem.at[weight]))
        outs[-1].start()

    def prob_copy(p):
        return pltpu.make_async_copy(p_s.at[pl.ds(2 * p, 2)], p_o.at[pl.ds(2 * p, 2)], out_sem.at[4])

    def pair(p, carry):
        qp, kp, vp = q_s[p], k_s[p], v_s[p]
        total = [None] * BLOCKS
        for which in range(2):
            h = 2 * p + which
            kz, vz = half_lanes(kp, which), half_lanes(vp, which)
            for bi in range(BLOCKS):
                rows = slice(bi * TILE, (bi + 1) * TILE)
                s = dot_nt(qp[rows], kz)
                if has_bias:
                    tiles = []
                    for bj in range(BLOCKS):
                        step = bi - bj
                        part = s[:, bj * TILE : (bj + 1) * TILE]
                        if abs(step) < 2:
                            part = part + bias[h, tile_of(step)]
                        else:
                            part = part + far[h, 0 if step > 0 else 1]
                        tiles.append(part)
                    s = jnp.concatenate(tiles, axis=1)
                s = jnp.where(segc[rows] == segr[...], s, MASKED)
                e = jnp.exp(s - jnp.max(s, axis=-1, keepdims=True))
                prob = (e * (1.0 / jnp.sum(e, axis=-1, keepdims=True))).astype(bf16)
                p_s[h, rows, :] = prob
                o = dot(prob, vz)
                total[bi] = o if total[bi] is None else total[bi] + o
        o_s[p] = jnp.concatenate(total, axis=0).astype(bf16)
        prob_copy(p).start()
        return carry

    lax.fori_loop(0, PAIRS, pair, 0)
    outs.append(pltpu.make_async_copy(o_s, o_o, out_sem.at[3]))
    outs[-1].start()
    mixed = jnp.concatenate([o_s[p] for p in range(PAIRS)], axis=1)
    wait_all(loads[3])
    result = src[...].astype(f32) + dot(mixed, matrix(w_s, 3))
    z[...] = result
    zlow[...] = result.astype(bf16)
    wait_all(outs)
    for p in range(PAIRS):
        prob_copy(p).wait()


VM = pl.BlockSpec(memory_space=pltpu.VMEM)
SM = pl.BlockSpec(memory_space=pltpu.SMEM)
HBM = pl.BlockSpec(memory_space=pl.ANY)
HEAD_ROWS = jax.ShapeDtypeStruct((PAIRS, LEN, TILE), bf16)
LOW_ROWS = jax.ShapeDtypeStruct((LEN, D), bf16)
FULL_ROWS = jax.ShapeDtypeStruct((LEN, D), f32)
ONE_ROW = jax.ShapeDtypeStruct((1, D), f32)
PARAMS = pltpu.CompilerParams(vmem_limit_bytes=VMEM_LIMIT)


def attn_fwd(me, src, gain, parts, segr, segc, ksrc=None, bias=None, far=None):
    has_bias = bias is not None
    args = [me, src, gain] + ([] if has_bias else [ksrc]) + [segr, segc]
    specs = [SM] + [VM] * (len(args) - 1)
    if has_bias:
        args += [bias, far]
        specs += [VM, SM]
    args += parts
    specs += [HBM] * len(parts)
    return pl.pallas_call(
        only(
            None if has_bias else 0,
            functools.partial(attn_fwd_kernel, has_bias, len(parts)),
        ),
        out_shape=(FULL_ROWS, LOW_ROWS)
        + (HEAD_ROWS,) * 4
        + (jax.ShapeDtypeStruct((HEADS, LEN, LEN), bf16),),
        in_specs=specs,
        out_specs=(VM,) * 2 + (HBM,) * 5,
        scratch_shapes=[pltpu.VMEM((4, 8, ROWS8, D), bf16)]
        + [pltpu.VMEM((PAIRS, LEN, TILE), bf16)] * 4
        + [pltpu.VMEM((HEADS, LEN, LEN), bf16)]
        + [pltpu.SemaphoreType.DMA((4,)), pltpu.SemaphoreType.DMA((5,))],
        compiler_params=PARAMS,
        name="self_fwd" if has_bias else "cross_fwd",
    )(*args)


def attn_bwd_kernel(has_bias, nparts, *refs):
    refs = list(refs)
    me_ref, gres, src, gain = refs[:4]
    refs = refs[4:]
    gother = ksrc = None
    if has_bias:
        gother, gains, hot = refs[:3]
        refs = refs[3:]
    else:
        ksrc = refs.pop(0)
    q_i, k_i, v_i, o_i, p_i = refs[:5]
    refs = refs[5:]
    parts = refs[:nparts]
    refs = refs[nparts:]
    din, keep, send = refs[:3]
    refs = refs[3:]
    if has_bias:
        vec_s = refs.pop()
    else:
        dgain, dkey = refs[:2]
        refs = refs[2:]
    w_s, p_s, do_s, dq_s, dk_s, dv_s, ds_s, keep_s, send_s, w_sem, p_sem, out_sem = refs
    me = me_ref[0]

    out_load = attn_loads(me, parts, w_s, (3,), w_sem.at[0])
    rest_load = attn_loads(me, parts, w_s, (0, 1, 2), w_sem.at[1])

    def prob_copy(p):
        return pltpu.make_async_copy(p_i.at[pl.ds(2 * p, 2)], p_s.at[pl.ds(2 * p, 2)], p_sem.at[p])

    start_all(out_load)
    for p in range(PAIRS):
        prob_copy(p).start()
    start_all(rest_load)
    base = gres[...].astype(f32)
    if has_bias:
        base = jnp.where(me_ref[1] == 1, gother[...].astype(f32), base)
    g = base.astype(bf16)
    wait_all(out_load)
    do = dot_nt(g, matrix(w_s, 3)).astype(bf16)
    for p in range(PAIRS):
        do_s[p] = do[:, p * TILE : (p + 1) * TILE]

    if has_bias:
        down = lax.broadcasted_iota(jnp.int32, (TILE, TILE), 0)
        along = lax.broadcasted_iota(jnp.int32, (TILE, TILE), 1)
        mirror = (down + along == TILE - 1).astype(bf16)

    def pair(p, carry):
        qp, kp, vp, dop = q_i[p], k_i[p], v_i[p], do_s[p]
        q_t, do_t = qp.T, dop.T
        total = [None] * BLOCKS
        prob_copy(p).wait()
        for which in range(2):
            h = 2 * p + which
            kz, vz = half_lanes(kp, which), half_lanes(vp, which)
            diag = {0: None, 1: None, -1: None, 2: None, -2: None}
            for bi in range(BLOCKS):
                rows = slice(bi * TILE, (bi + 1) * TILE)
                dp = dot_nt(dop[rows], vz)
                prob = p_s[h, rows, :].astype(f32)
                t = prob * dp
                ds = t - prob * jnp.sum(t, axis=-1, keepdims=True)
                if has_bias:
                    for bj in range(BLOCKS):
                        step = max(-2, min(2, bi - bj))
                        part = ds[:, bj * TILE : (bj + 1) * TILE]
                        diag[step] = part if diag[step] is None else diag[step] + part
                low = ds.astype(bf16)
                ds_s[which, rows, :] = low
                dq = dot(low, kz)
                total[bi] = dq if total[bi] is None else total[bi] + dq
            if has_bias:
                near = jnp.concatenate([diag[step] for step in (0, 1, -1)], axis=1)
                near = dot(mirror, near.astype(bf16))
                nothing = jnp.zeros((TILE, TILE), f32)
                for t in range(3):
                    part = near[:, t * TILE : (t + 1) * TILE]
                    part = pltpu.roll(
                        jnp.concatenate([part, nothing], axis=1), 0, 1, stride=1, stride_axis=0
                    )
                    vec_s[h, :, 2 * t * TILE : 2 * (t + 1) * TILE] = jnp.sum(
                        part, axis=0, keepdims=True
                    )
                for n, step in ((6, 2), (7, -2)):
                    vec_s[h, :, n * TILE : (n + 1) * TILE] = jnp.sum(
                        diag[step], axis=0, keepdims=True
                    )
            half = slice(which * HEAD, (which + 1) * HEAD)
            dk_s[p, half, :] = dot(q_t[half], ds_s[which]).astype(bf16)
            dv_s[p, half, :] = dot(do_t[half], p_s[h]).astype(bf16)
        dq_s[p] = jnp.concatenate(total, axis=0).astype(bf16)
        return carry

    lax.fori_loop(0, PAIRS, pair, 0)
    v = src[...].astype(f32)
    a = rms(v, gain[...]).astype(bf16)
    a_t = a.T
    b_t = a_t if ksrc is None else ksrc[...].T
    dq = jnp.concatenate([dq_s[p] for p in range(PAIRS)], axis=1)
    dk_t = dk_s[...].reshape(D, LEN)
    dv_t = dv_s[...].reshape(D, LEN)
    wait_all(rest_load)
    query_side = dot_nt(dq, matrix(w_s, 0))
    key_side = dot_nt(dk_t.T, matrix(w_s, 1)) + dot_nt(dv_t.T, matrix(w_s, 2))
    if has_bias:
        query_side = query_side + key_side
    else:
        dkey[...] = key_side.astype(bf16)
    dv, dg = rms_back(v, gain[...], query_side)
    din[...] = (base + dv).astype(din.dtype)
    if has_bias:
        table = dot(vec_s[...].reshape(HEADS, 8 * TILE).astype(bf16), hot[...])
        table = jnp.concatenate([table, jnp.zeros((HEADS, D - TILE), f32)], axis=1)
        rows = jnp.concatenate([table, dg, gains[...], jnp.zeros((1, D), f32)], axis=0)
        for slot in range(4):
            keep_s[slot, D // 2 :, :] = rows.astype(bf16)
            send_s[slot, D // 2 :, :] = rows.astype(bf16)
    else:
        dgain[...] = dg
    put_blocks(me, dot(a_t, dq), 0, keep_s, send_s)
    put_blocks(me, dot_nt(b_t, dk_t), 1, keep_s, send_s)
    put_blocks(me, dot_nt(b_t, dv_t), 2, keep_s, send_s)
    mixed = jnp.concatenate([o_i[p] for p in range(PAIRS)], axis=1)
    put_blocks(me, dot(mixed.T, g), 3, keep_s, send_s)
    outs = [
        pltpu.make_async_copy(send_s, send, out_sem.at[0]),
        pltpu.make_async_copy(keep_s, keep, out_sem.at[1]),
    ]
    start_all(outs)
    wait_all(outs)


BLOCKS8 = jax.ShapeDtypeStruct((4, D, D), bf16)


def attn_bwd(me, gres, src, gain, parts, saved, ksrc=None, others=()):
    has_bias = ksrc is None
    args = [me, gres, src, gain] + (list(others) if has_bias else [ksrc]) + [*saved, *parts]
    specs = [SM] + [VM] * (len(args) - 2 - len(parts)) + [HBM] * (1 + len(parts))
    rows = D // 2 + (EXTRA if has_bias else 0)
    pack = jax.ShapeDtypeStruct((4, rows, D), bf16)
    outs = [LOW_ROWS, pack, pack] if has_bias else [FULL_ROWS, pack, pack, ONE_ROW, LOW_ROWS]
    return pl.pallas_call(
        only(
            None if has_bias else 0,
            functools.partial(attn_bwd_kernel, has_bias, len(parts)),
        ),
        out_shape=tuple(outs),
        in_specs=specs,
        out_specs=tuple([VM, HBM, HBM] + [VM] * (len(outs) - 3)),
        scratch_shapes=[
            pltpu.VMEM((4, 8, ROWS8, D), bf16),
            pltpu.VMEM((HEADS, LEN, LEN), bf16),
            pltpu.VMEM((PAIRS, LEN, TILE), bf16),
            pltpu.VMEM((PAIRS, LEN, TILE), bf16),
            pltpu.VMEM((PAIRS, TILE, LEN), bf16),
            pltpu.VMEM((PAIRS, TILE, LEN), bf16),
            pltpu.VMEM((2, LEN, LEN), bf16),
            pltpu.VMEM((4, rows, D), bf16),
            pltpu.VMEM((4, rows, D), bf16),
            pltpu.SemaphoreType.DMA((2,)),
            pltpu.SemaphoreType.DMA((PAIRS,)),
            pltpu.SemaphoreType.DMA((2,)),
        ]
        + ([pltpu.VMEM((HEADS, 1, 8 * TILE), f32)] if has_bias else []),
        compiler_params=PARAMS,
        name="self_bwd" if has_bias else "cross_bwd",
    )(*args)


GELU_C = float(np.sqrt(2.0 / np.pi))


def gelu_parts(u):
    square = u * u
    t = jnp.tanh(GELU_C * (u + 0.044715 * (u * square)))
    half = 0.5 + 0.5 * t
    slope = half + (half * (1.0 - t)) * (u * (GELU_C + (3 * 0.044715 * GELU_C) * square))
    return u * half, slope


def ffn_kernel(mode, nparts, *refs):
    fwd, bwd = mode != "bwd", mode != "fwd"
    refs = list(refs)
    me_ref, x, gain = refs[:3]
    refs = refs[3:]
    g = refs.pop(0) if bwd else None
    if mode == "bwd":
        h_i, slope_i = refs[:2]
        refs = refs[2:]
    parts = refs[:nparts]
    refs = refs[nparts:]
    out = refs.pop(0) if fwd else None
    if mode == "fwd":
        h_o, slope_o = refs[:2]
        refs = refs[2:]
    if bwd:
        dx, dgain, keep, send = refs[:4]
        refs = refs[4:]
    wi_s, wo_s, w_sem = refs[:3]
    refs = refs[3:]
    if fwd:
        n_s, acc = refs[:2]
        refs = refs[2:]
    if bwd:
        nt_s, dn, keep_s, send_s, out_sem = refs
    me = me_ref[0]
    step = pl.program_id(0)
    plan = part_plan(nparts, 8)

    def in_loads(unit):
        copies = []
        for part, (flip, first, count) in zip(parts, plan):
            if first == 0:
                to = wi_s.at[unit] if flip is None else wi_s.at[unit, me ^ flip]
                copies.append(pltpu.make_async_copy(part.at[unit], to, w_sem.at[unit]))
        return copies

    def out_loads():
        copies = []
        for part, (flip, first, count) in zip(parts, plan):
            if first + count == 8:
                if flip is None:
                    for k in range(4):
                        copies.append(
                            pltpu.make_async_copy(part.at[4 + k], wo_s.at[:, k], w_sem.at[4])
                        )
                else:
                    copies.append(
                        pltpu.make_async_copy(
                            part.at[pl.ds(4 - first, 4)], wo_s.at[me ^ flip], w_sem.at[4]
                        )
                    )
        return copies

    @pl.when(step == 0)
    def _():
        start_all(in_loads(0))
        start_all(out_loads())
        for unit in range(1, 4):
            start_all(in_loads(unit))
        v = x[...].astype(f32)
        n = rms(v, gain[...]).astype(bf16)
        if fwd:
            n_s[...] = n
            acc[...] = v
        if bwd:
            nt_s[...] = n.T
            dn[...] = jnp.zeros_like(dn)

    for unit in range(4):

        @pl.when(step == unit)
        def _():
            wait_all(in_loads(unit))

    wi = wi_s[step].reshape(D, D)

    @pl.when(step == 0)
    def _():
        wait_all(out_loads())

    wo = wo_s[pl.ds(2 * step, 2)].reshape(D, D)
    hs, dus = [], []
    for i in range(PIECES):
        rows = slice(i * LEN // PIECES, (i + 1) * LEN // PIECES)
        if fwd:
            h, slope = gelu_parts(dot(n_s[rows, :], wi))
            h = h.astype(bf16)
            if mode == "fwd":
                h_o[0, rows, :] = h
                slope_o[0, rows, :] = slope.astype(bf16)
            acc[rows, :] += dot(h, wo)
        else:
            h, slope = h_i[0, rows, :], slope_i[0, rows, :].astype(f32)
        if bwd:
            du = (slope * dot_nt(g[rows, :], wo)).astype(bf16)
            dn[rows, :] += dot_nt(du, wi)
            hs.append(h)
            dus.append(du)
    if bwd:
        h, du = jnp.concatenate(hs), jnp.concatenate(dus)
        in_rows = pl.ds(pl.multiple_of(step * ROWS8, 32), ROWS8)
        put_blocks(me, dot(nt_s[...], du), in_rows, keep_s, send_s)
        dwo = dot(h.T, g[...]).astype(bf16)
        odd = (me % 2) == 1
        slot = step ^ (me // 2)
        for k in range(4):
            first, second = dwo[k * ROWS8 : (k + 1) * ROWS8], dwo[(4 + k) * ROWS8 : (5 + k) * ROWS8]
            rows = slice((4 + k) * ROWS8, (5 + k) * ROWS8)
            keep_s[slot, rows, :] = jnp.where(odd, second, first)
            send_s[slot, rows, :] = jnp.where(odd, first, second)

        def outs(c):
            slot = c ^ (me // 2)
            copies = []
            for n, (here, there) in enumerate(((send_s, send), (keep_s, keep))):
                part = pl.ds(pl.multiple_of(c * ROWS8, 32), ROWS8)
                copies.append(
                    pltpu.make_async_copy(here.at[:, part], there.at[:, part], out_sem.at[2 * n])
                )
                last = pl.ds(D // 2, D // 2)
                copies.append(
                    pltpu.make_async_copy(here.at[slot, last], there.at[slot, last], out_sem.at[2 * n + 1])
                )
            return copies

        start_all(outs(step))

    @pl.when(step == pl.num_programs(0) - 1)
    def _():
        if fwd:
            out[...] = acc[...].astype(bf16)
        if bwd:
            dv, dg = rms_back(x[...].astype(f32), gain[...], dn[...])
            dgain[...] = dg
            dx[...] = (g[...].astype(f32) + dv).astype(bf16)
            for c in range(4):
                wait_all(outs(c))


def ffn(mode, me, x, gain, parts, g=None, saved=()):
    fwd, bwd = mode != "bwd", mode != "fwd"
    whole = pl.BlockSpec((LEN, D), lambda c: (0, 0))
    one = pl.BlockSpec((1, D), lambda c: (0, 0))
    hidden = pl.BlockSpec((1, LEN, D), lambda c: (c, 0, 0))
    hidden_shape = jax.ShapeDtypeStruct((4, LEN, D), bf16)
    args, specs = [me, x, gain], [SM, whole, one]
    if bwd:
        args, specs = args + [g], specs + [whole]
    args += list(saved)
    specs += [hidden] * len(saved)
    args += parts
    specs += [HBM] * len(parts)
    shapes, out_specs = [], []
    scratch = [
        pltpu.VMEM((4, 8, ROWS8, D), bf16),
        pltpu.VMEM((8, 4, ROWS8, D), bf16),
        pltpu.SemaphoreType.DMA((5,)),
    ]
    if fwd:
        shapes, out_specs = [LOW_ROWS], [whole]
        scratch += [pltpu.VMEM((LEN, D), bf16), pltpu.VMEM((LEN, D), f32)]
    if mode == "fwd":
        shapes += [hidden_shape] * 2
        out_specs += [hidden] * 2
    if bwd:
        shapes += [LOW_ROWS, ONE_ROW, BLOCKS8, BLOCKS8]
        out_specs += [whole, one, HBM, HBM]
        scratch += [
            pltpu.VMEM((D, LEN), bf16),
            pltpu.VMEM((LEN, D), f32),
            pltpu.VMEM((4, D, D), bf16),
            pltpu.VMEM((4, D, D), bf16),
            pltpu.SemaphoreType.DMA((4,)),
        ]
    return pl.pallas_call(
        only(0 if mode == "both" else 1, functools.partial(ffn_kernel, mode, len(parts))),
        grid=(4,),
        out_shape=tuple(shapes),
        in_specs=specs,
        out_specs=tuple(out_specs),
        scratch_shapes=scratch,
        compiler_params=PARAMS,
        name="ffn_" + mode,
    )(*args)


def wide_add(*values):
    total = values[0].astype(f32)
    for value in values[1:]:
        total = total + value.astype(f32)
    return total.astype(bf16)


def diag_kernel(me_ref, keep, recv, by_x, by_y, keep_s, recv_s, sem):
    half = by_x.shape[0]
    loads = [
        pltpu.make_async_copy(keep.at[3], keep_s, sem.at[0]),
        pltpu.make_async_copy(recv.at[3], recv_s, sem.at[1]),
    ]
    start_all(loads)
    wait_all(loads)
    keep_s[...] = wide_add(keep_s[...], recv_s[...])
    stores = [
        pltpu.make_async_copy(keep_s.at[:half], by_x, sem.at[0]),
        pltpu.make_async_copy(keep_s.at[half:], by_y, sem.at[1]),
    ]
    start_all(stores)
    wait_all(stores)


def diag_add(role, me, keep, recv):
    _, r, c = keep.shape
    half = r // 32 * 16
    return pl.pallas_call(
        only(role, diag_kernel),
        out_shape=tuple(jax.ShapeDtypeStruct((n, c), bf16) for n in (half, r - half)),
        in_specs=[SM, HBM, HBM],
        out_specs=(HBM, HBM),
        scratch_shapes=[pltpu.VMEM((r, c), bf16)] * 2 + [pltpu.SemaphoreType.DMA((2,))],
        compiler_params=PARAMS,
        name="diag_add",
    )(me, keep, recv)


def rest_kernel(
    me_ref, keep, recv, from_x, from_y, own, for_x, for_y, keep_s, recv_s, x_s, y_s, sem
):
    half = from_x.shape[0]
    loads = []
    for slot in range(3):
        loads.append(pltpu.make_async_copy(keep.at[slot], keep_s.at[slot], sem.at[2 * slot]))
        loads.append(pltpu.make_async_copy(recv.at[slot], recv_s.at[slot], sem.at[2 * slot + 1]))
    loads.append(pltpu.make_async_copy(from_x, x_s, sem.at[6]))
    loads.append(pltpu.make_async_copy(from_y, y_s, sem.at[7]))
    start_all(loads[2:4] + loads[6:] + loads[4:6] + loads[:2])
    stores = []
    for slot, out in ((1, for_x), (2, for_y), (0, own)):
        wait_all(loads[2 * slot : 2 * slot + 2])
        if slot == 1:
            wait_all(loads[6:])
            top, low = (), (y_s[...],)
        else:
            top, low = ((x_s[...],), ()) if slot == 2 else ((), ())
        keep_s[slot, :half] = wide_add(keep_s[slot, :half], recv_s[slot, :half], *top)
        keep_s[slot, half:] = wide_add(keep_s[slot, half:], recv_s[slot, half:], *low)
        stores.append(pltpu.make_async_copy(keep_s.at[slot], out, sem.at[8 + slot]))
        stores[-1].start()
    wait_all(stores)


def rest_add(role, me, keep, recv, from_x, from_y):
    _, r, c = keep.shape
    half = r // 32 * 16
    shape = jax.ShapeDtypeStruct((r, c), bf16)
    return pl.pallas_call(
        only(role, rest_kernel),
        out_shape=(shape,) * 3,
        in_specs=[SM] + [HBM] * 4,
        out_specs=(HBM,) * 3,
        scratch_shapes=[pltpu.VMEM((3, r, c), bf16)] * 2
        + [pltpu.VMEM((half, c), bf16), pltpu.VMEM((r - half, c), bf16)]
        + [pltpu.SemaphoreType.DMA((11,))],
        compiler_params=PARAMS,
        name="rest_add",
    )(me, keep, recv, from_x, from_y)


ALL = (0, 1, 2, 3)
ENC = (1, 2)
DEC = (0, 3)


def across(x, flip, planes):
    wide, narrow = lax.axis_size("wide"), lax.axis_size("narrow")
    pairs = [(i * narrow + n, (i ^ flip) * narrow + n) for i in range(wide) for n in planes]
    return lax.ppermute(x, ("wide", "narrow"), pairs)


def between(x, pairs):
    return lax.ppermute(x, "narrow", pairs)


def in_units(local):
    return jnp.transpose(local.reshape(local.shape[0], 4, D), (1, 0, 2))


def out_units(local):
    return local.reshape(4, local.shape[0] // 4, D)


def tie(*values):
    return lax.optimization_barrier(values)


def whole_pack(shard):
    k = shard.shape[0]
    full = lax.all_gather(shard, "wide", axis=1)
    if k == 8:
        inner = full[:4].reshape(4, 8, ROWS8, D)
        outer = jnp.transpose(full[4:], (1, 0, 2, 3)).reshape(8, 4, ROWS8, D)
        return [jnp.concatenate([inner, jnp.transpose(outer, (1, 0, 2, 3))])]
    return [full.reshape(k, 8, ROWS8, D)]


def gather_near(shard, planes=ALL):
    return across(shard, 2, planes), across(shard, 4, planes), across(shard, 1, planes)


def gather_far(shard, near, planes=ALL):
    px, py, pc = near
    k = shard.shape[0]
    first = across(px[: k // 2], 4, planes)
    second = across(py[k // 2 :], 2, planes)
    parts = [px, py, first, second]
    return [shard] + parts + [pc] + [across(part, 1, planes) for part in parts]


def whole_scatter(keep, send):
    blocks = jnp.stack([keep, send], axis=1).reshape(8, -1, D)
    k = blocks.shape[1] // ROWS8
    weights = blocks[:, : k * ROWS8].reshape(8, k, ROWS8, D)
    inner = jnp.transpose(weights[:, :4], (1, 0, 2, 3)).reshape(4, D, D)
    inner = lax.psum_scatter(inner, "wide", scatter_dimension=1, tiled=True).reshape(-1, D)
    if k == 8:
        last = weights[:, 4:].reshape(FF, D)
        last = lax.psum_scatter(last, "wide", scatter_dimension=0, tiled=True)
    else:
        last = lax.psum(blocks[0, k * ROWS8 :], "wide")
    return jnp.concatenate([inner, last])


class Scatter:
    def __init__(self, me, keep, send, planes):
        self.me, self.keep, self.planes = me, keep, planes
        self.role = {ENC: 1, DEC: 0, ALL: None}[planes]
        self.small = lax.axis_size("wide") == 8
        self.state = (send,)
        if self.small:
            self.state = (across(send, 1, planes),)
        self.phase, self.token = 0, keep

    def go(self):
        if not self.small:
            return self
        if self.phase == 0:
            (self.recv,) = self.state
            by_x, by_y = diag_add(self.role, self.me, self.keep, self.recv)
            self.token = by_x
            self.state = across(by_x, 2, self.planes), across(by_y, 4, self.planes)
        elif self.phase == 1:
            own, for_x, for_y = rest_add(self.role, self.me, self.keep, self.recv, *self.state)
            self.token = own
            self.state = own, across(for_x, 2, self.planes), across(for_y, 4, self.planes)
        self.phase += 1
        return self

    def result(self):
        if not self.small:
            return whole_scatter(self.keep, self.state[0])
        return wide_add(*self.state)

    def halves(self):
        if not self.small:
            return jnp.split(self.result(), 2)
        half = self.state[0].shape[0] // 2
        return wide_add(*[v[:half] for v in self.state]), wide_add(*[v[half:] for v in self.state])


def tie_all(scatters, *values):
    counts = [len(s.state) for s in scatters]
    flat = tie(*[v for s in scatters for v in s.state], *values)
    for s, count in zip(scatters, counts):
        s.state, flat = flat[:count], flat[count:]
    return flat


class FromMiddle:
    def __init__(self, share, middle):
        self.share, self.middle = share, middle
        self.state = (between(share, [(1, 2), (2, 1)]),)

    def go(self):
        self.total = wide_add(self.share, *self.state)
        self.state = (between(self.total, [(1, 0), (2, 3)]),)
        return self

    def result(self):
        return jnp.where(self.middle, self.total, *self.state).astype(f32)


class FromEnds:
    def __init__(self, share, middle):
        self.share, self.middle = share, middle
        self.got, self.state = [], (between(share, [(0, 1), (3, 2)]),)

    def go(self):
        self.got.append(self.state[0])
        pairs = [(1, 2), (2, 1)] if len(self.got) == 1 else [(1, 0), (2, 3)]
        self.state = (between(self.state[0], pairs),)
        return self

    def result(self):
        near, far = self.got
        first = jnp.where(self.middle, near, self.share).astype(f32)
        return first + jnp.where(self.middle, far, *self.state).astype(f32)


def on_device(
    enc_in,
    dec_in,
    dec_cot,
    segments,
    enc_attn_gain,
    enc_query,
    enc_key,
    enc_value,
    enc_output,
    enc_table,
    enc_ffn_gain,
    enc_ffn_in,
    enc_ffn_out,
    dec_self_gain,
    dec_query,
    dec_key,
    dec_value,
    dec_output,
    dec_table,
    dec_cross_gain,
    cross_query,
    cross_key,
    cross_value,
    cross_output,
    dec_ffn_gain,
    dec_ffn_in,
    dec_ffn_out,
):
    plane = lax.axis_index("narrow")
    is_enc = (plane == 1) | (plane == 2)
    row = plane // 2

    def own(x):
        return lax.dynamic_slice_in_dim(x, row * LEN, LEN, 0)

    def pick(enc, dec):
        return jnp.where(is_enc, enc, dec)

    def gain_of(g):
        return g.astype(f32).reshape(1, D)

    seg = lax.dynamic_slice_in_dim(segments, row, 1, 0)
    segr, segc = seg, seg.reshape(LEN, 1)
    src = pick(own(enc_in), own(dec_in))
    cot = own(dec_cot)

    me = lax.axis_index("wide") if lax.axis_size("wide") == 8 else 0
    me = jnp.stack([jnp.asarray(me, jnp.int32), is_enc.astype(jnp.int32)])

    pack_a = jnp.stack(
        [
            pick(enc_query, dec_query),
            pick(enc_key, dec_key),
            pick(enc_value, dec_value),
            pick(enc_output, dec_output),
        ]
    )
    pack_f = jnp.concatenate(
        [in_units(pick(enc_ffn_in, dec_ffn_in)), out_units(pick(enc_ffn_out, dec_ffn_out))]
    )
    pack_c = jnp.stack([cross_query, cross_key, cross_value, cross_output])
    shard_rows = enc_query.shape[0]
    small = lax.axis_size("wide") == 8
    if small:
        near_a = gather_near(pack_a)

    enc_ids, enc_far = tile_ids(True)
    dec_ids, dec_far = tile_ids(False)
    ids = pick(jnp.asarray(enc_ids), jnp.asarray(dec_ids))
    far_ids = pick(jnp.asarray(enc_far), jnp.asarray(dec_far))
    buckets = jnp.arange(BUCKETS + 1, dtype=jnp.int32)
    hot = (ids[None] == buckets[:, None, None, None]).astype(bf16)
    far_hot = (far_ids[None] == buckets[:, None]).astype(bf16)
    table = jnp.concatenate([pick(enc_table, dec_table), jnp.full((1, HEADS), MASKED, bf16)])
    bias = jnp.einsum("bh,bsij->hsij", table, hot, preferred_element_type=f32)
    far = jnp.einsum("bh,bs->hs", table, far_hot, preferred_element_type=f32)
    enc_sums, dec_sums = sum_ids(True), sum_ids(False)
    sums_of = pick(jnp.asarray(enc_sums), jnp.asarray(dec_sums))
    sum_hot = (sums_of[:, None] == jnp.arange(TILE, dtype=jnp.int32)).astype(bf16)

    gain_a = pick(gain_of(enc_attn_gain), gain_of(dec_self_gain))
    enc_gain = gain_of(enc_ffn_gain)
    gain_c = gain_of(dec_cross_gain)
    if small:
        *near_a, pack_f, bias, far, src, cot, segc, me = tie(
            *near_a, pack_f, bias, far, src, cot, segc, me
        )
        w_attn = gather_far(pack_a, near_a)
        near_f = gather_near(pack_f)
    else:
        w_attn, w_ffn, w_cross = whole_pack(pack_a), whole_pack(pack_f), whole_pack(pack_c)
    z1, x1, *saved = attn_fwd(me, src, gain_a, w_attn, segr, segc, bias=bias, far=far)
    if small:
        z1, x1, *near_f, pack_c = tie(z1, x1, *near_f, pack_c)
        w_ffn = gather_far(pack_f, near_f)
        near_c = gather_near(pack_c, DEC)
    enc_out, *saved_f = ffn("fwd", me, x1, enc_gain, w_ffn)
    if small:
        enc_out, *near_c = tie(enc_out, *near_c)
    memory = between(enc_out, [(1, 0), (2, 3)])
    if small:
        w_cross = gather_far(pack_c, near_c, DEC)
    _, z2, *saved_c = attn_fwd(me, z1, gain_c, w_cross, segr, segc, ksrc=memory)

    def by_columns(x):
        return lax.all_to_all(x, "narrow", split_axis=1, concat_axis=0, tiled=True)

    def rows_by_block(parts):
        rows = [parts[n * LEN : (n + 1) * LEN] for n in range(4)]
        return jnp.concatenate([rows[1], rows[2]]), jnp.concatenate([rows[0], rows[3]])

    dec_out, gz2, dgain_df, *blocks = ffn("both", me, z2, gain_of(dec_ffn_gain), w_ffn, cot)
    sum_df = Scatter(me, *blocks, DEC)
    gz1, *blocks_c, dgain_c, genc_out = attn_bwd(
        me, gz2, z1, gain_c, w_cross, saved_c, ksrc=memory
    )
    genc = between(genc_out, [(0, 1), (3, 2)])
    sum_c = Scatter(me, *blocks_c, DEC)
    out_rows = pick(enc_out, dec_out)
    (out_rows,) = tie_all([sum_df, sum_c], out_rows)
    sum_df.go()
    genc, out_rows, _ = tie(genc, out_rows, sum_df.token)
    gx1, dgain_ef, *blocks = ffn("bwd", me, x1, enc_gain, w_ffn, genc, saved_f)
    gx1, out_rows, *blocks = tie_all([sum_df], gx1, out_rows, *blocks)
    sum_ef = Scatter(me, *blocks, ENC)
    sum_df.go()
    out_rows, _ = tie_all([sum_c], out_rows, sum_df.token)
    out_cols = by_columns(out_rows)
    sum_c.go()
    gains = jnp.concatenate([pick(dgain_ef, dgain_df), dgain_c])
    din, *blocks = attn_bwd(
        me, gz1, src, gain_a, w_attn, saved, others=(gx1, gains, sum_hot)
    )
    din, out_cols, *blocks = tie_all([sum_ef, sum_c, sum_df], din, out_cols, *blocks)
    sum_a = Scatter(me, *blocks, ALL)
    sum_ef.go()
    tie_all([sum_df, sum_c], sum_ef.token)
    first, last = sum_df.halves()
    all_d1 = FromEnds(first, is_enc)
    last = tie(last, first)[0]
    all_d2 = FromEnds(last, is_enc)
    tie_all([sum_c], last)
    sum_c.go()
    tie_all([sum_ef, sum_a], last)
    sum_ef.go()
    tie_all([all_d1], sum_ef.token)
    all_d1.go()
    tie_all([sum_a], sum_ef.token)
    sum_a.go()
    tie_all([all_d2, sum_c], sum_a.token)
    all_d2.go()
    all_c = FromEnds(sum_c.result(), is_enc)
    din, _ = tie(din, sum_a.token)
    grad_cols = by_columns(din)
    tie_all([sum_a, all_d1])
    sum_a.go()
    all_d1.go()
    tie_all([sum_ef, all_c, all_d2], sum_a.token)
    first, last = sum_ef.halves()
    all_f1 = FromMiddle(first, is_enc)
    last = tie(last, first)[0]
    all_f2 = FromMiddle(last, is_enc)
    all_d2.go()
    all_c.go()
    tie_all([sum_a], last)
    s_a = sum_a.result()
    all_e = FromMiddle(s_a, is_enc)
    all_s = FromEnds(s_a, is_enc)
    tie_all([all_f1], s_a)
    all_f1.go()
    tie_all([all_f2], all_f1.total)
    all_f2.go()
    tie_all([all_e, all_s, all_c], all_f2.total)
    all_e.go()
    all_s.go()
    all_c.go()
    tie_all([all_s], all_e.total)
    all_s.go()

    def split(f):
        return f[: 4 * shard_rows].reshape(4, shard_rows, D), f[4 * shard_rows :]

    g_c, g_s, g_e = (split(p.result()) for p in (all_c, all_s, all_e))

    def in_rows(f):
        return jnp.transpose(f.result().reshape(4, shard_rows, D), (1, 0, 2)).reshape(-1, FF)

    gi_e, gi_d = in_rows(all_f1), in_rows(all_d1)
    go_e, go_d = all_f2.result(), all_d2.result()
    more_e, more_s = g_e[1], g_s[1]
    g_e, g_s, g_c = g_e[0], g_s[0], g_c[0]
    tables = [jnp.transpose(m[:HEADS, :BUCKETS]) for m in (more_e, more_s)]
    sums = [more_e[HEADS], more_e[HEADS + 1], more_s[HEADS], more_s[HEADS + 2], more_s[HEADS + 1]]
    enc_cols, dec_cols = rows_by_block(out_cols)
    enc_grad_cols, dec_grad_cols = rows_by_block(grad_cols)
    return (
        enc_cols,
        dec_cols,
        enc_grad_cols,
        dec_grad_cols,
        sums[0],
        g_e[0],
        g_e[1],
        g_e[2],
        g_e[3],
        tables[0],
        sums[1],
        gi_e,
        go_e,
        sums[2],
        g_s[0],
        g_s[1],
        g_s[2],
        g_s[3],
        tables[1],
        sums[3],
        g_c[0],
        g_c[1],
        g_c[2],
        g_c[3],
        sums[4],
        gi_d,
        go_d,
    )


def solution(mesh):
    rows, copied = P("wide", None), P()
    block = P("wide", "narrow")
    gains = (copied,)
    attention = (rows,) * 4
    placed = (
        (rows,) * 4
        + gains
        + attention
        + (copied,)
        + gains
        + (rows,) * 2
        + gains
        + attention
        + (copied,)
        + gains
        + attention
        + gains
        + (rows,) * 2
    )
    return jax.shard_map(
        on_device,
        mesh=mesh,
        in_specs=placed,
        out_specs=(block,) * 4 + placed[4:],
        check_vma=False,
    )
```
